32 devices in a mesh: dp: 8 (over z, x), fsdp: 4 (over y, core).
Axes of the slice: x: 2, y: 2, z: 4, core: 2. Of those that a mesh axis runs over, the one named last changes fastest.
Arguments:
- enc_input: bfloat16 [16384, 512], P(('dp', 'fsdp')), may hold values from -6 to 6
- dec_input: bfloat16 [16384, 512], P(('dp', 'fsdp')), may hold values from -6 to 6
- target_mask: int32 [16384], P(('dp', 'fsdp')), may hold values 0 or 1
- src_lengths: int32 [32, 4], P(('dp', 'fsdp')), may hold values from 1 to 256, 512 in all within a row
- tgt_lengths: int32 [32, 4], P(('dp', 'fsdp')), may hold values from 1 to 128, as said below
- memory_route: int32 [32, 4], P(('dp', 'fsdp')), may hold values from 0 to 15, as said below
- enc_qkv: bfloat16 [3, 512, 512], P(None, ('dp', 'fsdp')), may hold values from -0.25 to 0.25
- enc_out: bfloat16 [512, 512], P(('dp', 'fsdp')), may hold values from -1 to 1
- enc_ffn_in: bfloat16 [512, 2048], P(('dp', 'fsdp')), may hold values from -0.25 to 0.25
- enc_ffn_out: bfloat16 [2048, 512], P(('dp', 'fsdp')), may hold values from -0.125 to 0.125
- enc_norms: bfloat16 [2, 2, 512], P(None, None, ('dp', 'fsdp')), may hold values from -0.5 to 1.5
- dec_qkv: bfloat16 [3, 512, 512], P(None, ('dp', 'fsdp')), may hold values from -0.25 to 0.25
- dec_out: bfloat16 [512, 512], P(('dp', 'fsdp')), may hold values from -1 to 1
- cross_qkv: bfloat16 [3, 512, 512], P(None, ('dp', 'fsdp')), may hold values from -0.25 to 0.25
- cross_out: bfloat16 [512, 512], P(('dp', 'fsdp')), may hold values from -1 to 1
- dec_ffn_in: bfloat16 [512, 2048], P(('dp', 'fsdp')), may hold values from -0.25 to 0.25
- dec_ffn_out: bfloat16 [2048, 512], P(('dp', 'fsdp')), may hold values from -0.125 to 0.125
- dec_norms: bfloat16 [3, 2, 512], P(None, None, ('dp', 'fsdp')), may hold values from -0.5 to 1.5
- mask_vector: bfloat16 [512], P(('dp', 'fsdp')), may hold values from -5 to 5
- out_cotangent: bfloat16 [16384, 512], P(('dp', 'fsdp')), may hold values from -6 to 6
Outputs:
- dec_output: bfloat16 [16384, 512], P(('dp', 'fsdp'))
- enc_input_grad: float32 [16384, 512], P(('dp', 'fsdp'))
- dec_input_grad: float32 [16384, 512], P(('dp', 'fsdp'))
- enc_qkv_grad: float32 [3, 512, 512], P(None, ('dp', 'fsdp'))
- enc_out_grad: float32 [512, 512], P(('dp', 'fsdp'))
- enc_ffn_in_grad: float32 [512, 2048], P(('dp', 'fsdp'))
- enc_ffn_out_grad: float32 [2048, 512], P(('dp', 'fsdp'))
- enc_norms_grad: float32 [2, 2, 512], P(None, None, ('dp', 'fsdp'))
- dec_qkv_grad: float32 [3, 512, 512], P(None, ('dp', 'fsdp'))
- dec_out_grad: float32 [512, 512], P(('dp', 'fsdp'))
- cross_qkv_grad: float32 [3, 512, 512], P(None, ('dp', 'fsdp'))
- cross_out_grad: float32 [512, 512], P(('dp', 'fsdp'))
- dec_ffn_in_grad: float32 [512, 2048], P(('dp', 'fsdp'))
- dec_ffn_out_grad: float32 [2048, 512], P(('dp', 'fsdp'))
- dec_norms_grad: float32 [3, 2, 512], P(None, None, ('dp', 'fsdp'))
- mask_vector_grad: float32 [512], P(('dp', 'fsdp'))
The draws below stay inside these ranges and needn't reach their ends.
Inputs may be any that keep to these rules, and one draw needn't show every extreme that they name: `src_lengths`: row r holds device r's source lengths in packing order; each row sums to 512 and has one entry of exactly 256. `tgt_lengths`: row r holds the target lengths of device r's 4 slots; each row has one entry of exactly 128. `memory_route`: entry j of row r = (d, f) sends that device's j-th source sentence to decoder device (d, entry // 4) and slot entry % 4. Within a row the devices named are all 4 devices of fsdp once each, and within one dp index every decoder slot is named exactly once.
All inputs are finite; a program needn't handle non-finite values. No bound on the sum of `target_mask` on one device may be relied on, other than what follows from the above.
Results may differ from the reference program's by a relative error of at most 0.025.
Values may be sent and summed in bfloat16 or wider, within the bound.
No kernel may reach another device: no remote copies, remote signals or barrier semaphores. Data moves between devices by JAX's collectives and lax.ppermute only.
A program may use at most 256 MiB of HBM per device.

```python
import math
import jax
import jax.numpy as jnp
import numpy as np
from jax import lax

D = 512
HEADS = 8
HEAD_DIM = 64
FF = 2048
TOK_DEV = 512
SEQ_DEV = 4
LMAX = 256
TSLOT = 128
TOKENS = 16384
N_DP = 8
N_FSDP = 4


def shuffled(key, count, width):
    score = jax.random.randint(key, (count, width), 0, 1 << 20) * width + jnp.arange(width, dtype=jnp.int32)[None, :]
    return jnp.argsort(score, axis=1).astype(jnp.int32)


def gain_bias_table(key, layers, gain_reach, bias_reach):
    gain_key, bias_key = jax.random.split(key)
    gains = jax.random.uniform(gain_key, (layers, 1, D), jnp.float32, 1.0 - gain_reach, 1.0 + gain_reach)
    biases = jax.random.uniform(bias_key, (layers, 1, D), jnp.float32, -bias_reach, bias_reach)
    return jnp.concatenate([gains, biases], axis=1).astype(jnp.bfloat16)


def draw_enc_norms(key, part):
    key = jax.random.fold_in(key, 5)
    return gain_bias_table(key, 2, 0.4, 0.3)


def draw_dec_norms(key, part):
    key = jax.random.fold_in(key, 7)
    return gain_bias_table(key, 3, 0.4, 0.3)


def draw_tgt_lengths(key, part):
    key = jax.random.fold_in(key, 11)
    base_key, pick_key = jax.random.split(key)
    count = N_DP * N_FSDP
    base = jax.random.randint(base_key, (count, SEQ_DEV), 1, TSLOT + 1)
    chosen = jax.random.randint(pick_key, (count,), 0, SEQ_DEV)
    full_slot = jnp.arange(SEQ_DEV, dtype=jnp.int32)[None, :] == chosen[:, None]
    return jnp.where(full_slot, TSLOT, base).astype(jnp.int32)


def draw_memory_route(key, part):
    key = jax.random.fold_in(key, 23)
    first_key, second_key = jax.random.split(key)
    width = N_FSDP
    spread = shuffled(first_key, N_DP * width, width).reshape(N_DP, width, width)
    target = shuffled(second_key, N_DP * width, width).reshape(N_DP, width, width)
    source = jnp.arange(width, dtype=jnp.int32)[None, :, None]
    dest_dev = (source + spread) % width
    dest_slot = jnp.take_along_axis(target.transpose(0, 2, 1), dest_dev, axis=2)
    return (dest_dev * width + dest_slot).reshape(N_DP * width, width).astype(jnp.int32)


def touch_ends(entries, key, least, largest):
    extent = entries.shape
    place = [jax.random.randint(jax.random.fold_in(key, axis), (), 0, extent[axis]) for axis in range(len(extent))]
    entries = entries.at[tuple(place)].set(least)
    longest = extent.index(max(extent))
    place[longest] = (place[longest] + 1) % extent[longest]
    return entries.at[tuple(place)].set(largest)


def with_spikes(drawn, rng, source, target, shards_of, factor):
    def block_of(axis_at):
        return (jnp.arange(drawn.shape[axis_at]) // (drawn.shape[axis_at] // shards_of)).reshape((-1,) + (1,) * (drawn.ndim - 1 - axis_at))

    one_side = jax.random.permutation(rng, shards_of)[block_of(target)]
    other_side = (block_of(target) + shards_of // 2) % shards_of
    return jnp.where((block_of(source) == one_side) | (block_of(source) == other_side), factor * drawn, drawn)


def block_levels(rng, dims, shards, low, high):
    gain = 1.0
    for axis_at, parts in shards:
        heights = jax.random.uniform(jax.random.fold_in(jax.random.fold_in(rng, 6), axis_at), (parts,), jnp.float32, low / len(shards), high / len(shards))
        gain = gain * jnp.repeat(jnp.exp(heights), dims[axis_at] // parts).reshape((-1,) + (1,) * (len(dims) - 1 - axis_at))
    return gain


def split_up(amount, total, most, skew):
    portions = [(1 << 20) // math.isqrt(standing ** skew) + 1 for standing in range(2, amount + 1)]
    rest, given = total - most - (amount - 1), [1] * (amount - 1)
    while rest > 0:
        free = [i for i in range(amount - 1) if given[i] < most]
        pool, left = sum([portions[i] for i in free]), rest
        for i in free:
            more = min(most - given[i], max(1, left * portions[i] // pool), rest)
            given[i] = given[i] + more
            rest = rest - more
    return np.array([most] + given)


def ragged_sizes(own_key, count, total, most, lean):
    if count == 2:
        one = jax.random.randint(own_key, (), max(1, total - most), min(most, total - 1) + 1)
        return jnp.stack([one, total - one])
    tallies = jnp.asarray(split_up(count, total, most, lean), jnp.int32)
    twos = (count - 1) // 2
    source_of, sink = tallies[1:1 + 2 * twos:2], tallies[2:2 + 2 * twos:2]
    room = jnp.minimum(source_of - 1, most - sink)
    moved = jax.random.randint(jax.random.fold_in(own_key, 1), (twos,), 0, 1 << 20) % (room + 1)
    tallies = tallies.at[1:1 + 2 * twos:2].set(source_of - moved).at[2:2 + 2 * twos:2].set(sink + moved)
    return tallies[jax.random.permutation(jax.random.fold_in(own_key, 2), count)]


def bell_draw(key, shape, scale, bound, shards=(), kind=jnp.bfloat16):
    array = scale * jax.random.normal(key, shape, jnp.float32)
    if shards:
        array = array * block_levels(key, shape, shards, -0.22, 0.18)
    return jnp.clip(array, -bound, bound).astype(kind)


def noise_with(own_key, shape, scale, limit, cuts, heavy, kind=jnp.bfloat16):
    values = scale * jax.random.normal(own_key, shape, jnp.float32)
    if cuts:
        values = values * block_levels(own_key, shape, cuts, -0.22, 0.18)
    return jnp.clip(with_spikes(values, jax.random.fold_in(own_key, 3), *heavy), -limit, limit).astype(kind)


def setup_inputs(seed: int = 0) -> dict:
    seeds = jax.random.split(jax.random.key(seed), 21)
    enc_input = noise_with(seeds[0], (TOKENS, D), 1.0, 6.0, ((0, 32),), (0, 1, 32, 2.75))
    dec_input = noise_with(seeds[1], (TOKENS, D), 1.0, 6.0, ((0, 32),), (0, 1, 32, 2.75))
    target_mask = touch_ends((jax.random.randint(seeds[2], (TOKENS,), 0, 3) < 1).astype(jnp.int32), jax.random.fold_in(seeds[2], 1), 0, 1)
    src_lengths = jax.vmap(lambda own: ragged_sizes(own, SEQ_DEV, TOK_DEV, LMAX, 2))(jax.random.split(seeds[3], (N_DP * N_FSDP))).reshape((N_DP * N_FSDP, SEQ_DEV)).astype(jnp.int32)
    tgt_lengths = draw_tgt_lengths(jax.random.fold_in(seeds[20], 71), 0)
    memory_route = draw_memory_route(jax.random.fold_in(seeds[20], 71), 0)
    enc_qkv = bell_draw(seeds[6], (3, D, D), D ** -0.5, 0.25, ((1, 32),))
    enc_out = bell_draw(seeds[7], (D, D), (D // 16) ** -0.5, 1.0, ((0, 32),))
    enc_ffn_in = bell_draw(seeds[8], (D, FF), D ** -0.5, 0.25, ((0, 32),))
    enc_ffn_out = bell_draw(seeds[9], (FF, D), FF ** -0.5, 0.125, ((0, 32),))
    enc_norms = draw_enc_norms(jax.random.fold_in(seeds[20], 71), 0)
    dec_qkv = bell_draw(seeds[11], (3, D, D), D ** -0.5, 0.25, ((1, 32),))
    dec_out = bell_draw(seeds[12], (D, D), (D // 16) ** -0.5, 1.0, ((0, 32),))
    cross_qkv = bell_draw(seeds[13], (3, D, D), D ** -0.5, 0.25, ((1, 32),))
    cross_out = bell_draw(seeds[14], (D, D), (D // 16) ** -0.5, 1.0, ((0, 32),))
    dec_ffn_in = bell_draw(seeds[15], (D, FF), D ** -0.5, 0.25, ((0, 32),))
    dec_ffn_out = bell_draw(seeds[16], (FF, D), FF ** -0.5, 0.125, ((0, 32),))
    dec_norms = draw_dec_norms(jax.random.fold_in(seeds[20], 71), 0)
    mask_vector = bell_draw(seeds[18], (D,), 1.0, 5.0, ((0, 32),))
    out_cotangent = noise_with(seeds[19], (TOKENS, D), 1.0, 6.0, ((0, 32),), (0, 1, 32, 2.75))
    return dict(enc_input=enc_input, dec_input=dec_input, target_mask=target_mask, src_lengths=src_lengths, tgt_lengths=tgt_lengths, memory_route=memory_route, enc_qkv=enc_qkv, enc_out=enc_out, enc_ffn_in=enc_ffn_in, enc_ffn_out=enc_ffn_out, enc_norms=enc_norms, dec_qkv=dec_qkv, dec_out=dec_out, cross_qkv=cross_qkv, cross_out=cross_out, dec_ffn_in=dec_ffn_in, dec_ffn_out=dec_ffn_out, dec_norms=dec_norms, mask_vector=mask_vector, out_cotangent=out_cotangent)


@jax.custom_vjp
def low(v):
    return lax.optimization_barrier(v.astype(jnp.bfloat16)).astype(jnp.float32)

@jax.custom_vjp
def low_back(v):
    return v

def low_keep(v):
    return (low(v), None)

def low_pass(kept, grad):
    return (grad,)

def back_keep(v):
    return (v, None)

def back_low(kept, grad):
    return (low(grad),)
low.defvjp(low_keep, low_pass)
low_back.defvjp(back_keep, back_low)

def rounded_both(value):
    return low(low_back(value))

def matmul(left, right):
    return jnp.dot(left, right, precision=lax.Precision.HIGHEST, preferred_element_type=jnp.float32)

def layer_norm(hidden, gain_row, bias_row):
    center = hidden - lax.optimization_barrier(jnp.mean(hidden, axis=-1, keepdims=True))
    spread = lax.optimization_barrier(jnp.mean(center * center, axis=-1, keepdims=True))
    return center * lax.rsqrt(spread + 1e-05) * gain_row + bias_row

def attention(queries, key_rows, value_rows, allowed):
    query_count = queries.shape[0]
    key_count = key_rows.shape[0]
    heads_q = queries.reshape(query_count, HEADS, HEAD_DIM)
    heads_k = key_rows.reshape(key_count, HEADS, HEAD_DIM)
    heads_v = value_rows.reshape(key_count, HEADS, HEAD_DIM)
    scores = jnp.einsum('qhe,khe->hqk', heads_q, heads_k, precision=lax.Precision.HIGHEST) * (1.0 / math.sqrt(HEAD_DIM))
    scores = low_back(scores)
    masked = jnp.where(allowed[None], scores, -1e+30)
    row_top = lax.optimization_barrier(jnp.max(masked, axis=-1, keepdims=True))
    weights_exp = jnp.where(allowed[None], jnp.exp(masked - row_top), 0.0)
    weights = low(weights_exp / lax.optimization_barrier(jnp.sum(weights_exp, axis=-1, keepdims=True)))
    mixture = jnp.einsum('hqk,khe->qhe', weights, heads_v, precision=lax.Precision.HIGHEST)
    return rounded_both(mixture.reshape(query_count, HEADS * HEAD_DIM))

def feed_forward(normed, weight_in, weight_out):
    inner_pre = low_back(matmul(low(normed), weight_in))
    active = low(jax.nn.gelu(inner_pre, approximate=True))
    return low_back(matmul(active, weight_out))

def encode(params, inputs, lengths):
    qkv_w, out_w, ffn_in, ffn_out, norm_params = params
    places = jnp.arange(TOK_DEV, dtype=jnp.int32)
    starts = (jnp.cumsum(lengths) - lengths).astype(jnp.int32)
    segment = lax.optimization_barrier(jnp.sum((places[:, None] >= starts[None, :]).astype(jnp.int32), axis=1))
    allowed = segment[:, None] == segment[None, :]
    queries = rounded_both(matmul(inputs, qkv_w[0]))
    key_rows = rounded_both(matmul(inputs, qkv_w[1]))
    value_rows = rounded_both(matmul(inputs, qkv_w[2]))
    branch = low_back(matmul(attention(queries, key_rows, value_rows, allowed), out_w))
    normed = layer_norm(inputs + branch, norm_params[0, 0], norm_params[0, 1])
    result = layer_norm(normed + feed_forward(normed, ffn_in, ffn_out), norm_params[1, 0], norm_params[1, 1])
    memory = rounded_both(result)
    padded = jnp.concatenate([memory, jnp.zeros((LMAX, D), memory.dtype)], axis=0)
    return jnp.stack([lax.dynamic_slice_in_dim(padded, starts[slot_index], LMAX, 0) for slot_index in range(SEQ_DEV)])

def decode(params, inputs, marked, lengths, memory, memory_slot):
    self_qkv, self_out, cross_w, cross_o, ffn_in, ffn_out, norm_params, mask_row = params
    places = jnp.arange(TOK_DEV, dtype=jnp.int32)
    slot_of = places // TSLOT
    inside = places % TSLOT
    slot_ids = jnp.arange(SEQ_DEV, dtype=jnp.int32)
    live_rows = jnp.any((slot_of[:, None] == slot_ids[None, :]) & (inside[:, None] < lengths[None, :]), axis=1)
    allowed = (slot_of[:, None] == slot_of[None, :]) & live_rows[None, :]
    start_rows = jnp.where(marked[:, None] == 1, mask_row[None, :], inputs)
    queries = rounded_both(matmul(start_rows, self_qkv[0]))
    key_rows = rounded_both(matmul(start_rows, self_qkv[1]))
    value_rows = rounded_both(matmul(start_rows, self_qkv[2]))
    branch = low_back(matmul(attention(queries, key_rows, value_rows, allowed), self_out))
    first_rows = layer_norm(start_rows + branch, norm_params[0, 0], norm_params[0, 1])
    memory_rows = memory.reshape(N_FSDP * LMAX, D)
    cross_allowed = memory_slot.reshape(-1)[None, :] == slot_of[:, None]
    cross_q = rounded_both(matmul(low(first_rows), cross_w[0]))
    cross_k = rounded_both(matmul(memory_rows, cross_w[1]))
    cross_v = rounded_both(matmul(memory_rows, cross_w[2]))
    branch = low_back(matmul(attention(cross_q, cross_k, cross_v, cross_allowed), cross_o))
    second_rows = layer_norm(first_rows + branch, norm_params[1, 0], norm_params[1, 1])
    return layer_norm(second_rows + feed_forward(second_rows, ffn_in, ffn_out), norm_params[2, 0], norm_params[2, 1])

def group_pass(params, group_block):
    enc_params, dec_params = params
    enc_rows, dec_rows, marked, src_len, tgt_len, route_code = group_block
    pieces = jax.vmap(encode, in_axes=(None, 0, 0))(enc_params, enc_rows, src_len)
    dest_dev = route_code // SEQ_DEV
    dest_slot = route_code % SEQ_DEV
    piece_rows = jnp.arange(LMAX, dtype=jnp.int32)
    key_slot = jnp.where(piece_rows[None, None, :] < src_len[:, :, None], dest_slot[:, :, None], -1)
    pick_table = dest_dev[:, :, None] == jnp.arange(N_FSDP, dtype=jnp.int32)[None, None, :]
    received = jnp.einsum('skd,sklc->dslc', pick_table.astype(jnp.float32), pieces, precision=lax.Precision.HIGHEST)
    received_slot = lax.optimization_barrier(jnp.sum(jnp.where(pick_table[:, :, :, None], key_slot[:, :, None, :], 0), axis=1)).transpose(1, 0, 2)
    return jax.vmap(decode, in_axes=(None, 0, 0, 0, 0, 0))(dec_params, dec_rows, marked, tgt_len, received, received_slot)

def reference(enc_input, dec_input, target_mask, src_lengths, tgt_lengths, memory_route, enc_qkv, enc_out, enc_ffn_in, enc_ffn_out, enc_norms, dec_qkv, dec_out, cross_qkv, cross_out, dec_ffn_in, dec_ffn_out, dec_norms, mask_vector, out_cotangent):
    row_shape = (N_DP, N_FSDP, TOK_DEV, D)
    int_shape = (N_DP, N_FSDP, SEQ_DEV)
    enc_params = tuple((weight.astype(jnp.float32) for weight in (enc_qkv, enc_out, enc_ffn_in, enc_ffn_out, enc_norms)))
    dec_params = tuple((weight.astype(jnp.float32) for weight in (dec_qkv, dec_out, cross_qkv, cross_out, dec_ffn_in, dec_ffn_out, dec_norms, mask_vector)))
    int_args = (target_mask.reshape(N_DP, N_FSDP, TOK_DEV), src_lengths.reshape(int_shape), tgt_lengths.reshape(int_shape), memory_route.reshape(int_shape))

    def forward(params, enc_rows, dec_rows):

        def one_group(group_block):
            return jax.checkpoint(group_pass)(params, group_block)
        return lax.map(one_group, (enc_rows, dec_rows) + int_args)
    result, pullback = jax.vjp(forward, (enc_params, dec_params), enc_input.astype(jnp.float32).reshape(row_shape), dec_input.astype(jnp.float32).reshape(row_shape))
    weight_grads, enc_grad, dec_grad = pullback(out_cotangent.astype(jnp.float32).reshape(row_shape))
    enc_g, dec_g = weight_grads
    return (result.reshape(TOKENS, D).astype(jnp.bfloat16), enc_grad.reshape(TOKENS, D), dec_grad.reshape(TOKENS, D), enc_g[0], enc_g[1], enc_g[2], enc_g[3], enc_g[4], dec_g[0], dec_g[1], dec_g[2], dec_g[3], dec_g[4], dec_g[5], dec_g[6], dec_g[7])
```

```python
from functools import partial
import math

import jax
import jax.numpy as jnp
from jax import lax
from jax.sharding import PartitionSpec as P

HEADS = 8
HEAD_DIM = 64
SCALE = 1.0 / math.sqrt(HEAD_DIM)
AXES = ("dp", "fsdp")
F32 = jnp.float32
BF16 = jnp.bfloat16


def layer_norm(hidden, gain_row, bias_row):
    center = hidden - jnp.mean(hidden, axis=-1, keepdims=True)
    spread = jnp.mean(center * center, axis=-1, keepdims=True)
    return center * lax.rsqrt(spread + 1e-05) * gain_row + bias_row


def project(row_block, weight):
    return jnp.dot(row_block, weight, preferred_element_type=F32)


def project_back(grad_block, weight):
    return lax.dot_general(grad_block, weight, (((1,), (1,)), ((), ())), preferred_element_type=F32)


def weight_grad(row_block, grad_block):
    return lax.dot_general(row_block, grad_block, (((0,), (0,)), ((), ())), preferred_element_type=F32)


def split_heads(rows):
    return rows.reshape(rows.shape[:-1] + (HEADS, HEAD_DIM))


def attend(queries, key_rows, value_rows, allowed):
    scores = jnp.einsum(
        "bqhe,bkhe->bhqk", split_heads(queries), split_heads(key_rows), preferred_element_type=F32
    )
    masked = jnp.where(allowed[:, None], scores * SCALE, -1e30)
    row_top = jnp.max(masked, axis=-1, keepdims=True)
    weights_exp = jnp.where(allowed[:, None], jnp.exp(masked - row_top), 0.0)
    row_total = jnp.sum(weights_exp, axis=-1, keepdims=True)
    weights = (weights_exp / row_total).astype(BF16)
    mixture = jnp.einsum("bhqk,bkhe->bqhe", weights, split_heads(value_rows), preferred_element_type=F32)
    return mixture.reshape(queries.shape).astype(BF16), row_top + jnp.log(row_total)


def attend_back(queries, key_rows, value_rows, allowed, log_total, grad_out):
    heads_q, heads_k, heads_v = split_heads(queries), split_heads(key_rows), split_heads(value_rows)
    grad_heads = split_heads(grad_out)
    scores = jnp.einsum("bqhe,bkhe->bhqk", heads_q, heads_k, preferred_element_type=F32) * SCALE
    weights = jnp.where(allowed[:, None], jnp.exp(scores - log_total), 0.0)
    grad_weights = jnp.einsum("bqhe,bkhe->bhqk", grad_heads, heads_v, preferred_element_type=F32)
    row_delta = jnp.sum(weights * grad_weights, axis=-1, keepdims=True)
    grad_scores = (weights * (grad_weights - row_delta)).astype(BF16)
    grad_query = jnp.einsum("bhqk,bkhe->bqhe", grad_scores, heads_k, preferred_element_type=F32) * SCALE
    grad_key = jnp.einsum("bhqk,bqhe->bkhe", grad_scores, heads_q, preferred_element_type=F32) * SCALE
    grad_value = jnp.einsum("bhqk,bqhe->bkhe", weights.astype(BF16), grad_heads, preferred_element_type=F32)
    return (
        grad_query.reshape(queries.shape).astype(BF16),
        grad_key.reshape(key_rows.shape).astype(BF16),
        grad_value.reshape(key_rows.shape).astype(BF16),
    )


def ffn_forward(normed_low, weight_in, weight_out):
    inner_pre = project(normed_low, weight_in)
    active = jax.nn.gelu(inner_pre, approximate=True).astype(BF16)
    return project(active, weight_out)


def ffn_back(normed_low, weight_in, weight_out, grad_out):
    inner_pre = project(normed_low, weight_in)
    active, gelu_back = jax.vjp(partial(jax.nn.gelu, approximate=True), inner_pre)
    grad_low = grad_out.astype(BF16)
    grad_w_out = weight_grad(active.astype(BF16), grad_low)
    grad_active = project_back(grad_low, weight_out)
    grad_inner = gelu_back(grad_active)[0].astype(BF16)
    grad_w_in = weight_grad(normed_low, grad_inner)
    return project_back(grad_inner, weight_in), grad_w_in, grad_w_out


def exchange(block, pairs):
    return lax.ppermute(block, AXES, pairs)


def pick(blocks, place):
    return lax.dynamic_index_in_dim(blocks, place, 0, keepdims=False)


def added(one, other):
    return (one.astype(F32) + other.astype(F32)).astype(BF16)


RING = (0, 1, 3, 2)


def sum_scatter(blocks, count):
    me = lax.axis_index(AXES)
    core, low, high = me % 2, (me // 2) % 2, (me // 4) % 2
    rest = count // 8
    tail = blocks.shape[1:]
    by_core = blocks.reshape((rest * 4, 2) + tail)
    sent = lax.dynamic_index_in_dim(by_core, 1 - core, 1, keepdims=False)
    kept = lax.dynamic_index_in_dim(by_core, core, 1, keepdims=False)
    kept = added(kept, exchange(sent, [(i, i ^ 1) for i in range(count)]))
    quads = kept.reshape((rest, 4) + tail)

    def two(first, second):
        parts = [lax.dynamic_index_in_dim(quads, place, 1, keepdims=True) for place in (first, second)]
        return jnp.concatenate(parts, axis=1)

    other_high, other_low = 1 - high, 1 - low
    sent = two(
        jnp.where(core == 0, 2 * other_high, other_low),
        jnp.where(core == 0, 2 * other_high + 1, other_low + 2),
    )
    kept = two(jnp.where(core == 0, 2 * high, low), jnp.where(core == 0, 2 * high + 1, low + 2))
    kept = added(kept, exchange(sent, [(i, i ^ (2 if i % 2 else 4)) for i in range(count)]))
    mine = jnp.where(core == 0, low, high)
    sent = lax.dynamic_index_in_dim(kept, 1 - mine, 1, keepdims=False)
    kept = lax.dynamic_index_in_dim(kept, mine, 1, keepdims=False)
    kept = added(kept, exchange(sent, [(i, i ^ (4 if i % 2 else 2)) for i in range(count)]))
    stride = 8
    while rest > 4:
        bit = (me // stride) % 2
        halves = kept.reshape((rest // 2, 2) + tail)
        sent = lax.dynamic_index_in_dim(halves, 1 - bit, 1, keepdims=False)
        kept = lax.dynamic_index_in_dim(halves, bit, 1, keepdims=False)
        kept = added(kept, exchange(sent, [(i, i ^ stride) for i in range(count)]))
        rest, stride = rest // 2, stride * 2
    order = RING if rest == 4 else tuple(range(rest))
    place_of = jnp.asarray([order.index(z) for z in range(rest)], jnp.int32)
    ring = jnp.asarray(order, jnp.int32)
    here = place_of[me // stride]
    onward = [
        (i, order[(order.index(i // stride) + 1) % rest] * stride + i % stride) for i in range(count)
    ]
    moving = pick(kept, ring[(here - 1) % rest]) if rest > 1 else kept[0]
    for step in range(rest - 1):
        arrived = exchange(moving, onward)
        own = pick(kept, ring[(here - 2 - step) % rest])
        moving = arrived.astype(F32) + own.astype(F32)
        if step < rest - 2:
            moving = moving.astype(BF16)
    return moving.astype(F32)


def on_device(
    enc_input,
    dec_input,
    target_mask,
    src_lengths,
    tgt_lengths,
    memory_route,
    enc_qkv,
    enc_out,
    enc_ffn_in,
    enc_ffn_out,
    enc_norms,
    dec_qkv,
    dec_out,
    cross_qkv,
    cross_out,
    dec_ffn_in,
    dec_ffn_out,
    dec_norms,
    mask_vector,
    out_cotangent,
):
    dp_count, groups = lax.axis_size("dp"), lax.axis_size("fsdp")
    count = dp_count * groups
    rows, width = enc_input.shape
    slots = src_lengths.shape[1]
    longest = rows // 2
    slot_rows = rows // slots
    part = enc_out.shape[0]
    inner = enc_ffn_in.shape[1]
    pieces_in = inner // width

    def square(weight):
        return weight.reshape(-1, width)

    def wide(weight):
        return weight.reshape(part, pieces_in, width).transpose(1, 0, 2).reshape(-1, width)

    small = jnp.concatenate(
        [
            enc_norms.reshape(-1),
            dec_norms.reshape(-1),
            mask_vector.reshape(-1),
            src_lengths[0].astype(BF16),
            memory_route[0].astype(BF16),
        ]
    )
    small_used = small.shape[0]
    small = jnp.pad(small, (0, part * width - small_used)).reshape(part, width)
    enc_pack = jnp.concatenate([square(enc_qkv), enc_out, wide(enc_ffn_in), enc_ffn_out, small])
    dec_pack = jnp.concatenate(
        [square(dec_qkv), dec_out, square(cross_qkv), cross_out, wide(dec_ffn_in), dec_ffn_out]
    )
    enc_all = lax.all_gather(enc_pack, AXES, axis=0, tiled=False)
    dec_all = lax.all_gather(dec_pack, AXES, axis=0, tiled=False)

    def block(gathered, first):
        return gathered[:, first * part : (first + 1) * part].reshape(width, width)

    def wide_block(gathered, first):
        picked = gathered[:, first * part : (first + pieces_in) * part]
        picked = picked.reshape(count, pieces_in, part, width).transpose(0, 2, 1, 3)
        return picked.reshape(width, inner)

    def tall_block(gathered, first):
        return gathered[:, first * part : (first + pieces_in) * part].reshape(inner, width)

    e_q, e_k, e_v, e_out = [block(enc_all, i) for i in range(4)]
    e_in, e_outff = wide_block(enc_all, 4), tall_block(enc_all, 4 + pieces_in)
    small_all = enc_all[:, (4 + 2 * pieces_in) * part :].reshape(count, part * width)[:, :small_used]
    at = 0

    def take(length):
        nonlocal at
        at += length
        return small_all[:, at - length : at]

    def table(layers):
        return take(layers * 2 * part).reshape(count, layers * 2, part).transpose(1, 0, 2).reshape(
            layers, 2, width
        ).astype(F32)

    e_norm = table(enc_norms.shape[0])
    d_norm = table(dec_norms.shape[0])
    mask_full = take(part).reshape(width)
    my_dp, my_group = lax.axis_index("dp"), lax.axis_index("fsdp")
    lengths_near = pick(take(slots).astype(jnp.int32).reshape(dp_count, groups, slots), my_dp)
    route_near = pick(take(slots).astype(jnp.int32).reshape(dp_count, groups, slots), my_dp)

    src_len = src_lengths[0]
    starts = jnp.cumsum(src_len) - src_len
    places = jnp.arange(rows, dtype=jnp.int32)
    segment = jnp.sum((places[:, None] >= starts[None, :]).astype(jnp.int32), axis=1)
    enc_allowed = (segment[:, None] == segment[None, :])[None]
    e_qkv = jnp.concatenate([e_q, e_k, e_v], axis=1)
    enc_proj = project(enc_input, e_qkv).astype(BF16)
    eq, ek, ev = [enc_proj[None, :, i * width : (i + 1) * width] for i in range(3)]
    enc_mixture, enc_total = attend(eq, ek, ev, enc_allowed)
    enc_first, enc_norm_one = jax.vjp(
        layer_norm, enc_input.astype(F32) + project(enc_mixture[0], e_out), e_norm[0, 0], e_norm[0, 1]
    )
    enc_first_low = enc_first.astype(BF16)
    enc_second, enc_norm_two = jax.vjp(
        layer_norm, enc_first + ffn_forward(enc_first_low, e_in, e_outff), e_norm[1, 0], e_norm[1, 1]
    )
    memory = enc_second.astype(BF16)

    padded = jnp.concatenate([memory, jnp.zeros((longest, width), BF16)], axis=0)
    dest_dev = memory_route[0] // slots
    ids = jnp.arange(groups, dtype=jnp.int32)
    piece_starts = jnp.sum(jnp.where(dest_dev[None, :] == ids[:, None], starts[None, :], 0), axis=1)
    pieces = jnp.stack(
        [lax.dynamic_slice_in_dim(padded, piece_starts[g], longest, 0) for g in range(groups)]
    )
    memory_in = lax.all_to_all(pieces, "fsdp", split_axis=0, concat_axis=0, tiled=True)
    to_me = route_near // slots == my_group
    source_slot = jnp.sum(jnp.where(to_me, route_near % slots, 0), axis=1)
    source_len = jnp.sum(jnp.where(to_me, lengths_near, 0), axis=1)
    chosen = source_slot[None, :] == jnp.arange(slots, dtype=jnp.int32)[:, None]
    slot_source = jnp.sum(jnp.where(chosen, ids[None, :], 0), axis=1)
    slot_len = jnp.sum(jnp.where(chosen, source_len[None, :], 0), axis=1)

    d_blocks = [block(dec_all, i) for i in range(8)]
    d_in, d_outff = wide_block(dec_all, 8), tall_block(dec_all, 8 + pieces_in)
    d_out, c_out = d_blocks[3], d_blocks[7]
    marked = target_mask[:, None] == 1
    start_rows = jnp.where(marked, mask_full[None, :], dec_input)
    d_qkv = jnp.concatenate(d_blocks[:3], axis=1)
    dec_proj = project(start_rows, d_qkv).astype(BF16)
    by_slot = (slots, slot_rows, width)
    dq, dk, dv = [dec_proj[:, i * width : (i + 1) * width].reshape(by_slot) for i in range(3)]
    inside = jnp.arange(slot_rows, dtype=jnp.int32)
    dec_allowed = jnp.broadcast_to(
        inside[None, None, :] < tgt_lengths[0][:, None, None], (slots, slot_rows, slot_rows)
    )
    dec_mixture, dec_total = attend(dq, dk, dv, dec_allowed)
    dec_mixture = dec_mixture.reshape(rows, width)
    dec_first, dec_norm_one = jax.vjp(
        layer_norm, start_rows.astype(F32) + project(dec_mixture, d_out), d_norm[0, 0], d_norm[0, 1]
    )
    dec_first_low = dec_first.astype(BF16)

    memory_rows = jnp.stack([pick(memory_in, slot_source[s]) for s in range(slots)]).reshape(
        slots * longest, width
    )
    piece_rows = jnp.arange(longest, dtype=jnp.int32)
    cross_allowed = jnp.broadcast_to(
        piece_rows[None, None, :] < slot_len[:, None, None], (slots, slot_rows, longest)
    )
    cq = project(dec_first_low, d_blocks[4]).astype(BF16).reshape(by_slot)
    c_kv = jnp.concatenate(d_blocks[5:7], axis=1)
    cross_kv = project(memory_rows, c_kv).astype(BF16)
    ck = cross_kv[:, :width].reshape(slots, longest, width)
    cv = cross_kv[:, width:].reshape(slots, longest, width)
    cross_mixture, cross_total = attend(cq, ck, cv, cross_allowed)
    cross_mixture = cross_mixture.reshape(rows, width)
    dec_second, dec_norm_two = jax.vjp(
        layer_norm, dec_first + project(cross_mixture, c_out), d_norm[1, 0], d_norm[1, 1]
    )
    dec_second_low = dec_second.astype(BF16)
    dec_third, dec_norm_three = jax.vjp(
        layer_norm, dec_second + ffn_forward(dec_second_low, d_in, d_outff), d_norm[2, 0], d_norm[2, 1]
    )
    dec_output = dec_third.astype(BF16)

    def cut(grad):
        return grad.astype(BF16).reshape(count, -1, width)

    def cut_wide(grad):
        grad = grad.astype(BF16).reshape(count, part, pieces_in, width)
        return grad.transpose(0, 2, 1, 3).reshape(count, pieces_in * part, width)

    def cut_columns(grad):
        return cut_wide(grad) if grad.shape[1] == inner else (
            grad.astype(BF16).reshape(count, part, -1, width).transpose(0, 2, 1, 3).reshape(count, -1, width)
        )

    def cut_small(rows_of):
        stacked = jnp.stack(rows_of).astype(BF16).reshape(-1, count, part).transpose(1, 0, 2)
        stacked = stacked.reshape(count, -1)
        return jnp.pad(stacked, ((0, 0), (0, part * width - stacked.shape[1]))).reshape(count, part, width)

    grad_third_in, gain_three, bias_three = dec_norm_three(out_cotangent.astype(F32))
    grad_from_ffn, grad_dec_ffn_in, grad_dec_ffn_out = ffn_back(dec_second_low, d_in, d_outff, grad_third_in)
    grad_second_in, gain_two, bias_two = dec_norm_two(grad_third_in + grad_from_ffn)
    grad_branch = grad_second_in.astype(BF16)
    grad_cross_out = weight_grad(cross_mixture, grad_branch)
    grad_cross_mix = project_back(grad_branch, c_out).astype(BF16)
    grad_cq, grad_ck, grad_cv = attend_back(
        cq, ck, cv, cross_allowed, cross_total, grad_cross_mix.reshape(by_slot)
    )
    grad_cq = grad_cq.reshape(rows, width)
    grad_ckv = jnp.concatenate(
        [grad_ck.reshape(slots * longest, width), grad_cv.reshape(slots * longest, width)], axis=1
    )
    grad_cross_q = weight_grad(dec_first_low, grad_cq)
    grad_cross_kv = weight_grad(memory_rows, grad_ckv)
    grad_memory = project_back(grad_ckv, c_kv).astype(BF16).reshape(slots, longest, width)
    grad_memory = jnp.stack([pick(grad_memory, source_slot[g]) for g in range(groups)])
    returned = lax.all_to_all(grad_memory, "fsdp", split_axis=0, concat_axis=0, tiled=True)
    first_sum = sum_scatter(
        jnp.concatenate(
            [
                cut(grad_cross_q),
                cut_columns(grad_cross_kv),
                cut(grad_cross_out),
                cut_wide(grad_dec_ffn_in),
                cut(grad_dec_ffn_out),
            ],
            axis=1,
        ),
        count,
    )
    grad_first_in, gain_one, bias_one = dec_norm_one(grad_second_in + project_back(grad_cq, d_blocks[4]))
    grad_branch = grad_first_in.astype(BF16)
    grad_dec_out = weight_grad(dec_mixture, grad_branch)
    grad_dec_mix = project_back(grad_branch, d_out).astype(BF16)
    grad_self = attend_back(dq, dk, dv, dec_allowed, dec_total, grad_dec_mix.reshape(by_slot))
    grad_proj = jnp.concatenate([g.reshape(rows, width) for g in grad_self], axis=1)
    grad_dec_qkv = weight_grad(start_rows, grad_proj)
    grad_start = grad_first_in + project_back(grad_proj, d_qkv)
    dec_input_grad = jnp.where(marked, 0.0, grad_start)
    grad_mask = jnp.sum(jnp.where(marked, grad_start, 0.0), axis=0)

    grad_padded = jnp.zeros((rows + longest, width), F32)
    for g in range(groups):
        current = lax.dynamic_slice_in_dim(grad_padded, piece_starts[g], longest, 0)
        grad_padded = lax.dynamic_update_slice_in_dim(
            grad_padded, current + returned[g].astype(F32), piece_starts[g], 0
        )
    grad_enc_second_in, enc_gain_two, enc_bias_two = enc_norm_two(grad_padded[:rows])
    grad_from_ffn, grad_enc_ffn_in, grad_enc_ffn_out = ffn_back(
        enc_first_low, e_in, e_outff, grad_enc_second_in
    )
    second_sum = sum_scatter(
        jnp.concatenate(
            [
                cut_columns(grad_dec_qkv),
                cut(grad_dec_out),
                cut_wide(grad_enc_ffn_in),
                cut(grad_enc_ffn_out),
            ],
            axis=1,
        ),
        count,
    )
    grad_enc_first_in, enc_gain_one, enc_bias_one = enc_norm_one(grad_enc_second_in + grad_from_ffn)
    grad_branch = grad_enc_first_in.astype(BF16)
    grad_enc_out = weight_grad(enc_mixture[0], grad_branch)
    grad_enc_mix = project_back(grad_branch, e_out).astype(BF16)
    grad_enc = attend_back(eq, ek, ev, enc_allowed, enc_total, grad_enc_mix[None])
    grad_proj = jnp.concatenate([g[0] for g in grad_enc], axis=1)
    grad_enc_qkv = weight_grad(enc_input, grad_proj)
    enc_input_grad = grad_enc_first_in + project_back(grad_proj, e_qkv)
    small_rows = [
        enc_gain_one,
        enc_bias_one,
        enc_gain_two,
        enc_bias_two,
        gain_one,
        bias_one,
        gain_two,
        bias_two,
        gain_three,
        bias_three,
        grad_mask,
    ]
    third_sum = sum_scatter(
        jnp.concatenate([cut_columns(grad_enc_qkv), cut(grad_enc_out), cut_small(small_rows)], axis=1), count
    )

    def piece(summed, first, pieces=1):
        return summed[first * part : (first + pieces) * part]

    def wide_piece(summed, first):
        picked = piece(summed, first, pieces_in).reshape(pieces_in, part, width)
        return picked.transpose(1, 0, 2).reshape(part, inner)

    small_sum = piece(third_sum, 4).reshape(-1)[: len(small_rows) * part].reshape(-1, part)
    return (
        dec_output,
        enc_input_grad,
        dec_input_grad,
        piece(third_sum, 0, 3).reshape(3, part, width),
        piece(third_sum, 3),
        wide_piece(second_sum, 4),
        piece(second_sum, 4 + pieces_in, pieces_in),
        small_sum[:4].reshape(2, 2, part),
        piece(second_sum, 0, 3).reshape(3, part, width),
        piece(second_sum, 3),
        piece(first_sum, 0, 3).reshape(3, part, width),
        piece(first_sum, 3),
        wide_piece(first_sum, 4),
        piece(first_sum, 4 + pieces_in, pieces_in),
        small_sum[4:10].reshape(3, 2, part),
        small_sum[10],
    )


def solution(mesh):
    rows = P(AXES, None)
    flat = P(AXES)
    cube = P(None, AXES, None)
    norm = P(None, None, AXES)
    in_specs = (
        (rows, rows, flat, rows, rows, rows)
        + (cube, rows, rows, rows, norm)
        + (cube, rows, cube, rows, rows, rows, norm, flat)
        + (rows,)
    )
    out_specs = (
        (rows, rows, rows)
        + (cube, rows, rows, rows, norm)
        + (cube, rows, cube, rows, rows, rows, norm, flat)
    )
    return jax.shard_map(on_device, mesh=mesh, in_specs=in_specs, out_specs=out_specs, check_vma=False)
```

```python
import math

import jax
import jax.numpy as jnp
from jax import lax
from jax.experimental import pallas as pl
from jax.experimental.pallas import tpu as pltpu
from jax.sharding import PartitionSpec as P

HEADS = 8
HEAD_DIM = 64
SCALE = 1.0 / math.sqrt(HEAD_DIM)
AXES = ("dp", "fsdp")
F32 = jnp.float32
BF16 = jnp.bfloat16


MASKED = -1e30
GELU_C = math.sqrt(2.0 / math.pi)
GELU_A = 0.044715


def nn(left, right):
    return jnp.dot(left, right, preferred_element_type=F32)


def nt(left, right):
    return lax.dot_general(left, right, (((1,), (1,)), ((), ())), preferred_element_type=F32)


def norm_parts(hidden):
    center = hidden - jnp.mean(hidden, axis=-1, keepdims=True)
    scale = lax.rsqrt(jnp.mean(center * center, axis=-1, keepdims=True) + 1e-05)
    return center * scale, scale


def norm_back(grad, unit, scale, gain):
    inner = grad * gain
    mean_one = jnp.mean(inner, axis=-1, keepdims=True)
    mean_two = jnp.mean(inner * unit, axis=-1, keepdims=True)
    return (
        scale * (inner - mean_one - unit * mean_two),
        jnp.sum(grad * unit, axis=0, keepdims=True),
        jnp.sum(grad, axis=0, keepdims=True),
    )


def gelu_tanh(pre):
    return jnp.tanh(GELU_C * (pre + GELU_A * (pre * pre * pre)))


def gelu_back(pre):
    tanh = gelu_tanh(pre)
    slope = GELU_C * (1.0 + 3.0 * GELU_A * (pre * pre))
    return 0.5 * pre * (1.0 + tanh), 0.5 * (1.0 + tanh) + 0.5 * pre * (1.0 - tanh * tanh) * slope


def block(ref, first):
    width = ref.shape[2]
    part = width // ref.shape[0]
    return ref[:, first * part : (first + 1) * part, :].reshape(width, width)


def tall(ref, index, first):
    count, _, width = ref.shape
    part = width // count
    pieces = 4
    some = count // pieces
    picked = ref[index * some : (index + 1) * some, first * part : (first + pieces) * part, :]
    return picked.reshape(width, width)


def put(ref, first, grad):
    count, _, width = ref.shape
    part = width // count
    ref[:, first * part : (first + 1) * part, :] = grad.astype(BF16).reshape(count, part, width)


def put_tall(ref, index, first, grad):
    count, _, width = ref.shape
    part = width // count
    pieces = 4
    some = count // pieces
    ref[index * some : (index + 1) * some, first * part : (first + pieces) * part, :] = grad.astype(
        BF16
    ).reshape(some, pieces * part, width)


def put_rows(ref, first, rows_of):
    count, _, width = ref.shape
    part = width // count
    used = sum(row.shape[0] for row in rows_of)
    rows = jnp.concatenate(rows_of + [jnp.zeros((part - used, width), F32)], axis=0)
    ref[:, first * part : (first + 1) * part, :] = jnp.broadcast_to(
        rows.astype(BF16)[None], (count, part, width)
    )


PAIR = 2 * HEAD_DIM


def twice(pair_rows):
    lane = lax.broadcasted_iota(jnp.int32, pair_rows.shape, 1)
    zero = jnp.zeros_like(pair_rows)
    return jnp.concatenate(
        [jnp.where(lane < HEAD_DIM, pair_rows, zero), jnp.where(lane < HEAD_DIM, zero, pair_rows)], axis=0
    )


def pair_forward(queries, keys, values, bias):
    count = keys.shape[0]
    scores = nt(queries, twice(keys))
    parts, logs = [], []
    for head in range(2):
        masked = scores[:, head * count : (head + 1) * count] + bias
        top = jnp.max(masked, axis=-1, keepdims=True)
        raised = jnp.exp(masked - top)
        total = jnp.sum(raised, axis=-1, keepdims=True)
        parts.append(raised * (1.0 / total))
        logs.append(top + jnp.log(total))
    low = jnp.concatenate([part.astype(BF16) for part in parts], axis=1)
    return nn(low, twice(values)), parts, logs


def pair_weights(queries, keys, bias, logs):
    count = keys.shape[0]
    scores = nt(queries, twice(keys))
    return [
        jnp.exp(scores[:, head * count : (head + 1) * count] + bias - logs[head]) for head in range(2)
    ]


def unmix(turned, count):
    both = jnp.concatenate(
        [turned[:HEAD_DIM, :count], turned[HEAD_DIM:, count:]], axis=0
    )
    return both.T


def pair_backward(queries, keys, values, parts, grad_out):
    count = keys.shape[0]
    grad_weights = nt(grad_out, twice(values))
    grad_scores = []
    for head in range(2):
        grad_part = grad_weights[:, head * count : (head + 1) * count]
        delta = jnp.sum(parts[head] * grad_part, axis=-1, keepdims=True)
        grad_scores.append((parts[head] * (grad_part - delta)).astype(BF16))
    grad_scores = jnp.concatenate(grad_scores, axis=1)
    weights = jnp.concatenate([part.astype(BF16) for part in parts], axis=1)
    grad_query = nn(grad_scores, twice(keys)) * SCALE
    grad_key = unmix(nn(queries.T, grad_scores), count)
    grad_value = unmix(nn(grad_out.T, weights), count)
    return grad_query.astype(BF16), grad_key.astype(BF16), grad_value.astype(BF16)


def segment_bias(starts, rows):
    down = lax.broadcasted_iota(jnp.int32, (rows, 1), 0)
    across = lax.broadcasted_iota(jnp.int32, (1, rows), 1)
    segment_down = jnp.zeros_like(down)
    segment_across = jnp.zeros_like(across)
    for sentence in range(1, starts.shape[0]):
        segment_down += (down >= starts[sentence]).astype(jnp.int32)
        segment_across += (across >= starts[sentence]).astype(jnp.int32)
    return jnp.where(segment_down == segment_across, 0.0, MASKED)


def lanes(pair):
    return slice(pair * PAIR, (pair + 1) * PAIR)


def encoder_forward(
    starts, piece_starts, x_ref, weight_ref, norm_ref,
    pieces_ref, qkv_ref, mix_ref, log_ref, hidden_one_ref, hidden_two_ref, bias_ref, active_ref,
):
    rows, width = x_ref.shape
    longest = pieces_ref.shape[1]
    rows_in = x_ref[...]
    bias_ref[...] = segment_bias(starts, rows)
    qkv_ref[0] = (nn(rows_in, block(weight_ref, 0)) * SCALE).astype(BF16)
    qkv_ref[1] = nn(rows_in, block(weight_ref, 1)).astype(BF16)
    qkv_ref[2] = nn(rows_in, block(weight_ref, 2)).astype(BF16)
    for pair in range(HEADS // 2):
        at = lanes(pair)
        mixture, _, logs = pair_forward(qkv_ref[0, :, at], qkv_ref[1, :, at], qkv_ref[2, :, at], bias_ref[...])
        mix_ref[:, at] = mixture.astype(BF16)
        for head in range(2):
            log_ref[:, 2 * pair + head : 2 * pair + head + 1] = logs[head]
    hidden = rows_in.astype(F32) + nn(mix_ref[...], block(weight_ref, 3))
    hidden_one_ref[...] = hidden
    unit, _ = norm_parts(hidden)
    first = unit * norm_ref[0:1, :] + norm_ref[1:2, :]
    low = first.astype(BF16)
    for j in range(4):
        pre = nn(low, block(weight_ref, 4 + j))
        active_ref[:, j * width : (j + 1) * width] = (0.5 * pre * (1.0 + gelu_tanh(pre))).astype(BF16)
    hidden = first
    for j in range(4):
        hidden = hidden + nn(active_ref[:, j * width : (j + 1) * width], tall(weight_ref, j, 8))
    hidden_two_ref[...] = hidden
    unit, _ = norm_parts(hidden)
    memory = (unit * norm_ref[2:3, :] + norm_ref[3:4, :]).astype(BF16)
    down = lax.broadcasted_iota(jnp.int32, (longest, rows), 0)
    across = lax.broadcasted_iota(jnp.int32, (longest, rows), 1)
    for g in range(pieces_ref.shape[0]):
        chosen = jnp.where(across - down == piece_starts[g], 1.0, 0.0).astype(BF16)
        pieces_ref[g] = nn(chosen, memory).astype(BF16)


def replaced(marked_ref, mask_ref, rows_ref):
    marked = marked_ref[...] == 1
    return jnp.where(marked, mask_ref[...].astype(F32), rows_ref[...].astype(F32))


def slot_bias(length, count):
    across = lax.broadcasted_iota(jnp.int32, (1, count), 1)
    return jnp.where(across < length, 0.0, MASKED)


def self_forward(
    lengths, x_ref, marked_ref, mask_ref, weight_ref,
    qkv_ref, mix_ref, log_ref, hidden_ref,
):
    rows, width = x_ref.shape
    slots = lengths.shape[0]
    tall_slot = rows // slots
    start = replaced(marked_ref, mask_ref, x_ref)
    low = start.astype(BF16)
    qkv_ref[0] = (nn(low, block(weight_ref, 0)) * SCALE).astype(BF16)
    qkv_ref[1] = nn(low, block(weight_ref, 1)).astype(BF16)
    qkv_ref[2] = nn(low, block(weight_ref, 2)).astype(BF16)
    for slot in range(slots):
        here = slice(slot * tall_slot, (slot + 1) * tall_slot)
        bias = slot_bias(lengths[slot], tall_slot)
        for pair in range(HEADS // 2):
            at = lanes(pair)
            mixture, _, logs = pair_forward(
                qkv_ref[0, here, at], qkv_ref[1, here, at], qkv_ref[2, here, at], bias
            )
            mix_ref[here, at] = mixture.astype(BF16)
            for head in range(2):
                log_ref[here, 2 * pair + head : 2 * pair + head + 1] = logs[head]
    hidden_ref[...] = start + nn(mix_ref[...], block(weight_ref, 3))


def decoder_main(
    slot_source, slot_length, hidden_ref, memory_ref, cotangent_ref, weight_ref, norm_ref,
    output_ref, grads_ref, grad_memory_ref, grad_first_ref, norm_grads_ref,
    q_ref, kv_ref, mix_ref, parts_ref, pre_ref, active_ref, grad_mix_ref, grad_q_ref, grad_kv_ref,
):
    rows, width = hidden_ref.shape
    slots = slot_source.shape[0]
    groups, longest, _ = memory_ref.shape
    tall_slot = rows // slots
    unit, scale = norm_parts(hidden_ref[...])
    first = unit * norm_ref[0:1, :] + norm_ref[1:2, :]
    first_low = first.astype(BF16)
    q_ref[...] = (nn(first_low, block(weight_ref, 4)) * SCALE).astype(BF16)
    memory = memory_ref[...].reshape(groups * longest, width)
    kv_ref[0] = nn(memory, block(weight_ref, 5)).astype(BF16).reshape(groups, longest, width)
    kv_ref[1] = nn(memory, block(weight_ref, 6)).astype(BF16).reshape(groups, longest, width)
    for slot in range(slots):
        here = slice(slot * tall_slot, (slot + 1) * tall_slot)
        source = slot_source[slot]
        bias = slot_bias(slot_length[slot], longest)
        for pair in range(HEADS // 2):
            at = lanes(pair)
            mixture, parts, _ = pair_forward(q_ref[here, at], kv_ref[0, source, :, at], kv_ref[1, source, :, at], bias)
            mix_ref[here, at] = mixture.astype(BF16)
            for head in range(2):
                parts_ref[slot, 2 * pair + head] = parts[head]
    hidden = first + nn(mix_ref[...], block(weight_ref, 7))
    unit_two, scale_two = norm_parts(hidden)
    second = unit_two * norm_ref[2:3, :] + norm_ref[3:4, :]
    low = second.astype(BF16)
    hidden = second
    for j in range(4):
        at = slice(j * width, (j + 1) * width)
        pre = nn(low, block(weight_ref, 8 + j))
        pre_ref[:, at] = pre
        active_ref[:, at] = (0.5 * pre * (1.0 + gelu_tanh(pre))).astype(BF16)
    for j in range(4):
        hidden = hidden + nn(active_ref[:, j * width : (j + 1) * width], tall(weight_ref, j, 12))
    unit_three, scale_three = norm_parts(hidden)
    output_ref[...] = (unit_three * norm_ref[4:5, :] + norm_ref[5:6, :]).astype(BF16)
    grad, gain_three, bias_three = norm_back(
        cotangent_ref[...].astype(F32), unit_three, scale_three, norm_ref[4:5, :]
    )
    grad_low = grad.astype(BF16)
    turned = low.T
    for j in range(4):
        at = slice(j * width, (j + 1) * width)
        put_tall(grads_ref, j, 8, nn(active_ref[:, at].T, grad_low))
        _, slope = gelu_back(pre_ref[:, at])
        grad_inner = (nt(grad_low, tall(weight_ref, j, 12)) * slope).astype(BF16)
        put(grads_ref, 4 + j, nn(turned, grad_inner))
        grad = grad + nt(grad_inner, block(weight_ref, 8 + j))
    grad, gain_two, bias_two = norm_back(grad, unit_two, scale_two, norm_ref[2:3, :])
    grad_low = grad.astype(BF16)
    put(grads_ref, 3, nn(mix_ref[...].T, grad_low))
    grad_mix_ref[...] = nt(grad_low, block(weight_ref, 7)).astype(BF16)
    for slot in range(slots):
        here = slice(slot * tall_slot, (slot + 1) * tall_slot)
        source = slot_source[slot]
        for pair in range(HEADS // 2):
            at = lanes(pair)
            parts = [parts_ref[slot, 2 * pair + head] for head in range(2)]
            grad_q, grad_k, grad_v = pair_backward(
                q_ref[here, at], kv_ref[0, source, :, at], kv_ref[1, source, :, at], parts, grad_mix_ref[here, at]
            )
            grad_q_ref[here, at] = grad_q
            grad_kv_ref[0, source, :, at] = grad_k
            grad_kv_ref[1, source, :, at] = grad_v
    grad_k = grad_kv_ref[0].reshape(groups * longest, width)
    grad_v = grad_kv_ref[1].reshape(groups * longest, width)
    grad_memory_ref[...] = (
        (nt(grad_k, block(weight_ref, 5)) + nt(grad_v, block(weight_ref, 6)))
        .astype(BF16)
        .reshape(groups, longest, width)
    )
    put(grads_ref, 0, nn(first_low.T, grad_q_ref[...]))
    turned = memory.T
    put(grads_ref, 1, nn(turned, grad_k))
    put(grads_ref, 2, nn(turned, grad_v))
    grad_first_ref[...] = grad + nt(grad_q_ref[...], block(weight_ref, 4))
    for index, row in enumerate((gain_two, bias_two, gain_three, bias_three)):
        norm_grads_ref[index : index + 1, :] = row


def self_backward(
    lengths, x_ref, marked_ref, mask_ref, weight_ref, qkv_ref, mix_ref, log_ref, hidden_ref, grad_first_ref, norm_ref,
    grads_ref, grad_x_ref, small_ref, grad_mix_ref, grad_proj_ref,
):
    rows, width = x_ref.shape
    slots = lengths.shape[0]
    tall_slot = rows // slots
    unit, scale = norm_parts(hidden_ref[...])
    grad, gain, bias_row = norm_back(grad_first_ref[...], unit, scale, norm_ref[0:1, :])
    grad_low = grad.astype(BF16)
    put(grads_ref, 3, nn(mix_ref[...].T, grad_low))
    grad_mix_ref[...] = nt(grad_low, block(weight_ref, 3)).astype(BF16)
    for slot in range(slots):
        here = slice(slot * tall_slot, (slot + 1) * tall_slot)
        bias = slot_bias(lengths[slot], tall_slot)
        for pair in range(HEADS // 2):
            at = lanes(pair)
            queries, keys, values = [qkv_ref[i, here, at] for i in range(3)]
            logs = [log_ref[here, 2 * pair + head : 2 * pair + head + 1] for head in range(2)]
            parts = pair_weights(queries, keys, bias, logs)
            grads = pair_backward(queries, keys, values, parts, grad_mix_ref[here, at])
            for i in range(3):
                grad_proj_ref[i, here, at] = grads[i]
    turned = replaced(marked_ref, mask_ref, x_ref).astype(BF16).T
    for i in range(3):
        put(grads_ref, i, nn(turned, grad_proj_ref[i]))
        grad = grad + nt(grad_proj_ref[i], block(weight_ref, i))
    marked = marked_ref[...] == 1
    grad_x_ref[...] = jnp.where(marked, 0.0, grad)
    small_ref[0:1, :] = gain
    small_ref[1:2, :] = bias_row
    small_ref[2:3, :] = jnp.sum(jnp.where(marked, grad, 0.0), axis=0, keepdims=True)


def encoder_ffn_backward(
    piece_starts, piece_lengths, pieces_ref, hidden_one_ref, hidden_two_ref, weight_ref, norm_ref,
    grads_ref, grad_first_ref, small_ref,
):
    rows, width = hidden_one_ref.shape
    groups, longest, _ = pieces_ref.shape
    down = lax.broadcasted_iota(jnp.int32, (rows, longest), 0)
    across = lax.broadcasted_iota(jnp.int32, (rows, longest), 1)
    grad = jnp.zeros((rows, width), F32)
    for g in range(groups):
        chosen = (down - across == piece_starts[g]) & (across < piece_lengths[g])
        grad = grad + nn(jnp.where(chosen, 1.0, 0.0).astype(BF16), pieces_ref[g])
    unit, scale = norm_parts(hidden_two_ref[...])
    grad, gain, bias_row = norm_back(grad, unit, scale, norm_ref[2:3, :])
    grad_low = grad.astype(BF16)
    unit, _ = norm_parts(hidden_one_ref[...])
    low = (unit * norm_ref[0:1, :] + norm_ref[1:2, :]).astype(BF16)
    turned = low.T
    for j in range(4):
        active, slope = gelu_back(nn(low, block(weight_ref, 4 + j)))
        put_tall(grads_ref, j, 4, nn(active.astype(BF16).T, grad_low))
        grad_inner = (nt(grad_low, tall(weight_ref, j, 8)) * slope).astype(BF16)
        put(grads_ref, j, nn(turned, grad_inner))
        grad = grad + nt(grad_inner, block(weight_ref, 4 + j))
    grad_first_ref[...] = grad
    small_ref[0:1, :] = gain
    small_ref[1:2, :] = bias_row


def encoder_attention_backward(
    starts, x_ref, weight_ref, qkv_ref, mix_ref, log_ref, hidden_ref, grad_first_ref, norm_ref,
    small_one_ref, small_two_ref, small_three_ref,
    grads_ref, grad_x_ref, bias_ref, grad_mix_ref, grad_proj_ref,
):
    rows, width = x_ref.shape
    unit, scale = norm_parts(hidden_ref[...])
    grad, gain, bias_row = norm_back(grad_first_ref[...], unit, scale, norm_ref[0:1, :])
    grad_low = grad.astype(BF16)
    bias_ref[...] = segment_bias(starts, rows)
    put(grads_ref, 3, nn(mix_ref[...].T, grad_low))
    grad_mix_ref[...] = nt(grad_low, block(weight_ref, 3)).astype(BF16)
    for pair in range(HEADS // 2):
        at = lanes(pair)
        queries, keys, values = [qkv_ref[i, :, at] for i in range(3)]
        logs = [log_ref[:, 2 * pair + head : 2 * pair + head + 1] for head in range(2)]
        parts = pair_weights(queries, keys, bias_ref[...], logs)
        grads = pair_backward(queries, keys, values, parts, grad_mix_ref[:, at])
        for i in range(3):
            grad_proj_ref[i, :, at] = grads[i]
    turned = x_ref[...].T
    for i in range(3):
        put(grads_ref, i, nn(turned, grad_proj_ref[i]))
        grad = grad + nt(grad_proj_ref[i], block(weight_ref, i))
    grad_x_ref[...] = grad
    put_rows(
        grads_ref, 4, [gain, bias_row, small_three_ref[...], small_one_ref[0:2, :], small_two_ref[...], small_one_ref[2:3, :]]
    )


VMEM = pl.BlockSpec(memory_space=pltpu.VMEM)
SMEM = pl.BlockSpec(memory_space=pltpu.SMEM)


def run(kernel, scalars, arrays, outs, scratch=(), gflop=1.0):
    return pl.pallas_call(
        kernel,
        out_shape=[jax.ShapeDtypeStruct(shape, kind) for shape, kind in outs],
        in_specs=[SMEM] * len(scalars) + [VMEM] * len(arrays),
        out_specs=[VMEM] * len(outs),
        scratch_shapes=[pltpu.VMEM(shape, kind) for shape, kind in scratch],
        compiler_params=pltpu.CompilerParams(vmem_limit_bytes=56 << 20),
        cost_estimate=pl.CostEstimate(flops=int(gflop * 2e9), bytes_accessed=1 << 20, transcendentals=0),
    )(*scalars, *arrays)


def exchange(block, pairs):
    return lax.ppermute(block, AXES, pairs)


def pick(blocks, place):
    return lax.dynamic_index_in_dim(blocks, place, 0, keepdims=False)


def added(one, other):
    return (one.astype(F32) + other.astype(F32)).astype(BF16)


RING = (0, 1, 3, 2)


def sum_scatter(packs, count):
    me = lax.axis_index(AXES)
    core, low, high = me % 2, (me // 2) % 2, (me // 4) % 2
    rest = count // 8
    by_core = [pack.reshape((rest * 4, 2) + pack.shape[1:]) for pack in packs]
    sent, kept = [
        jnp.concatenate([lax.dynamic_index_in_dim(pack, side, 1, keepdims=False) for pack in by_core], axis=1)
        for side in (1 - core, core)
    ]
    tail = sent.shape[1:]
    kept = added(kept, exchange(sent, [(i, i ^ 1) for i in range(count)]))
    quads = kept.reshape((rest, 4) + tail)

    def two(first, second):
        parts = [lax.dynamic_index_in_dim(quads, place, 1, keepdims=True) for place in (first, second)]
        return jnp.concatenate(parts, axis=1)

    other_high, other_low = 1 - high, 1 - low
    sent = two(
        jnp.where(core == 0, 2 * other_high, other_low),
        jnp.where(core == 0, 2 * other_high + 1, other_low + 2),
    )
    kept = two(jnp.where(core == 0, 2 * high, low), jnp.where(core == 0, 2 * high + 1, low + 2))
    kept = added(kept, exchange(sent, [(i, i ^ (2 if i % 2 else 4)) for i in range(count)]))
    mine = jnp.where(core == 0, low, high)
    sent = lax.dynamic_index_in_dim(kept, 1 - mine, 1, keepdims=False)
    kept = lax.dynamic_index_in_dim(kept, mine, 1, keepdims=False)
    kept = added(kept, exchange(sent, [(i, i ^ (4 if i % 2 else 2)) for i in range(count)]))
    stride = 8
    while rest > 4:
        bit = (me // stride) % 2
        halves = kept.reshape((rest // 2, 2) + tail)
        sent = lax.dynamic_index_in_dim(halves, 1 - bit, 1, keepdims=False)
        kept = lax.dynamic_index_in_dim(halves, bit, 1, keepdims=False)
        kept = added(kept, exchange(sent, [(i, i ^ stride) for i in range(count)]))
        rest, stride = rest // 2, stride * 2
    order = RING if rest == 4 else tuple(range(rest))
    place_of = jnp.asarray([order.index(z) for z in range(rest)], jnp.int32)
    ring = jnp.asarray(order, jnp.int32)
    here = place_of[me // stride]
    onward = [
        (i, order[(order.index(i // stride) + 1) % rest] * stride + i % stride) for i in range(count)
    ]
    moving = pick(kept, ring[(here - 1) % rest]) if rest > 1 else kept[0]
    for step in range(rest - 1):
        arrived = exchange(moving, onward)
        own = pick(kept, ring[(here - 2 - step) % rest])
        moving = arrived.astype(F32) + own.astype(F32)
        if step < rest - 2:
            moving = moving.astype(BF16)
    return moving.astype(F32)


def on_device(
    enc_input,
    dec_input,
    target_mask,
    src_lengths,
    tgt_lengths,
    memory_route,
    enc_qkv,
    enc_out,
    enc_ffn_in,
    enc_ffn_out,
    enc_norms,
    dec_qkv,
    dec_out,
    cross_qkv,
    cross_out,
    dec_ffn_in,
    dec_ffn_out,
    dec_norms,
    mask_vector,
    out_cotangent,
):
    dp_count, groups = lax.axis_size("dp"), lax.axis_size("fsdp")
    count = dp_count * groups
    rows, width = enc_input.shape
    slots = src_lengths.shape[1]
    longest = rows // 2
    slot_rows = rows // slots
    part = enc_out.shape[0]
    inner = enc_ffn_in.shape[1]
    pieces_in = inner // width

    def square(weight):
        return weight.reshape(-1, width)

    def wide(weight):
        return weight.reshape(part, pieces_in, width).transpose(1, 0, 2).reshape(-1, width)

    small = jnp.concatenate(
        [
            enc_norms.reshape(-1),
            dec_norms.reshape(-1),
            mask_vector.reshape(-1),
            src_lengths[0].astype(BF16),
            memory_route[0].astype(BF16),
        ]
    )
    small_used = small.shape[0]
    small = jnp.pad(small, (0, part * width - small_used)).reshape(part, width)
    enc_pack = jnp.concatenate([square(enc_qkv), enc_out, wide(enc_ffn_in), enc_ffn_out, small])
    dec_pack = jnp.concatenate(
        [square(dec_qkv), dec_out, square(cross_qkv), cross_out, wide(dec_ffn_in), dec_ffn_out]
    )
    enc_all = lax.all_gather(enc_pack, AXES, axis=0, tiled=False)
    dec_all = lax.all_gather(dec_pack, AXES, axis=0, tiled=False)

    small_all = enc_all[:, (4 + 2 * pieces_in) * part :].reshape(count, part * width)[:, :small_used]
    at = 0

    def take(length):
        nonlocal at
        at += length
        return small_all[:, at - length : at]

    def table(layers):
        picked = take(layers * 2 * part).reshape(count, layers * 2, part)
        return picked.transpose(1, 0, 2).reshape(layers * 2, width).astype(F32)

    e_norm = table(enc_norms.shape[0])
    d_norm = table(dec_norms.shape[0])
    mask_full = take(part).reshape(1, width)
    my_dp, my_group = lax.axis_index("dp"), lax.axis_index("fsdp")
    lengths_near = pick(take(slots).astype(jnp.int32).reshape(dp_count, groups, slots), my_dp)
    route_near = pick(take(slots).astype(jnp.int32).reshape(dp_count, groups, slots), my_dp)

    kernel_part = max(part, 16)
    kernel_count = width // kernel_part
    joined = kernel_part // part

    def coarse(pack):
        if joined == 1:
            return pack
        picked = pack.reshape(kernel_count, joined, -1, part, width).transpose(0, 2, 1, 3, 4)
        return picked.reshape(kernel_count, -1, width)

    def coarse_tall(pack):
        return pack.reshape(kernel_count, -1, width)

    def fine(pack):
        if joined == 1:
            return pack
        picked = pack.reshape(kernel_count, -1, joined, part, width).transpose(0, 2, 1, 3, 4)
        return picked.reshape(count, -1, width)

    def fine_tall(pack):
        return pack.reshape(count, -1, width)

    if joined > 1:
        first, last = (4 + pieces_in) * part, (4 + 2 * pieces_in) * part
        enc_all = jnp.concatenate([coarse(enc_all[:, :first]), coarse_tall(enc_all[:, first:last])], axis=1)
        first = (8 + pieces_in) * part
        dec_all = jnp.concatenate([coarse(dec_all[:, :first]), coarse_tall(dec_all[:, first:])], axis=1)

    src_len = src_lengths[0]
    starts = jnp.cumsum(src_len) - src_len
    dest_dev = memory_route[0] // slots
    ids = jnp.arange(groups, dtype=jnp.int32)
    sent_to = dest_dev[None, :] == ids[:, None]
    piece_starts = jnp.sum(jnp.where(sent_to, starts[None, :], 0), axis=1)
    piece_lengths = jnp.sum(jnp.where(sent_to, src_len[None, :], 0), axis=1)
    to_me = route_near // slots == my_group
    source_slot = jnp.sum(jnp.where(to_me, route_near % slots, 0), axis=1)
    source_len = jnp.sum(jnp.where(to_me, lengths_near, 0), axis=1)
    chosen = source_slot[None, :] == jnp.arange(slots, dtype=jnp.int32)[:, None]
    slot_source = jnp.sum(jnp.where(chosen, ids[None, :], 0), axis=1)
    slot_length = jnp.sum(jnp.where(chosen, source_len[None, :], 0), axis=1)

    plane, three = (rows, width), (3, rows, width)
    memory_shape = (groups, longest, width)
    logs_shape = (rows, HEADS)

    def pack_of(pieces):
        return (kernel_count, pieces * kernel_part, width)

    pieces, e_qkv, e_mix, e_logs, e_hidden_one, e_hidden_two = run(
        encoder_forward,
        (starts, piece_starts),
        (enc_input, enc_all, e_norm),
        ((memory_shape, BF16), (three, BF16), (plane, BF16), (logs_shape, F32), (plane, F32), (plane, F32)),
        ((((rows, rows), F32)), ((rows, inner), BF16)),
        gflop=2.5,
    )
    memory_in = lax.all_to_all(pieces, "fsdp", split_axis=0, concat_axis=0, tiled=True)
    tgt_len = tgt_lengths[0]
    marked = target_mask[:, None]
    d_qkv, d_mix, d_logs, d_hidden = run(
        self_forward,
        (tgt_len,),
        (dec_input, marked, mask_full, dec_all),
        ((three, BF16), (plane, BF16), (logs_shape, F32), (plane, F32)),
        gflop=0.7,
    )
    dec_output, first_grads, grad_memory, grad_first, small_two = run(
        decoder_main,
        (slot_source, slot_length),
        (d_hidden, memory_in, out_cotangent, dec_all, d_norm),
        (
            (plane, BF16),
            (pack_of(4 + 2 * pieces_in), BF16),
            (memory_shape, BF16),
            (plane, F32),
            ((4, width), F32),
        ),
        (
            (plane, BF16),
            ((2,) + memory_shape, BF16),
            (plane, BF16),
            ((slots, HEADS, slot_rows, longest), F32),
            ((rows, inner), F32),
            ((rows, inner), BF16),
            (plane, BF16),
            (plane, BF16),
            ((2,) + memory_shape, BF16),
        ),
        gflop=8.0,
    )
    returned = lax.all_to_all(grad_memory, "fsdp", split_axis=0, concat_axis=0, tiled=True)

    def to_sum(pack, squares, tails):
        if joined == 1:
            return [pack]
        first = squares * kernel_part
        return [fine(pack[:, :first]), fine_tall(pack[:, first:])][: 1 + tails]

    first_sum = sum_scatter(to_sum(first_grads, 4 + pieces_in, 1), count)
    self_grads, dec_input_grad, small_one = run(
        self_backward,
        (tgt_len,),
        (dec_input, marked, mask_full, dec_all, d_qkv, d_mix, d_logs, d_hidden, grad_first, d_norm),
        ((pack_of(4), BF16), (plane, F32), ((3, width), F32)),
        ((plane, BF16), (three, BF16)),
        gflop=1.5,
    )
    ffn_grads, grad_enc_first, small_three = run(
        encoder_ffn_backward,
        (piece_starts, piece_lengths),
        (returned, e_hidden_one, e_hidden_two, enc_all, e_norm),
        ((pack_of(2 * pieces_in), BF16), (plane, F32), ((2, width), F32)),
        gflop=3.0,
    )
    second_sum = sum_scatter(to_sum(self_grads, 4, 0) + to_sum(ffn_grads, pieces_in, 1), count)
    attention_grads, enc_input_grad = run(
        encoder_attention_backward,
        (starts,),
        (
            enc_input, enc_all, e_qkv, e_mix, e_logs, e_hidden_one, grad_enc_first, e_norm,
            small_one, small_two, small_three,
        ),
        ((pack_of(5), BF16), (plane, F32)),
        (((rows, rows), F32), (plane, BF16), (three, BF16)),
        gflop=3.5,
    )
    third_sum = sum_scatter(to_sum(attention_grads, 4, 0), count)

    def piece(summed, first, pieces=1):
        return summed[first * part : (first + pieces) * part]

    def wide_piece(summed, first):
        picked = piece(summed, first, pieces_in).reshape(pieces_in, part, width)
        return picked.transpose(1, 0, 2).reshape(part, inner)

    if joined == 1:
        small_sum = piece(third_sum, 4)
    else:
        small_sum = lax.psum(attention_grads[0, 4 * kernel_part :].astype(F32), AXES)
    small_sum = lax.dynamic_slice_in_dim(small_sum[:11], lax.axis_index(AXES) * part, part, 1)
    return (
        dec_output,
        enc_input_grad,
        dec_input_grad,
        piece(third_sum, 0, 3).reshape(3, part, width),
        piece(third_sum, 3),
        wide_piece(second_sum, 4),
        piece(second_sum, 4 + pieces_in, pieces_in),
        small_sum[:4].reshape(2, 2, part),
        piece(second_sum, 0, 3).reshape(3, part, width),
        piece(second_sum, 3),
        piece(first_sum, 0, 3).reshape(3, part, width),
        piece(first_sum, 3),
        wide_piece(first_sum, 4),
        piece(first_sum, 4 + pieces_in, pieces_in),
        small_sum[4:10].reshape(3, 2, part),
        small_sum[10],
    )


def solution(mesh):
    rows = P(AXES, None)
    flat = P(AXES)
    cube = P(None, AXES, None)
    norm = P(None, None, AXES)
    in_specs = (
        (rows, rows, flat, rows, rows, rows)
        + (cube, rows, rows, rows, norm)
        + (cube, rows, cube, rows, rows, rows, norm, flat)
        + (rows,)
    )
    out_specs = (
        (rows, rows, rows)
        + (cube, rows, rows, rows, norm)
        + (cube, rows, cube, rows, rows, rows, norm, flat)
    )
    return jax.shard_map(on_device, mesh=mesh, in_specs=in_specs, out_specs=out_specs, check_vma=False)
```

```python
import math

import jax
import jax.numpy as jnp
import numpy as np
from jax import lax
from jax.experimental import pallas as pl
from jax.experimental.pallas import tpu as pltpu
from jax.sharding import PartitionSpec as P

HEADS = 8
HEAD_DIM = 64
SCALE = 1.0 / math.sqrt(HEAD_DIM)
AXES = ("dp", "fsdp")
F32 = jnp.float32
BF16 = jnp.bfloat16


MASKED = -1e30
GELU_C = math.sqrt(2.0 / math.pi)
GELU_A = 0.044715


def nn(left, right):
    return jnp.dot(left, right, preferred_element_type=F32)


def nt(left, right):
    return lax.dot_general(left, right, (((1,), (1,)), ((), ())), preferred_element_type=F32)


def norm_parts(hidden):
    center = hidden - jnp.mean(hidden, axis=-1, keepdims=True)
    scale = lax.rsqrt(jnp.mean(center * center, axis=-1, keepdims=True) + 1e-05)
    return center * scale, scale


def norm_back(grad, unit, scale, gain):
    inner = grad * gain
    mean_one = jnp.mean(inner, axis=-1, keepdims=True)
    mean_two = jnp.mean(inner * unit, axis=-1, keepdims=True)
    return (
        scale * (inner - mean_one - unit * mean_two),
        jnp.sum(grad * unit, axis=0, keepdims=True),
        jnp.sum(grad, axis=0, keepdims=True),
    )


def gelu_tanh(pre):
    return jnp.tanh(GELU_C * (pre + GELU_A * (pre * pre * pre)))


def gelu_back(pre):
    tanh = gelu_tanh(pre)
    slope = GELU_C * (1.0 + 3.0 * GELU_A * (pre * pre))
    return 0.5 * pre * (1.0 + tanh), 0.5 * (1.0 + tanh) + 0.5 * pre * (1.0 - tanh * tanh) * slope


def block(ref, first):
    width = ref.shape[2]
    part = width // ref.shape[0]
    return ref[:, first * part : (first + 1) * part, :].reshape(width, width)


def tall(ref, index, first):
    count, _, width = ref.shape
    part = width // count
    some = count // 4
    picked = ref[index * some : (index + 1) * some, first * part : (first + 4) * part, :]
    return picked.reshape(width, width)


CORNERS = [(x, y, side) for x in range(2) for y in range(2) for side in range(2)]


def place_of(x, y, side):
    return 8 * x + 4 * y if side == 0 else 8 * y + 4 * x


def put(ref, core, first, grad):
    width = grad.shape[1]
    part = width // 32
    cut = grad.astype(BF16).reshape(4, 2, 2, 2, part, width)
    rows = slice(first * part, (first + 1) * part)
    for x, y, side in CORNERS:
        half = core if side == 0 else 1 - core
        place = place_of(x, y, side)
        ref[half, place : place + 4, rows, :] = cut[:, x, y, side]


def put_tall(ref, core, index, first, grad):
    width = grad.shape[1]
    part = width // 32
    cut = grad.astype(BF16).reshape(2, 2, 2, 4 * part, width)
    rows = slice(first * part, (first + 4) * part)
    for x, y, side in CORNERS:
        half = core if side == 0 else 1 - core
        ref[half, place_of(x, y, side) + index, rows, :] = cut[x, y, side]


def put_rows(ref, first, rows_of):
    halves, count, _, width = ref.shape
    part = width // (halves * count)
    used = sum(row.shape[0] for row in rows_of)
    rows = jnp.concatenate(rows_of + [jnp.zeros((part - used, width), F32)], axis=0)
    ref[:, :, first * part : (first + 1) * part, :] = jnp.broadcast_to(
        rows.astype(BF16)[None, None], (halves, count, part, width)
    )


def bring_pieces(place, refs, target, sems, first=0):
    part = target.shape[2] // target.shape[0]
    rows = pl.ds(first * part, target.shape[1])
    copies = []
    for array, ref in enumerate(refs):
        for index in range(8):
            number = array * 8 + index
            copies.append(pltpu.make_async_copy(ref.at[index, rows], target.at[place[number]], sems.at[number]))
    for copy in copies:
        copy.start()
    return copies


def bring_rows(ref, first, count, target, sem):
    copy = pltpu.make_async_copy(ref.at[:, pl.ds(first, count), :], target, sem)
    copy.start()
    return copy


def send_halves(halves_ref, kept_ref, sent_ref, sems):
    copies = [
        pltpu.make_async_copy(halves_ref.at[half], ref, sems.at[half])
        for half, ref in enumerate((kept_ref, sent_ref))
    ]
    for copy in copies:
        copy.start()
    return copies


def wait_all(copies):
    for copy in copies:
        copy.wait()


PAIR = 2 * HEAD_DIM


def twice(pair_rows):
    lane = lax.broadcasted_iota(jnp.int32, pair_rows.shape, 1)
    zero = jnp.zeros_like(pair_rows)
    return jnp.concatenate(
        [jnp.where(lane < HEAD_DIM, pair_rows, zero), jnp.where(lane < HEAD_DIM, zero, pair_rows)], axis=0
    )


def pair_forward(queries, keys, values, bias):
    count = keys.shape[0]
    scores = nt(queries, twice(keys))
    parts, logs = [], []
    for head in range(2):
        masked = scores[:, head * count : (head + 1) * count] + bias
        top = jnp.max(masked, axis=-1, keepdims=True)
        raised = jnp.exp(masked - top)
        total = jnp.sum(raised, axis=-1, keepdims=True)
        parts.append(raised * (1.0 / total))
        logs.append(top + jnp.log(total))
    low = jnp.concatenate([part.astype(BF16) for part in parts], axis=1)
    return nn(low, twice(values)), parts, logs


def pair_weights(queries, keys, bias, logs):
    count = keys.shape[0]
    scores = nt(queries, twice(keys))
    return [
        jnp.exp(scores[:, head * count : (head + 1) * count] + bias - logs[head]) for head in range(2)
    ]


def unmix(turned, count):
    both = jnp.concatenate(
        [turned[:HEAD_DIM, :count], turned[HEAD_DIM:, count:]], axis=0
    )
    return both.T


def pair_backward(queries, keys, values, parts, grad_out):
    count = keys.shape[0]
    grad_weights = nt(grad_out, twice(values))
    grad_scores = []
    for head in range(2):
        grad_part = grad_weights[:, head * count : (head + 1) * count]
        delta = jnp.sum(parts[head] * grad_part, axis=-1, keepdims=True)
        grad_scores.append((parts[head] * (grad_part - delta)).astype(BF16))
    grad_scores = jnp.concatenate(grad_scores, axis=1)
    weights = jnp.concatenate([part.astype(BF16) for part in parts], axis=1)
    grad_query = nn(grad_scores, twice(keys)) * SCALE
    grad_key = unmix(nn(queries.T, grad_scores), count)
    grad_value = unmix(nn(grad_out.T, weights), count)
    return grad_query.astype(BF16), grad_key.astype(BF16), grad_value.astype(BF16)


def sentence_starts(lengths):
    starts = [0]
    for sentence in range(lengths.shape[1] - 1):
        starts.append(starts[-1] + lengths[0, sentence])
    return starts


def piece_places(lengths, route, slots):
    starts = sentence_starts(lengths)
    first, length = [], []
    for device in range(route.shape[1]):
        here, count = jnp.int32(0), jnp.int32(0)
        for sentence in range(route.shape[1]):
            goes = route[0, sentence] // slots == device
            here = here + jnp.where(goes, starts[sentence], 0)
            count = count + jnp.where(goes, lengths[0, sentence], 0)
        first.append(here)
        length.append(count)
    return first, length


def segment_bias(lengths, rows):
    down = lax.broadcasted_iota(jnp.int32, (rows, 1), 0)
    across = lax.broadcasted_iota(jnp.int32, (1, rows), 1)
    segment_down = jnp.zeros_like(down)
    segment_across = jnp.zeros_like(across)
    starts = sentence_starts(lengths)
    for sentence in range(1, len(starts)):
        segment_down += (down >= starts[sentence]).astype(jnp.int32)
        segment_across += (across >= starts[sentence]).astype(jnp.int32)
    return jnp.where(segment_down == segment_across, 0.0, MASKED)


def lanes(pair):
    return slice(pair * PAIR, (pair + 1) * PAIR)


def pack_weights(
    me, src_ref, route_ref, mask_ref, e_qkv_ref, e_out_ref, e_in_ref, e_outff_ref, e_norm_ref,
    d_qkv_ref, d_out_ref, c_qkv_ref, c_out_ref, d_in_ref, d_outff_ref, d_norm_ref,
    attention_ref, ffn_ref, decoder_ref,
):
    part, width = e_out_ref.shape
    lane = lax.broadcasted_iota(jnp.int32, (part, width), 1)
    row = lax.broadcasted_iota(jnp.int32, (part, width), 0)
    spread = jnp.where(lane - row == me[0] * part, 1.0, 0.0).astype(BF16)
    ints = [nn(ref[...].astype(F32).astype(BF16), spread[4 * i : 4 * i + 4]) for i, ref in enumerate((src_ref, route_ref))]
    rows = [nn(e_norm_ref[i], spread) for i in range(2)] + [nn(d_norm_ref[i], spread) for i in range(3)]
    rows = rows + [nn(mask_ref[...], spread), ints[0] + ints[1]]
    used = sum(r.shape[0] for r in rows)
    rows = jnp.concatenate(rows + [jnp.zeros((part - used, width), F32)], axis=0)

    def fill(ref, first, weight):
        ref[first * part : first * part + weight.shape[0], :] = weight

    for i in range(3):
        fill(attention_ref, i, e_qkv_ref[i])
        fill(decoder_ref, i, d_qkv_ref[i])
        fill(decoder_ref, 4 + i, c_qkv_ref[i])
    fill(attention_ref, 3, e_out_ref[...])
    fill(attention_ref, 4, rows.astype(BF16))
    fill(decoder_ref, 3, d_out_ref[...])
    fill(decoder_ref, 7, c_out_ref[...])
    for j in range(4):
        fill(ffn_ref, j, e_in_ref[:, j * width : (j + 1) * width])
        fill(decoder_ref, 8 + j, d_in_ref[:, j * width : (j + 1) * width])
    fill(ffn_ref, 4, e_outff_ref[...])
    fill(decoder_ref, 12, d_outff_ref[...])


def encoder_attention(
    place, lengths, x_ref, part_a, part_b, part_c, part_d,
    qkv_ref, mix_ref, log_ref, hidden_ref, table_ref, bias_ref, weight_ref, sems,
):
    rows, width = x_ref.shape
    copies = bring_pieces(place, (part_a, part_b, part_c, part_d), weight_ref, sems)
    rows_in = x_ref[...]
    bias_ref[...] = segment_bias(lengths, rows)
    wait_all(copies)
    part = width // weight_ref.shape[0]
    table_ref[...] = jnp.sum(weight_ref[:, 4 * part : 5 * part, :].astype(F32), axis=0)
    qkv_ref[0] = (nn(rows_in, block(weight_ref, 0)) * SCALE).astype(BF16)
    qkv_ref[1] = nn(rows_in, block(weight_ref, 1)).astype(BF16)
    qkv_ref[2] = nn(rows_in, block(weight_ref, 2)).astype(BF16)
    for pair in range(HEADS // 2):
        at = lanes(pair)
        mixture, _, logs = pair_forward(qkv_ref[0, :, at], qkv_ref[1, :, at], qkv_ref[2, :, at], bias_ref[...])
        mix_ref[:, at] = mixture.astype(BF16)
        for head in range(2):
            log_ref[:, 2 * pair + head : 2 * pair + head + 1] = logs[head]
    hidden_ref[...] = rows_in.astype(F32) + nn(mix_ref[...], block(weight_ref, 3))


def encoder_ffn(
    place, lengths, route, hidden_one_ref, table_ref, part_a, part_b, part_c, part_d,
    pieces_ref, hidden_two_ref, active_out_ref, slope_out_ref, active_ref, slope_ref, weight_ref, sems,
):
    rows, width = hidden_one_ref.shape
    groups, longest, _ = pieces_ref.shape
    copies = bring_pieces(place, (part_a, part_b, part_c, part_d), weight_ref, sems)
    unit, _ = norm_parts(hidden_one_ref[...])
    first = unit * table_ref[0:1, :] + table_ref[1:2, :]
    low = first.astype(BF16)
    wait_all(copies)
    for j in range(4):
        active, slope = gelu_back(nn(low, block(weight_ref, j)))
        active_ref[j] = active.astype(BF16)
        slope_ref[j] = slope.astype(BF16)
    copies = [
        pltpu.make_async_copy(active_ref, active_out_ref, sems.at[32]),
        pltpu.make_async_copy(slope_ref, slope_out_ref, sems.at[33]),
    ]
    for copy in copies:
        copy.start()
    hidden = first
    for j in range(4):
        hidden = hidden + nn(active_ref[j], tall(weight_ref, j, 4))
    hidden_two_ref[...] = hidden
    unit, _ = norm_parts(hidden)
    memory = (unit * table_ref[2:3, :] + table_ref[3:4, :]).astype(BF16)
    down = lax.broadcasted_iota(jnp.int32, (longest, rows), 0)
    across = lax.broadcasted_iota(jnp.int32, (longest, rows), 1)
    starts, _ = piece_places(lengths, route, lengths.shape[1])
    for g in range(groups):
        chosen = jnp.where(across - down == starts[g], 1.0, 0.0).astype(BF16)
        pieces_ref[g] = nn(chosen, memory).astype(BF16)
    wait_all(copies)


def replaced(marked_ref, table_ref, rows_ref):
    marked = marked_ref[...] == 1
    return jnp.where(marked, table_ref[10:11, :], rows_ref[...].astype(F32))


def slot_bias(length, count):
    across = lax.broadcasted_iota(jnp.int32, (1, count), 1)
    return jnp.where(across < length, 0.0, MASKED)


def self_forward(
    lengths, x_ref, marked_ref, table_ref, gathered_ref,
    qkv_ref, mix_ref, log_ref, hidden_ref, weight_ref, sems,
):
    rows, width = x_ref.shape
    slots = lengths.shape[1]
    tall_slot = rows // slots
    copies = [bring_rows(gathered_ref, 0, weight_ref.shape[1], weight_ref, sems.at[0])]
    start = replaced(marked_ref, table_ref, x_ref)
    low = start.astype(BF16)
    wait_all(copies)
    qkv_ref[0] = (nn(low, block(weight_ref, 0)) * SCALE).astype(BF16)
    qkv_ref[1] = nn(low, block(weight_ref, 1)).astype(BF16)
    qkv_ref[2] = nn(low, block(weight_ref, 2)).astype(BF16)
    for slot in range(slots):
        here = slice(slot * tall_slot, (slot + 1) * tall_slot)
        bias = slot_bias(lengths[0, slot], tall_slot)
        for pair in range(HEADS // 2):
            at = lanes(pair)
            mixture, _, logs = pair_forward(
                qkv_ref[0, here, at], qkv_ref[1, here, at], qkv_ref[2, here, at], bias
            )
            mix_ref[here, at] = mixture.astype(BF16)
            for head in range(2):
                log_ref[here, 2 * pair + head : 2 * pair + head + 1] = logs[head]
    hidden_ref[...] = start + nn(mix_ref[...], block(weight_ref, 3))


def decoder_upper(
    core, slot_source, slot_length, hidden_ref, memory_ref, cotangent_ref, table_ref, gathered_ref,
    output_ref, kept_ref, sent_ref, parts_out_ref, q_ref, kv_ref, mix_ref, grad_ref, small_ref,
    parts_ref, slope_ref, active_ref, weight_ref, ffn_ref, halves_ref, sems,
):
    rows, width = hidden_ref.shape
    slots = slot_source.shape[0]
    groups, longest, _ = memory_ref.shape
    tall_slot = rows // slots
    part_rows = weight_ref.shape[1]
    cross_copy = bring_rows(gathered_ref, part_rows, part_rows, weight_ref, sems.at[0])
    ffn_copy = bring_rows(gathered_ref, 2 * part_rows, 2 * part_rows, ffn_ref, sems.at[1])
    unit, _ = norm_parts(hidden_ref[...])
    first = unit * table_ref[4:5, :] + table_ref[5:6, :]
    first_low = first.astype(BF16)
    memory = memory_ref[...].reshape(groups * longest, width)
    cross_copy.wait()
    q_ref[...] = (nn(first_low, block(weight_ref, 0)) * SCALE).astype(BF16)
    kv_ref[0] = nn(memory, block(weight_ref, 1)).astype(BF16).reshape(groups, longest, width)
    kv_ref[1] = nn(memory, block(weight_ref, 2)).astype(BF16).reshape(groups, longest, width)
    for slot in range(slots):
        here = slice(slot * tall_slot, (slot + 1) * tall_slot)
        source = slot_source[slot]
        bias = slot_bias(slot_length[slot], longest)
        for pair in range(HEADS // 2):
            at = lanes(pair)
            mixture, parts, _ = pair_forward(q_ref[here, at], kv_ref[0, source, :, at], kv_ref[1, source, :, at], bias)
            mix_ref[here, at] = mixture.astype(BF16)
            for head in range(2):
                parts_ref[slot, 2 * pair + head] = parts[head]
    parts_copy = pltpu.make_async_copy(parts_ref, parts_out_ref, sems.at[2])
    parts_copy.start()
    hidden = first + nn(mix_ref[...], block(weight_ref, 3))
    unit_two, scale_two = norm_parts(hidden)
    second = unit_two * table_ref[6:7, :] + table_ref[7:8, :]
    low = second.astype(BF16)
    hidden = second
    ffn_copy.wait()
    for j in range(4):
        active, slope = gelu_back(nn(low, block(ffn_ref, j)))
        slope_ref[j] = slope
        active_ref[j] = active.astype(BF16)
    for j in range(4):
        hidden = hidden + nn(active_ref[j], tall(ffn_ref, j, 4))
    unit_three, scale_three = norm_parts(hidden)
    output_ref[...] = (unit_three * table_ref[8:9, :] + table_ref[9:10, :]).astype(BF16)
    grad, gain_three, bias_three = norm_back(
        cotangent_ref[...].astype(F32), unit_three, scale_three, table_ref[8:9, :]
    )
    grad_low = grad.astype(BF16)
    turned = low.T
    for j in range(4):
        put_tall(halves_ref, core[0], j, 4, nn(active_ref[j].T, grad_low))
        grad_inner = (nt(grad_low, tall(ffn_ref, j, 4)) * slope_ref[j]).astype(BF16)
        put(halves_ref, core[0], j, nn(turned, grad_inner))
        grad = grad + nt(grad_inner, block(ffn_ref, j))
    copies = send_halves(halves_ref, kept_ref, sent_ref, sems.at[pl.ds(3, 2)])
    grad, gain_two, bias_two = norm_back(grad, unit_two, scale_two, table_ref[6:7, :])
    grad_ref[...] = grad
    for index, row in enumerate((gain_two, bias_two, gain_three, bias_three)):
        small_ref[index : index + 1, :] = row
    wait_all([parts_copy] + copies)


def cross_backward(
    core, slot_source, hidden_ref, memory_ref, table_ref, q_ref, kv_ref, mix_ref, grad_second_ref, gathered_ref, parts_in_ref,
    kept_ref, sent_ref, grad_memory_ref, grad_first_ref,
    parts_ref, grad_mix_ref, grad_q_ref, grad_kv_ref, weight_ref, halves_ref, sems,
):
    rows, width = hidden_ref.shape
    slots = slot_source.shape[0]
    groups, longest, _ = memory_ref.shape
    tall_slot = rows // slots
    part_rows = weight_ref.shape[1]
    cross_copy = bring_rows(gathered_ref, part_rows, part_rows, weight_ref, sems.at[0])
    parts_copy = pltpu.make_async_copy(parts_in_ref, parts_ref, sems.at[1])
    parts_copy.start()
    grad = grad_second_ref[...]
    grad_low = grad.astype(BF16)
    put(halves_ref, core[0], 3, nn(mix_ref[...].T, grad_low))
    cross_copy.wait()
    grad_mix_ref[...] = nt(grad_low, block(weight_ref, 3)).astype(BF16)
    parts_copy.wait()
    for slot in range(slots):
        here = slice(slot * tall_slot, (slot + 1) * tall_slot)
        source = slot_source[slot]
        for pair in range(HEADS // 2):
            at = lanes(pair)
            parts = [parts_ref[slot, 2 * pair + head] for head in range(2)]
            grad_q, grad_k, grad_v = pair_backward(
                q_ref[here, at], kv_ref[0, source, :, at], kv_ref[1, source, :, at], parts, grad_mix_ref[here, at]
            )
            grad_q_ref[here, at] = grad_q
            grad_kv_ref[0, source, :, at] = grad_k
            grad_kv_ref[1, source, :, at] = grad_v
    grad_k = grad_kv_ref[0].reshape(groups * longest, width)
    grad_v = grad_kv_ref[1].reshape(groups * longest, width)
    grad_memory_ref[...] = (
        (nt(grad_k, block(weight_ref, 1)) + nt(grad_v, block(weight_ref, 2)))
        .astype(BF16)
        .reshape(groups, longest, width)
    )
    unit, _ = norm_parts(hidden_ref[...])
    first_low = (unit * table_ref[4:5, :] + table_ref[5:6, :]).astype(BF16)
    put(halves_ref, core[0], 0, nn(first_low.T, grad_q_ref[...]))
    turned = memory_ref[...].reshape(groups * longest, width).T
    put(halves_ref, core[0], 1, nn(turned, grad_k))
    put(halves_ref, core[0], 2, nn(turned, grad_v))
    copies = send_halves(halves_ref, kept_ref, sent_ref, sems.at[pl.ds(2, 2)])
    grad_first_ref[...] = grad + nt(grad_q_ref[...], block(weight_ref, 0))
    wait_all(copies)


def self_backward(
    core, lengths, x_ref, marked_ref, table_ref, qkv_ref, mix_ref, log_ref, hidden_ref, grad_first_ref,
    gathered_ref, kept_ref, sent_ref, grad_x_ref, small_ref, grad_mix_ref, grad_proj_ref, weight_ref, halves_ref, sems,
):
    rows, width = x_ref.shape
    slots = lengths.shape[1]
    tall_slot = rows // slots
    weight_copies = [bring_rows(gathered_ref, 0, weight_ref.shape[1], weight_ref, sems.at[2])]
    unit, scale = norm_parts(hidden_ref[...])
    grad, gain, bias_row = norm_back(grad_first_ref[...], unit, scale, table_ref[4:5, :])
    grad_low = grad.astype(BF16)
    put(halves_ref, core[0], 3, nn(mix_ref[...].T, grad_low))
    wait_all(weight_copies)
    grad_mix_ref[...] = nt(grad_low, block(weight_ref, 3)).astype(BF16)
    for slot in range(slots):
        here = slice(slot * tall_slot, (slot + 1) * tall_slot)
        bias = slot_bias(lengths[0, slot], tall_slot)
        for pair in range(HEADS // 2):
            at = lanes(pair)
            queries, keys, values = [qkv_ref[i, here, at] for i in range(3)]
            logs = [log_ref[here, 2 * pair + head : 2 * pair + head + 1] for head in range(2)]
            parts = pair_weights(queries, keys, bias, logs)
            grads = pair_backward(queries, keys, values, parts, grad_mix_ref[here, at])
            for i in range(3):
                grad_proj_ref[i, here, at] = grads[i]
    turned = replaced(marked_ref, table_ref, x_ref).astype(BF16).T
    for i in range(3):
        put(halves_ref, core[0], i, nn(turned, grad_proj_ref[i]))
    copies = send_halves(halves_ref, kept_ref, sent_ref, sems.at[pl.ds(0, 2)])
    for i in range(3):
        grad = grad + nt(grad_proj_ref[i], block(weight_ref, i))
    marked = marked_ref[...] == 1
    grad_x_ref[...] = jnp.where(marked, 0.0, grad)
    small_ref[0:1, :] = gain
    small_ref[1:2, :] = bias_row
    small_ref[2:3, :] = jnp.sum(jnp.where(marked, grad, 0.0), axis=0, keepdims=True)
    wait_all(copies)


def encoder_ffn_backward(
    core, place, lengths, route, pieces_ref, hidden_one_ref, hidden_two_ref, table_ref, active_ref, slope_ref,
    mix_ref, part_a, part_b, part_c, part_d,
    kept_ref, sent_ref, grad_first_ref, small_ref, weight_ref, halves_ref, sems,
):
    rows, width = hidden_one_ref.shape
    groups, longest, _ = pieces_ref.shape
    weight_copies = bring_pieces(place, (part_a, part_b, part_c, part_d), weight_ref, sems)
    down = lax.broadcasted_iota(jnp.int32, (rows, longest), 0)
    across = lax.broadcasted_iota(jnp.int32, (rows, longest), 1)
    starts, counts = piece_places(lengths, route, lengths.shape[1])
    grad = jnp.zeros((rows, width), F32)
    for g in range(groups):
        chosen = (down - across == starts[g]) & (across < counts[g])
        grad = grad + nn(jnp.where(chosen, 1.0, 0.0).astype(BF16), pieces_ref[g])
    unit, scale = norm_parts(hidden_two_ref[...])
    grad, gain, bias_row = norm_back(grad, unit, scale, table_ref[2:3, :])
    grad_low = grad.astype(BF16)
    unit, scale = norm_parts(hidden_one_ref[...])
    low = (unit * table_ref[0:1, :] + table_ref[1:2, :]).astype(BF16)
    turned = low.T
    wait_all(weight_copies)
    for j in range(4):
        put_tall(halves_ref, core[0], j, 4, nn(active_ref[j].T, grad_low))
        grad_inner = (nt(grad_low, tall(weight_ref, j, 4)) * slope_ref[j].astype(F32)).astype(BF16)
        put(halves_ref, core[0], j, nn(turned, grad_inner))
        grad = grad + nt(grad_inner, block(weight_ref, j))
    small_ref[2:3, :] = gain
    small_ref[3:4, :] = bias_row
    grad, gain, bias_row = norm_back(grad, unit, scale, table_ref[0:1, :])
    small_ref[0:1, :] = gain
    small_ref[1:2, :] = bias_row
    put(halves_ref, core[0], 8, nn(mix_ref[...].T, grad.astype(BF16)))
    copies = send_halves(halves_ref, kept_ref, sent_ref, sems.at[pl.ds(32, 2)])
    grad_first_ref[...] = grad
    wait_all(copies)


def encoder_attention_backward(
    core, place, lengths, x_ref, qkv_ref, log_ref, grad_in_ref, small_one_ref, small_two_ref, small_three_ref,
    part_a, part_b, part_c, part_d,
    kept_ref, sent_ref, grad_x_ref, bias_ref, grad_mix_ref, grad_proj_ref, weight_ref, halves_ref, sems,
):
    rows, width = x_ref.shape
    weight_copies = bring_pieces(place, (part_a, part_b, part_c, part_d), weight_ref, sems)
    bias_ref[...] = segment_bias(lengths, rows)
    put_rows(halves_ref, 3, [small_three_ref[...], small_one_ref[0:2, :], small_two_ref[...], small_one_ref[2:3, :]])
    grad = grad_in_ref[...]
    wait_all(weight_copies)
    grad_mix_ref[...] = nt(grad.astype(BF16), block(weight_ref, 3)).astype(BF16)
    for pair in range(HEADS // 2):
        at = lanes(pair)
        queries, keys, values = [qkv_ref[i, :, at] for i in range(3)]
        logs = [log_ref[:, 2 * pair + head : 2 * pair + head + 1] for head in range(2)]
        parts = pair_weights(queries, keys, bias_ref[...], logs)
        grads = pair_backward(queries, keys, values, parts, grad_mix_ref[:, at])
        for i in range(3):
            grad_proj_ref[i, :, at] = grads[i]
    turned = x_ref[...].T
    for i in range(3):
        put(halves_ref, core[0], i, nn(turned, grad_proj_ref[i]))
    copies = send_halves(halves_ref, kept_ref, sent_ref, sems.at[pl.ds(32, 2)])
    for i in range(3):
        grad = grad + nt(grad_proj_ref[i], block(weight_ref, i))
    grad_x_ref[...] = grad
    wait_all(copies)


def finish(kept_ref, one_ref, two_ref, three_ref, *outs):
    total = kept_ref[...].astype(F32) + one_ref[...].astype(F32) + two_ref[...].astype(F32) + three_ref[...].astype(F32)
    width = total.shape[1]
    at = 0
    for ref in outs:
        if len(ref.shape) == 3:
            parts = [ref.at[i] for i in range(ref.shape[0])]
        else:
            parts = [ref.at[:, i * width : (i + 1) * width] for i in range(ref.shape[1] // width)]
        for one in parts:
            rows = one.shape[0]
            one[...] = total[at : at + rows, :]
            at += rows


VMEM = pl.BlockSpec(memory_space=pltpu.VMEM)
SMEM = pl.BlockSpec(memory_space=pltpu.SMEM)
ANY = pl.BlockSpec(memory_space=pl.ANY)


def run(kernel, scalars, arrays, outs, scratch=(), far=(), far_outs=(), sems=0, us=1.0, start=(), end=()):
    kinds = [pltpu.VMEM(shape, kind) for shape, kind in scratch]
    if sems:
        kinds.append(pltpu.SemaphoreType.DMA((sems,)))
    given, sends = (tuple(scalars), tuple(arrays), tuple(far)), [one.sends for one in start]
    if start:
        given, sends = lax.optimization_barrier((given, sends))
    for one, ready in zip(start, sends):
        one.sends = ready
        one.start()
    results = pl.pallas_call(
        kernel,
        out_shape=[jax.ShapeDtypeStruct(shape, kind) for shape, kind in outs],
        in_specs=[SMEM] * len(scalars) + [VMEM] * len(arrays) + [ANY] * len(far),
        out_specs=[ANY if index in far_outs else VMEM for index in range(len(outs))],
        scratch_shapes=kinds,
        compiler_params=pltpu.CompilerParams(vmem_limit_bytes=56 << 20),
        cost_estimate=pl.CostEstimate(flops=int(us * 1.15e9), bytes_accessed=1 << 20, transcendentals=0),
    )(*given[0], *given[1], *given[2])
    if end:
        results, got = lax.optimization_barrier((results, [one.got for one in end]))
        for one, blocks in zip(end, got):
            one.got = blocks
            one.finish()
    return results


def exchange(block, pairs):
    return lax.ppermute(block, AXES, pairs)


def pick(blocks, place):
    return lax.dynamic_index_in_dim(blocks, place, 0, keepdims=False)


def added(one, other):
    return (one.astype(F32) + other.astype(F32)).astype(BF16)


RING = (0, 1, 3, 2)


def sum_scatter(packs, count):
    me = lax.axis_index(AXES)
    core, low, high = me % 2, (me // 2) % 2, (me // 4) % 2
    rest = count // 8
    by_core = [pack.reshape((rest * 4, 2) + pack.shape[1:]) for pack in packs]
    sent, kept = [
        jnp.concatenate([lax.dynamic_index_in_dim(pack, side, 1, keepdims=False) for pack in by_core], axis=1)
        for side in (1 - core, core)
    ]
    tail = sent.shape[1:]
    kept = added(kept, exchange(sent, [(i, i ^ 1) for i in range(count)]))
    quads = kept.reshape((rest, 4) + tail)

    def two(first, second):
        parts = [lax.dynamic_index_in_dim(quads, place, 1, keepdims=True) for place in (first, second)]
        return jnp.concatenate(parts, axis=1)

    other_high, other_low = 1 - high, 1 - low
    sent = two(
        jnp.where(core == 0, 2 * other_high, other_low),
        jnp.where(core == 0, 2 * other_high + 1, other_low + 2),
    )
    kept = two(jnp.where(core == 0, 2 * high, low), jnp.where(core == 0, 2 * high + 1, low + 2))
    kept = added(kept, exchange(sent, [(i, i ^ (2 if i % 2 else 4)) for i in range(count)]))
    mine = jnp.where(core == 0, low, high)
    sent = lax.dynamic_index_in_dim(kept, 1 - mine, 1, keepdims=False)
    kept = lax.dynamic_index_in_dim(kept, mine, 1, keepdims=False)
    kept = added(kept, exchange(sent, [(i, i ^ (4 if i % 2 else 2)) for i in range(count)]))
    stride = 8
    while rest > 4:
        bit = (me // stride) % 2
        halves = kept.reshape((rest // 2, 2) + tail)
        sent = lax.dynamic_index_in_dim(halves, 1 - bit, 1, keepdims=False)
        kept = lax.dynamic_index_in_dim(halves, bit, 1, keepdims=False)
        kept = added(kept, exchange(sent, [(i, i ^ stride) for i in range(count)]))
        rest, stride = rest // 2, stride * 2
    order = RING if rest == 4 else tuple(range(rest))
    place_of = jnp.asarray([order.index(z) for z in range(rest)], jnp.int32)
    ring = jnp.asarray(order, jnp.int32)
    here = place_of[me // stride]
    onward = [
        (i, order[(order.index(i // stride) + 1) % rest] * stride + i % stride) for i in range(count)
    ]
    moving = pick(kept, ring[(here - 1) % rest]) if rest > 1 else kept[0]
    for step in range(rest - 1):
        arrived = exchange(moving, onward)
        own = pick(kept, ring[(here - 2 - step) % rest])
        moving = arrived.astype(F32) + own.astype(F32)
        if step < rest - 2:
            moving = moving.astype(BF16)
    return moving.astype(F32)


OUT_FIRST = [(i, i ^ (2 if i % 2 else 4)) for i in range(32)]
OUT_SECOND = [(i, i ^ (4 if i % 2 else 2)) for i in range(32)]
CORES = [(i, i ^ 1) for i in range(32)]


def gather_places():
    table = np.zeros((32, 32), np.int32)
    for me in range(32):
        for number in range(32):
            core = (me ^ (number // 16)) % 2
            first, second, level = (number // 8) % 2, (number // 4) % 2, number % 4
            x, y = (first, second) if core == 0 else (second, first)
            table[me, number] = ((me - me % 2) ^ (level * 8) ^ (x * 4) ^ (y * 2)) + core
    return table


def gather_blocks(mine):
    levels = [exchange(mine, [(i, i ^ (8 * k)) for i in range(32)]) for k in (1, 2, 3)]
    near = jnp.stack([mine] + levels)
    near = jnp.concatenate([near, exchange(near, OUT_SECOND)])
    far = exchange(near, OUT_FIRST)
    return near, far, exchange(near, CORES), exchange(far, CORES)


class Scatter:
    def __init__(self, kept, sent):
        me = lax.axis_index(AXES)
        core, low, high = me % 2, (me // 2) % 2, (me // 4) % 2
        self.bits = (jnp.where(core == 0, high, low), jnp.where(core == 0, low, high))
        self.level = me // 8
        self.kept, self.sends, self.stage = kept, [sent], 0

    def start(self):
        pairs = ([CORES], [OUT_FIRST], [OUT_SECOND], [[(i, i ^ (8 * k)) for i in range(32)] for k in (1, 2, 3)])
        self.got = [exchange(block, to) for block, to in zip(self.sends, pairs[self.stage])]
        return self.got

    def finish(self):
        if self.stage == 3:
            self.sends = []
            return self.sends
        got, size = self.got[0], self.kept.shape[0]

        def summed(place, count):
            return added(
                lax.dynamic_slice_in_dim(self.kept, place, count, 0), lax.dynamic_slice_in_dim(got, place, count, 0)
            )

        if self.stage < 2:
            half = size // 2
            bit = self.bits[self.stage]
            kept, sends = summed(bit * half, half), [summed((1 - bit) * half, half)]
        else:
            kept = summed(self.level, 1)[0]
            sends = [summed(jnp.bitwise_xor(self.level, k), 1)[0] for k in (1, 2, 3)]
        self.kept, self.sends, self.stage = kept, sends, self.stage + 1
        return self.sends


def on_device(
    enc_input,
    dec_input,
    target_mask,
    src_lengths,
    tgt_lengths,
    memory_route,
    enc_qkv,
    enc_out,
    enc_ffn_in,
    enc_ffn_out,
    enc_norms,
    dec_qkv,
    dec_out,
    cross_qkv,
    cross_out,
    dec_ffn_in,
    dec_ffn_out,
    dec_norms,
    mask_vector,
    out_cotangent,
):
    dp_count, groups = lax.axis_size("dp"), lax.axis_size("fsdp")
    count = dp_count * groups
    rows, width = enc_input.shape
    slots = src_lengths.shape[1]
    longest = rows // 2
    slot_rows = rows // slots
    part = enc_out.shape[0]
    inner = enc_ffn_in.shape[1]
    pieces_in = inner // width

    direct = count == 32 and part == 16
    kernel_part = width // 32
    joined = kernel_part // part
    me = lax.axis_index(AXES)
    my_dp, my_group = lax.axis_index("dp"), lax.axis_index("fsdp")

    def split(pack, squares):
        first = pack[:, : squares * part].reshape(32, joined, squares, part, width).transpose(0, 2, 1, 3, 4)
        return jnp.concatenate([first.reshape(32, -1, width), pack[:, squares * part :].reshape(32, -1, width)], axis=1)

    def unsplit(kept, sent, squares, used):
        kept = kept.reshape((2, 2, 4) + kept.shape[1:]).transpose(2, 0, 1, 3, 4)
        sent = sent.reshape((2, 2, 4) + sent.shape[1:]).transpose(2, 1, 0, 3, 4)
        pack = jnp.stack([kept, sent], axis=3).reshape(32, -1, width)
        first = pack[:, : squares * kernel_part].reshape(32, squares, joined, part, width).transpose(0, 2, 1, 3, 4)
        rest = pack[:, squares * kernel_part : used * kernel_part].reshape(count, -1, width)
        return jnp.concatenate([first.reshape(count, -1, width), rest], axis=1)

    if direct:
        core = (me % 2).reshape(1)
        attention_pack, ffn_pack, decoder_pack = run(
            pack_weights,
            (me.reshape(1),),
            (
                src_lengths, memory_route, mask_vector.reshape(1, part),
                enc_qkv, enc_out, enc_ffn_in, enc_ffn_out, enc_norms,
                dec_qkv, dec_out, cross_qkv, cross_out, dec_ffn_in, dec_ffn_out, dec_norms,
            ),
            (((5 * part, width), BF16), ((8 * part, width), BF16), ((16 * part, width), BF16)),
            us=2.0,
        )
        dec_all = lax.all_gather(decoder_pack, AXES, axis=0, tiled=False)
        attention_blocks = gather_blocks(attention_pack)
        ffn_blocks = gather_blocks(ffn_pack)
        place = jnp.asarray(gather_places())[me]
    else:
        core = jnp.zeros((1,), jnp.int32)

        def square(weight):
            return weight.reshape(-1, width)

        def wide(weight):
            return weight.reshape(part, pieces_in, width).transpose(1, 0, 2).reshape(-1, width)

        def whole(norms):
            return lax.all_gather(norms, AXES, axis=norms.ndim - 1, tiled=True).reshape(-1, width)

        def gathered(weights):
            return lax.all_gather(jnp.concatenate(weights), AXES, axis=0, tiled=False)

        rows_of = [whole(enc_norms), whole(dec_norms), whole(mask_vector)]
        first_rows = jnp.pad(jnp.concatenate(rows_of), ((0, kernel_part - 11), (0, 0)))
        small_blocks = jnp.concatenate([first_rows[None], jnp.zeros((31, kernel_part, width), BF16)])
        attention_all = split(gathered([square(enc_qkv), enc_out]), 4)
        attention_all = jnp.concatenate([attention_all, small_blocks], axis=1)
        attention_blocks = tuple(attention_all[i * 8 : i * 8 + 8] for i in range(4))
        ffn_all = split(gathered([wide(enc_ffn_in), enc_ffn_out]), pieces_in)
        ffn_blocks = tuple(ffn_all[i * 8 : i * 8 + 8] for i in range(4))
        decoder = [square(dec_qkv), dec_out, square(cross_qkv), cross_out, wide(dec_ffn_in), dec_ffn_out]
        dec_all = split(gathered(decoder), 8 + pieces_in)
        place = jnp.arange(32, dtype=jnp.int32)

    plane, three = (rows, width), (3, rows, width)
    memory_shape = (groups, longest, width)
    logs_shape = (rows, HEADS)
    parts_shape = (slots, HEADS, slot_rows, longest)

    def half_of(pieces):
        return ((16, pieces * kernel_part, width), BF16)

    def halves_of(pieces):
        return ((2, 16, pieces * kernel_part, width), BF16)

    def weights_of(pieces):
        return ((32, pieces * kernel_part, width), BF16)

    e_qkv, e_mix, e_logs, e_hidden_one, table = run(
        encoder_attention,
        (place, src_lengths),
        (enc_input,),
        ((three, BF16), (plane, BF16), (logs_shape, F32), (plane, F32), ((kernel_part, width), F32)),
        (((rows, rows), F32), weights_of(5)),
        far=attention_blocks,
        sems=32,
        us=9.5,
    )
    half_ffn = ((4, rows, width), BF16)
    pieces, e_hidden_two, e_active, e_slope = run(
        encoder_ffn,
        (place, src_lengths, memory_route),
        (e_hidden_one, table),
        ((memory_shape, BF16), (plane, F32), half_ffn, half_ffn),
        (half_ffn, half_ffn, weights_of(2 * pieces_in)),
        far=ffn_blocks,
        far_outs=(2, 3),
        sems=34,
        us=9.0,
    )
    memory_in = lax.all_to_all(pieces, "fsdp", split_axis=0, concat_axis=0, tiled=True)
    marked = target_mask[:, None]
    d_qkv, d_mix, d_logs, d_hidden = run(
        self_forward,
        (tgt_lengths,),
        (dec_input, marked, table),
        ((three, BF16), (plane, BF16), (logs_shape, F32), (plane, F32)),
        (weights_of(4),),
        far=(dec_all,),
        sems=1,
        us=6.4,
    )
    if direct:
        ints = table[11].reshape(dp_count, groups, part)
        ints = lax.dynamic_index_in_dim(ints, my_dp, 0, keepdims=False).astype(jnp.int32)
        lengths_near, route_near = ints[:, :slots], ints[:, slots : 2 * slots]
    else:
        lengths_near = lax.all_gather(src_lengths[0], "fsdp")
        route_near = lax.all_gather(memory_route[0], "fsdp")
    ids = jnp.arange(groups, dtype=jnp.int32)
    wanted = my_group * slots + jnp.arange(slots, dtype=jnp.int32)
    chosen = route_near[None] == wanted[:, None, None]
    slot_source = jnp.sum(jnp.where(chosen, ids[None, :, None], 0), axis=(1, 2))
    slot_length = jnp.sum(jnp.where(chosen, lengths_near[None], 0), axis=(1, 2))

    dec_output, kept, sent, parts, q_rows, kv_rows, c_mix, grad_second, small_two = run(
        decoder_upper,
        (core, slot_source, slot_length),
        (d_hidden, memory_in, out_cotangent, table),
        (
            (plane, BF16), half_of(8), half_of(8), (parts_shape, F32), (plane, BF16), ((2,) + memory_shape, BF16),
            (plane, BF16), (plane, F32), ((4, width), F32),
        ),
        (
            (parts_shape, F32), ((4, rows, width), F32), half_ffn, weights_of(4), weights_of(8), halves_of(8),
        ),
        far=(dec_all,),
        far_outs=(1, 2, 3),
        sems=5,
        us=23.0,
    )

    def begin(kept, sent):
        return Scatter(kept, sent) if direct else None

    def some(*chains):
        return chains if direct else ()

    dffn_halves = (kept, sent)
    dffn = begin(kept, sent)
    *cross_halves, grad_memory, grad_first = run(
        cross_backward,
        (core, slot_source),
        (d_hidden, memory_in, table, q_rows, kv_rows, c_mix, grad_second),
        (half_of(4), half_of(4), (memory_shape, BF16), (plane, F32)),
        (
            (parts_shape, F32), (plane, BF16), (plane, BF16), ((2,) + memory_shape, BF16), weights_of(4), halves_of(4),
        ),
        far=(dec_all, parts),
        far_outs=(0, 1),
        sems=4,
        us=16.0,
        start=some(dffn),
        end=some(dffn),
    )
    returned = lax.all_to_all(grad_memory, "fsdp", split_axis=0, concat_axis=0, tiled=True)
    *own_halves, dec_input_grad, small_one = run(
        self_backward,
        (core, tgt_lengths),
        (dec_input, marked, table, d_qkv, d_mix, d_logs, d_hidden, grad_first),
        (half_of(4), half_of(4), (plane, F32), ((3, width), F32)),
        ((plane, BF16), (three, BF16), weights_of(4), halves_of(4)),
        far=(dec_all,),
        far_outs=(0, 1),
        sems=3,
        us=12.4,
        start=some(dffn),
        end=some(dffn),
    )
    middle = begin(*[jnp.concatenate(halves, axis=1) for halves in zip(cross_halves, own_halves)])
    *effn_halves, grad_enc, small_three = run(
        encoder_ffn_backward,
        (core, place, src_lengths, memory_route),
        (returned, e_hidden_one, e_hidden_two, table, e_active, e_slope, e_mix),
        (half_of(9), half_of(9), (plane, F32), ((4, width), F32)),
        (weights_of(8), halves_of(9)),
        far=ffn_blocks,
        far_outs=(0, 1),
        sems=34,
        us=14.0,
        start=some(dffn, middle),
        end=some(dffn, middle),
    )
    effn = begin(*effn_halves)
    *eatt_halves, enc_input_grad = run(
        encoder_attention_backward,
        (core, place, src_lengths),
        (enc_input, e_qkv, e_logs, grad_enc, small_one, small_two, small_three),
        (half_of(4), half_of(4), (plane, F32)),
        (((rows, rows), F32), (plane, BF16), (three, BF16), weights_of(5), halves_of(4)),
        far=attention_blocks,
        far_outs=(0, 1),
        sems=34,
        us=15.0,
        start=some(dffn, middle, effn),
        end=some(middle, effn),
    )
    eatt = begin(*eatt_halves)

    def ends(chain, *shapes):
        return run(finish, (), (chain.kept, *chain.got), [(shape, F32) for shape in shapes])

    cube, square_part, wide_part, tall_part = (3, part, width), (part, width), (part, inner), (inner // count, width)
    if direct:
        dec_ffn_grads = ends(dffn, wide_part, tall_part)
        eatt.start()
        middle.start()
        effn.start()
        eatt.finish()
        eatt.start()
        middle.finish()
        middle.start()
        middle_grads = ends(middle, cube, square_part, cube, square_part)
        effn.finish()
        effn.start()
        eatt.finish()
        eatt.start()
        effn.finish()
        effn.start()
        enc_ffn_grads = ends(effn, wide_part, tall_part, square_part)
        eatt.finish()
        eatt.start()
        qkv_grads, small_sum = ends(eatt, cube, square_part)
    else:

        def piece(summed, first, pieces=1):
            return summed[first * part : (first + pieces) * part]

        def wide_piece(summed):
            picked = piece(summed, 0, pieces_in).reshape(pieces_in, part, width)
            return picked.transpose(1, 0, 2).reshape(part, inner)

        effn_pack = unsplit(*[half[:, : 8 * kernel_part] for half in effn_halves], 4, 8)
        eout_pack = unsplit(*[half[:, 8 * kernel_part :] for half in effn_halves], 1, 1)
        packs = [
            unsplit(*dffn_halves, 4, 8),
            jnp.concatenate([unsplit(*cross_halves, 4, 4), unsplit(*own_halves, 4, 4)], axis=1),
            jnp.concatenate([effn_pack, eout_pack], axis=1),
            unsplit(*eatt_halves, 3, 3),
        ]
        dffn_sum, middle_sum, effn_sum, eatt_sum = [sum_scatter([pack], count) for pack in packs]
        dec_ffn_grads = (wide_piece(dffn_sum), piece(dffn_sum, pieces_in, pieces_in))
        enc_ffn_grads = (wide_piece(effn_sum), piece(effn_sum, pieces_in, pieces_in), piece(effn_sum, 8))
        middle_grads = [
            piece(middle_sum, 0, 3).reshape(cube), piece(middle_sum, 3), piece(middle_sum, 4, 3).reshape(cube), piece(middle_sum, 7)
        ]
        qkv_grads = piece(eatt_sum, 0, 3).reshape(cube)
        small_sum = lax.psum(eatt_halves[0][0, 3 * kernel_part :].astype(F32), AXES)

    small_sum = lax.dynamic_slice_in_dim(small_sum[:11], me * part, part, 1)
    return (
        dec_output,
        enc_input_grad,
        dec_input_grad,
        qkv_grads,
        enc_ffn_grads[2],
        *enc_ffn_grads[:2],
        small_sum[:4].reshape(2, 2, part),
        *middle_grads[2:],
        *middle_grads[:2],
        *dec_ffn_grads,
        small_sum[4:10].reshape(3, 2, part),
        small_sum[10],
    )


def solution(mesh):
    rows = P(AXES, None)
    flat = P(AXES)
    cube = P(None, AXES, None)
    norm = P(None, None, AXES)
    in_specs = (
        (rows, rows, flat, rows, rows, rows)
        + (cube, rows, rows, rows, norm)
        + (cube, rows, cube, rows, rows, rows, norm, flat)
        + (rows,)
    )
    out_specs = (
        (rows, rows, rows)
        + (cube, rows, rows, rows, norm)
        + (cube, rows, cube, rows, rows, rows, norm, flat)
    )
    return jax.shard_map(on_device, mesh=mesh, in_specs=in_specs, out_specs=out_specs, check_vma=False)
```

```python
import math
from functools import partial

import jax
import jax.numpy as jnp
import numpy as np
from jax import lax
from jax.experimental import pallas as pl
from jax.experimental.pallas import tpu as pltpu
from jax.sharding import PartitionSpec as P

HEADS = 8
HEAD_DIM = 64
SCALE = 1.0 / math.sqrt(HEAD_DIM)
AXES = ("dp", "fsdp")
F32 = jnp.float32
BF16 = jnp.bfloat16


MASKED = -1e30
GELU_C = math.sqrt(2.0 / math.pi)
GELU_A = 0.044715


def nn(left, right):
    return jnp.dot(left, right, preferred_element_type=F32)


def nt(left, right):
    return lax.dot_general(left, right, (((1,), (1,)), ((), ())), preferred_element_type=F32)


def norm_parts(hidden):
    center = hidden - jnp.mean(hidden, axis=-1, keepdims=True)
    scale = lax.rsqrt(jnp.mean(center * center, axis=-1, keepdims=True) + 1e-05)
    return center * scale, scale


def norm_back(grad, unit, scale, gain):
    inner = grad * gain
    mean_one = jnp.mean(inner, axis=-1, keepdims=True)
    mean_two = jnp.mean(inner * unit, axis=-1, keepdims=True)
    return (
        scale * (inner - mean_one - unit * mean_two),
        jnp.sum(grad * unit, axis=0, keepdims=True),
        jnp.sum(grad, axis=0, keepdims=True),
    )


def gelu_tanh(pre):
    return jnp.tanh(GELU_C * (pre + GELU_A * (pre * pre * pre)))


def gelu_back(pre):
    tanh = gelu_tanh(pre)
    slope = GELU_C * (1.0 + 3.0 * GELU_A * (pre * pre))
    return 0.5 * pre * (1.0 + tanh), 0.5 * (1.0 + tanh) + 0.5 * pre * (1.0 - tanh * tanh) * slope


def block(ref, first):
    width = ref.shape[2]
    part = width // ref.shape[0]
    return ref[:, first * part : (first + 1) * part, :].reshape(width, width)


def wide(ref, first, count):
    return jnp.concatenate([block(ref, first + index) for index in range(count)], axis=1)


def tall(ref, first):
    count, _, width = ref.shape
    part = width // count
    return ref[:, first * part : (first + 4) * part, :].reshape(4 * width, width)


CORNERS = [(x, y, side) for x in range(2) for y in range(2) for side in range(2)]


def place_of(x, y, side):
    return 8 * x + 4 * y if side == 0 else 8 * y + 4 * x


def put(ref, core, first, grad):
    width = grad.shape[1]
    part = width // 32
    cut = grad.astype(BF16).reshape(4, 2, 2, 2, part, width)
    rows = slice(first * part, (first + 1) * part)
    for x, y, side in CORNERS:
        half = core if side == 0 else 1 - core
        place = place_of(x, y, side)
        ref[half, place : place + 4, rows, :] = cut[:, x, y, side]


def put_wide(ref, core, first, grad):
    width = ref.shape[3]
    for index in range(grad.shape[1] // width):
        put(ref, core, first + index, grad[:, index * width : (index + 1) * width])


def put_tall(ref, core, first, grad):
    width = grad.shape[1]
    part = width // 32
    rows = slice(first * part, (first + 4) * part)
    cut = grad.astype(BF16).reshape(4, 2, 2, 2, 4 * part, width)
    for x, y, side in CORNERS:
        half = core if side == 0 else 1 - core
        place = place_of(x, y, side)
        ref[half, place : place + 4, rows, :] = cut[:, x, y, side]


def put_rows(ref, first, rows_of):
    halves, count, _, width = ref.shape
    part = width // (halves * count)
    used = sum(row.shape[0] for row in rows_of)
    rows = jnp.concatenate(rows_of + [jnp.zeros((part - used, width), F32)], axis=0)
    ref[:, :, first * part : (first + 1) * part, :] = jnp.broadcast_to(
        rows.astype(BF16)[None, None], (halves, count, part, width)
    )


def bring_pieces(place, refs, target, sems, first=0):
    part = target.shape[2] // target.shape[0]
    rows = pl.ds(first * part, target.shape[1])
    copies = []
    for array, ref in enumerate(refs):
        for index in range(8):
            number = array * 8 + index
            copies.append(pltpu.make_async_copy(ref.at[index, rows], target.at[place[number]], sems.at[number]))
    for copy in copies:
        copy.start()
    return copies


def bring_rows(ref, first, count, target, sem):
    copy = pltpu.make_async_copy(ref.at[:, pl.ds(first, count), :], target, sem)
    copy.start()
    return copy


def send_halves(halves_ref, kept_ref, sent_ref, sems, first=0, count=None):
    part = halves_ref.shape[3] // 32
    rows = pl.ds(first * part, halves_ref.shape[2] if count is None else count * part)
    copies = [
        pltpu.make_async_copy(halves_ref.at[half, :, rows], ref.at[:, rows], sems.at[half])
        for half, ref in enumerate((kept_ref, sent_ref))
    ]
    for copy in copies:
        copy.start()
    return copies


def wait_all(copies):
    for copy in copies:
        copy.wait()


PAIR = 2 * HEAD_DIM


def twice(pair_rows):
    lane = lax.broadcasted_iota(jnp.int32, pair_rows.shape, 1)
    zero = jnp.zeros_like(pair_rows)
    return jnp.concatenate(
        [jnp.where(lane < HEAD_DIM, pair_rows, zero), jnp.where(lane < HEAD_DIM, zero, pair_rows)], axis=0
    )


def each_head(scores, count):
    return [scores[:, head * count : (head + 1) * count] for head in range(2)]


def pair_scores(queries, keys):
    return jnp.concatenate([nt(q, twice(k)) for q, k in zip(queries, keys)], axis=0)


def pair_forward(queries, keys, values, bias):
    count = keys[0][0].shape[0]
    scores = [pair_scores(q, k) for q, k in zip(queries, keys)]
    masked = [part + bias for both in scores for part in each_head(both, count)]
    tops = [jnp.max(part, axis=-1, keepdims=True) for part in masked]
    raised = [jnp.exp(part - top) for part, top in zip(masked, tops)]
    totals = [jnp.sum(part, axis=-1, keepdims=True) for part in raised]
    parts = [part * (1.0 / total) for part, total in zip(raised, totals)]
    logs = [top + jnp.log(total) for top, total in zip(tops, totals)]
    mixtures = []
    for pair, blocks in enumerate(values):
        low = jnp.concatenate([part.astype(BF16) for part in parts[2 * pair : 2 * pair + 2]], axis=1)
        rows = low.shape[0] // len(blocks)
        mixed = [nn(low[i * rows : (i + 1) * rows], twice(v)) for i, v in enumerate(blocks)]
        mixtures.append(jnp.concatenate(mixed, axis=0))
    return mixtures, parts, logs


def pair_weights(queries, keys, bias, logs):
    scores = each_head(pair_scores(queries, keys), keys[0].shape[0])
    return [jnp.exp(part + bias - log) for part, log in zip(scores, logs)]


def turned_products(rows_of, weights, count):
    rows = weights.shape[0] // len(rows_of)
    results = []
    for index, block_rows in enumerate(rows_of):
        both = nn(block_rows.T, weights[index * rows : (index + 1) * rows])
        own = jnp.concatenate([both[:HEAD_DIM, :count], both[HEAD_DIM:, count:]], axis=0)
        results.append(own.astype(BF16).T)
    return results


def pair_backward(queries, keys, values, parts, grads_out):
    count = keys[0].shape[0]
    grad_parts = each_head(pair_scores(grads_out, values), count)
    grad_scores = []
    for part, grad_part in zip(parts, grad_parts):
        delta = jnp.sum(part * grad_part, axis=-1, keepdims=True)
        grad_scores.append((part * (grad_part - delta)).astype(BF16))
    grad_scores = jnp.concatenate(grad_scores, axis=1)
    weights = jnp.concatenate([part.astype(BF16) for part in parts], axis=1)
    rows = grad_scores.shape[0] // len(keys)
    grad_query = [nn(grad_scores[i * rows : (i + 1) * rows], twice(k)) for i, k in enumerate(keys)]
    return (
        (jnp.concatenate(grad_query, axis=0) * SCALE).astype(BF16),
        turned_products(queries, grad_scores, count),
        turned_products(grads_out, weights, count),
    )


def sentence_starts(lengths):
    starts = [0]
    for sentence in range(lengths.shape[1] - 1):
        starts.append(starts[-1] + lengths[0, sentence])
    return starts


def piece_places(lengths, route, slots):
    starts = sentence_starts(lengths)
    first, length = [], []
    for device in range(route.shape[1]):
        here, count = jnp.int32(0), jnp.int32(0)
        for sentence in range(route.shape[1]):
            goes = route[0, sentence] // slots == device
            here = here + jnp.where(goes, starts[sentence], 0)
            count = count + jnp.where(goes, lengths[0, sentence], 0)
        first.append(here)
        length.append(count)
    return first, length


def segment_bias(lengths, rows):
    down = lax.broadcasted_iota(jnp.int32, (rows, 1), 0)
    across = lax.broadcasted_iota(jnp.int32, (1, rows), 1)
    segment_down = jnp.zeros_like(down)
    segment_across = jnp.zeros_like(across)
    starts = sentence_starts(lengths)
    for sentence in range(1, len(starts)):
        segment_down += (down >= starts[sentence]).astype(jnp.int32)
        segment_across += (across >= starts[sentence]).astype(jnp.int32)
    return jnp.where(segment_down == segment_across, 0.0, MASKED)


def lanes(pair):
    return slice(pair * PAIR, (pair + 1) * PAIR)


def pack_weights(
    me, src_ref, route_ref, mask_ref, e_qkv_ref, e_out_ref, e_in_ref, e_outff_ref, e_norm_ref,
    d_qkv_ref, d_out_ref, c_qkv_ref, c_out_ref, d_in_ref, d_outff_ref, d_norm_ref,
    attention_ref, ffn_ref, decoder_ref,
):
    part, width = e_out_ref.shape
    lane = lax.broadcasted_iota(jnp.int32, (part, width), 1)
    row = lax.broadcasted_iota(jnp.int32, (part, width), 0)
    spread = jnp.where(lane - row == me[0] * part, 1.0, 0.0).astype(BF16)
    ints = [nn(ref[...].astype(F32).astype(BF16), spread[4 * i : 4 * i + 4]) for i, ref in enumerate((src_ref, route_ref))]
    rows = [nn(e_norm_ref[i], spread) for i in range(2)] + [nn(d_norm_ref[i], spread) for i in range(3)]
    rows = rows + [nn(mask_ref[...], spread), ints[0] + ints[1]]
    used = sum(r.shape[0] for r in rows)
    rows = jnp.concatenate(rows + [jnp.zeros((part - used, width), F32)], axis=0)

    def fill(ref, first, weight):
        ref[first * part : first * part + weight.shape[0], :] = weight

    for i in range(3):
        fill(attention_ref, i, e_qkv_ref[i])
        fill(decoder_ref, i, d_qkv_ref[i])
        fill(decoder_ref, 4 + i, c_qkv_ref[i])
    fill(attention_ref, 3, e_out_ref[...])
    fill(attention_ref, 4, rows.astype(BF16))
    fill(decoder_ref, 3, d_out_ref[...])
    fill(decoder_ref, 7, c_out_ref[...])
    for j in range(4):
        fill(ffn_ref, j, e_in_ref[:, j * width : (j + 1) * width])
        fill(decoder_ref, 8 + j, d_in_ref[:, j * width : (j + 1) * width])
    fill(ffn_ref, 4, e_outff_ref[...])
    fill(decoder_ref, 12, d_outff_ref[...])


def put_logs(log_ref, pairs, logs):
    for index, log in enumerate(logs):
        head = 2 * pairs[0] + index
        log_ref[:, head : head + 1] = log


def encoder_attention(
    place, lengths, x_ref, part_a, part_b, part_c, part_d,
    mix_ref, log_ref, hidden_ref, table_ref, qkv, bias_ref, weight_ref, sems,
):
    rows, width = x_ref.shape
    copies = bring_pieces(place, (part_a, part_b, part_c, part_d), weight_ref, sems)
    rows_in = x_ref[...]
    bias_ref[...] = segment_bias(lengths, rows)
    wait_all(copies)
    part = width // weight_ref.shape[0]
    table_ref[...] = jnp.sum(weight_ref[:, 4 * part : 5 * part, :].astype(F32), axis=0)
    qkv_ref = qkv.ref
    qkv_ref[0] = (nn(rows_in, block(weight_ref, 0)) * SCALE).astype(BF16)
    qkv_ref[1] = nn(rows_in, block(weight_ref, 1)).astype(BF16)
    qkv_ref[2] = nn(rows_in, block(weight_ref, 2)).astype(BF16)
    qkv.send()
    for pair in range(HEADS // 2):
        at = lanes(pair)
        mixtures, _, logs = pair_forward(*[[[qkv_ref[i, :, at]]] for i in range(3)], bias_ref[...])
        mix_ref[:, at] = mixtures[0].astype(BF16)
        put_logs(log_ref, (pair,), logs)
    hidden_ref[...] = rows_in.astype(F32) + nn(mix_ref[...], block(weight_ref, 3))


def encoder_ffn(
    place, lengths, route, hidden_one_ref, table_ref, part_a, part_b, part_c, part_d,
    pieces_ref, active, slope, hidden_two, weight_ref, sems,
):
    rows, width = hidden_one_ref.shape
    groups, longest, _ = pieces_ref.shape
    copies = bring_pieces(place, (part_a, part_b, part_c, part_d), weight_ref, sems)
    unit, _ = norm_parts(hidden_one_ref[...])
    first = unit * table_ref[0:1, :] + table_ref[1:2, :]
    low = first.astype(BF16)
    wait_all(copies)
    for j in range(4):
        value, slope_value = gelu_back(nn(low, block(weight_ref, j)))
        active.ref[:, j * width : (j + 1) * width] = value.astype(BF16)
        slope.ref[:, j * width : (j + 1) * width] = slope_value.astype(BF16)
    active.send()
    slope.send()
    hidden = first + nn(active.ref[...], tall(weight_ref, 4))
    hidden_two.ref[...] = hidden
    hidden_two.send()
    unit, _ = norm_parts(hidden)
    memory = (unit * table_ref[2:3, :] + table_ref[3:4, :]).astype(BF16)
    down = lax.broadcasted_iota(jnp.int32, (longest, rows), 0)
    across = lax.broadcasted_iota(jnp.int32, (longest, rows), 1)
    starts, _ = piece_places(lengths, route, lengths.shape[1])
    for g in range(groups):
        chosen = jnp.where(across - down == starts[g], 1.0, 0.0).astype(BF16)
        pieces_ref[g] = nn(chosen, memory).astype(BF16)


def replaced(target_ref, table_ref, rows_ref):
    marked = target_ref[...] == 1
    return jnp.where(marked, table_ref[10:11, :], rows_ref[...].astype(F32))


def slot_bias(length, count):
    across = lax.broadcasted_iota(jnp.int32, (1, count), 1)
    return jnp.where(across < length, 0.0, MASKED)


def slot_biases(lengths, count, rows):
    return jnp.concatenate(
        [jnp.broadcast_to(slot_bias(length, count), (rows, count)) for length in lengths], axis=0
    )


def slot_rows_of(rows, slots):
    return [slice(slot * (rows // slots), (slot + 1) * (rows // slots)) for slot in range(slots)]


def self_forward(
    lengths, x_ref, target_ref, table_ref, gathered_ref,
    mix_ref, log_ref, hidden_ref, target_out_ref, qkv, weight_ref, sems,
):
    rows, width = x_ref.shape
    slots = lengths.shape[1]
    target_out_ref[...] = target_ref[...]
    copies = [bring_rows(gathered_ref, 0, weight_ref.shape[1], weight_ref, sems.at[0])]
    start = replaced(target_ref, table_ref, x_ref)
    low = start.astype(BF16)
    bias = slot_biases([lengths[0, slot] for slot in range(slots)], rows // slots, rows // slots)
    wait_all(copies)
    qkv_ref = qkv.ref
    qkv_ref[0] = (nn(low, block(weight_ref, 0)) * SCALE).astype(BF16)
    qkv_ref[1] = nn(low, block(weight_ref, 1)).astype(BF16)
    qkv_ref[2] = nn(low, block(weight_ref, 2)).astype(BF16)
    qkv.send()
    for first in range(0, HEADS // 2, 2):
        pairs = (first, first + 1)
        mixtures, _, logs = pair_forward(
            *[[[qkv_ref[i, here, lanes(pair)] for here in slot_rows_of(rows, slots)] for pair in pairs] for i in range(3)], bias
        )
        for pair, mixture in zip(pairs, mixtures):
            mix_ref[:, lanes(pair)] = mixture.astype(BF16)
        put_logs(log_ref, pairs, logs)
    hidden_ref[...] = start + nn(mix_ref[...], block(weight_ref, 3))


def decoder_upper(
    core, slot_source, slot_length, hidden_ref, memory_ref, table_ref, cotangent, gathered_ref,
    output_ref, kept_ref, sent_ref, grad_ref, small_ref, parts, q, kv, mix,
    slope_ref, active_ref, inner_ref, weight_ref, ffn_ref, halves_ref, sems,
):
    rows, width = hidden_ref.shape
    slots = slot_source.shape[0]
    groups, longest, _ = memory_ref.shape
    part_rows = weight_ref.shape[1]
    cross_copy = bring_rows(gathered_ref, part_rows, part_rows, weight_ref, sems.at[0])
    ffn_copy = bring_rows(gathered_ref, 2 * part_rows, 2 * part_rows, ffn_ref, sems.at[1])
    unit, _ = norm_parts(hidden_ref[...])
    first = unit * table_ref[4:5, :] + table_ref[5:6, :]
    first_low = first.astype(BF16)
    memory = memory_ref[...].reshape(groups * longest, width)
    cross_copy.wait()
    q.ref[...] = (nn(first_low, block(weight_ref, 0)) * SCALE).astype(BF16)
    for i in range(2):
        kv.ref[i] = nn(memory, block(weight_ref, 1 + i)).astype(BF16).reshape(groups, longest, width)
    q.send()
    kv.send()
    bias = slot_biases([slot_length[slot] for slot in range(slots)], longest, rows // slots)
    sources = [slot_source[slot] for slot in range(slots)]
    for start in range(0, HEADS // 2, 2):
        pairs = (start, start + 1)
        mixtures, weights, _ = pair_forward(
            [[q.ref[here, lanes(pair)] for here in slot_rows_of(rows, slots)] for pair in pairs],
            [[kv.ref[0, source, :, lanes(pair)] for source in sources] for pair in pairs],
            [[kv.ref[1, source, :, lanes(pair)] for source in sources] for pair in pairs],
            bias,
        )
        for index, pair in enumerate(pairs):
            mix.ref[:, lanes(pair)] = mixtures[index].astype(BF16)
            for head in range(2):
                parts.ref[2 * pair + head] = weights[2 * index + head]
    parts.send()
    mix.send()
    hidden = first + nn(mix.ref[...], block(weight_ref, 3))
    unit_two, scale_two = norm_parts(hidden)
    second = unit_two * table_ref[6:7, :] + table_ref[7:8, :]
    low = second.astype(BF16)
    ffn_copy.wait()
    for j in range(4):
        at = slice(j * width, (j + 1) * width)
        active, slope = gelu_back(nn(low, block(ffn_ref, j)))
        slope_ref[:, at] = slope
        active_ref[:, at] = active.astype(BF16)
    hidden = second + nn(active_ref[...], tall(ffn_ref, 4))
    unit_three, scale_three = norm_parts(hidden)
    output_ref[...] = (unit_three * table_ref[8:9, :] + table_ref[9:10, :]).astype(BF16)
    grad, gain_three, bias_three = norm_back(
        cotangent.get()[...].astype(F32), unit_three, scale_three, table_ref[8:9, :]
    )
    grad_low = grad.astype(BF16)
    put_tall(halves_ref, core[0], 4, nn(active_ref[...].T, grad_low))
    inner_ref[...] = (nt(grad_low, tall(ffn_ref, 4)) * slope_ref[...]).astype(BF16)
    put_wide(halves_ref, core[0], 0, nn(low.T, inner_ref[...]))
    copies = send_halves(halves_ref, kept_ref, sent_ref, sems.at[pl.ds(2, 2)])
    grad = grad + nt(inner_ref[...], wide(ffn_ref, 0, 4))
    grad, gain_two, bias_two = norm_back(grad, unit_two, scale_two, table_ref[6:7, :])
    grad_ref[...] = grad
    for index, row in enumerate((gain_two, bias_two, gain_three, bias_three)):
        small_ref[index : index + 1, :] = row
    wait_all(copies)


def cross_backward(
    slot_source, grad_second_ref, q, kv, parts, gathered_ref,
    grad_memory_ref, grad_q_ref, grad_kv_ref, grad_mix_ref, weight_ref, sems,
):
    rows, width = grad_second_ref.shape
    slots = slot_source.shape[0]
    _, groups, longest, _ = grad_kv_ref.shape
    part_rows = weight_ref.shape[1]
    cross_copy = bring_rows(gathered_ref, part_rows, part_rows, weight_ref, sems.at[0])
    grad_low = grad_second_ref[...].astype(BF16)
    cross_copy.wait()
    grad_mix_ref[...] = nt(grad_low, block(weight_ref, 3)).astype(BF16)
    q_ref, kv_ref, parts_ref = q.get(), kv.get(), parts.get()
    sources = [slot_source[slot] for slot in range(slots)]
    slices = slot_rows_of(rows, slots)
    for pair in range(HEADS // 2):
        at = lanes(pair)
        grad_query, grads_k, grads_v = pair_backward(
            [q_ref[here, at] for here in slices],
            [kv_ref[0, source, :, at] for source in sources],
            [kv_ref[1, source, :, at] for source in sources],
            [parts_ref[2 * pair + head] for head in range(2)],
            [grad_mix_ref[here, at] for here in slices],
        )
        grad_q_ref[:, at] = grad_query
        for source, grad_k, grad_v in zip(sources, grads_k, grads_v):
            grad_kv_ref[0, source, :, at] = grad_k
            grad_kv_ref[1, source, :, at] = grad_v
    grad_k = grad_kv_ref[0].reshape(groups * longest, width)
    grad_v = grad_kv_ref[1].reshape(groups * longest, width)
    grad_memory_ref[...] = (
        (nt(grad_k, block(weight_ref, 1)) + nt(grad_v, block(weight_ref, 2)))
        .astype(BF16)
        .reshape(groups, longest, width)
    )


def decoder_lower(
    core, lengths, table_ref, grad_second_ref, grad_q_ref, hidden_ref, mix, memory, grad_kv, own_mix, qkv, logs_in, x, target, gathered_ref,
    kept_ref, sent_ref, grad_x_ref, small_ref, grad_mix_ref, grad_proj_ref, weight_ref, halves_ref, sems,
):
    rows, width = hidden_ref.shape
    slots = lengths.shape[1]
    copies = [bring_rows(gathered_ref, 0, weight_ref.shape[1], weight_ref, sems.at[0])]
    unit, scale = norm_parts(hidden_ref[...])
    first_low = (unit * table_ref[4:5, :] + table_ref[5:6, :]).astype(BF16)
    put(halves_ref, core[0], 0, nn(first_low.T, grad_q_ref[...]))
    grad_second = grad_second_ref[...]
    put(halves_ref, core[0], 3, nn(mix.get()[...].T, grad_second.astype(BF16)))
    wait_all(copies)
    grad = grad_second + nt(grad_q_ref[...], block(weight_ref, 4))
    grad, gain, bias_row = norm_back(grad, unit, scale, table_ref[4:5, :])
    grad_low = grad.astype(BF16)
    grad_mix_ref[...] = nt(grad_low, block(weight_ref, 3)).astype(BF16)
    put(halves_ref, core[0], 7, nn(own_mix.get()[...].T, grad_low))
    memory_ref, grad_kv_ref = memory.get(), grad_kv.get()
    turned = memory_ref[...].reshape(-1, width).T
    for i in range(2):
        put(halves_ref, core[0], 1 + i, nn(turned, grad_kv_ref[i].reshape(-1, width)))
    copies = send_halves(halves_ref, kept_ref, sent_ref, sems.at[pl.ds(1, 2)], 0, 4)
    bias = slot_biases([lengths[0, slot] for slot in range(slots)], rows // slots, rows // slots)
    qkv_ref, log_ref = qkv.get(), logs_in.get()
    slices = slot_rows_of(rows, slots)
    for pair in range(HEADS // 2):
        at = lanes(pair)
        queries, keys, values = [[qkv_ref[i, here, at] for here in slices] for i in range(3)]
        logs = [log_ref[:, 2 * pair + head : 2 * pair + head + 1] for head in range(2)]
        parts = pair_weights(queries, keys, bias, logs)
        grad_query, grads_k, grads_v = pair_backward(queries, keys, values, parts, [grad_mix_ref[here, at] for here in slices])
        grad_proj_ref[0, :, at] = grad_query
        grad_proj_ref[1, :, at] = jnp.concatenate(grads_k, axis=0)
        grad_proj_ref[2, :, at] = jnp.concatenate(grads_v, axis=0)
    x_ref, target_ref = x.get(), target.get()
    turned = replaced(target_ref, table_ref, x_ref).astype(BF16).T
    for i in range(3):
        put(halves_ref, core[0], 4 + i, nn(turned, grad_proj_ref[i]))
    copies += send_halves(halves_ref, kept_ref, sent_ref, sems.at[pl.ds(3, 2)], 4, 4)
    for i in range(3):
        grad = grad + nt(grad_proj_ref[i], block(weight_ref, i))
    marked = target_ref[...] == 1
    grad_x_ref[...] = jnp.where(marked, 0.0, grad)
    small_ref[0:1, :] = gain
    small_ref[1:2, :] = bias_row
    small_ref[2:3, :] = jnp.sum(jnp.where(marked, grad, 0.0), axis=0, keepdims=True)
    wait_all(copies)


def encoder_ffn_backward(
    core, place, lengths, route, pieces_ref, hidden_two_ref, table_ref, small_one_ref, small_two_ref,
    hidden_one, active, slope, mix, part_a, part_b, part_c, part_d,
    kept_ref, sent_ref, grad_first_ref, weight_ref, inner_ref, halves_ref, sems,
):
    rows, width = hidden_two_ref.shape
    groups, longest, _ = pieces_ref.shape
    weight_copies = bring_pieces(place, (part_a, part_b, part_c, part_d), weight_ref, sems)
    down = lax.broadcasted_iota(jnp.int32, (rows, longest), 0)
    across = lax.broadcasted_iota(jnp.int32, (rows, longest), 1)
    starts, counts = piece_places(lengths, route, lengths.shape[1])
    grad = jnp.zeros((rows, width), F32)
    for g in range(groups):
        chosen = (down - across == starts[g]) & (across < counts[g])
        grad = grad + nn(jnp.where(chosen, 1.0, 0.0).astype(BF16), pieces_ref[g])
    unit, scale = norm_parts(hidden_two_ref[...])
    grad, gain_two, bias_two = norm_back(grad, unit, scale, table_ref[2:3, :])
    grad_low = grad.astype(BF16)
    put_tall(halves_ref, core[0], 4, nn(active.get()[...].T, grad_low))
    wait_all(weight_copies)
    inner_ref[...] = (nt(grad_low, tall(weight_ref, 4)) * slope.get()[...].astype(F32)).astype(BF16)
    unit, scale = norm_parts(hidden_one.get()[...])
    low = (unit * table_ref[0:1, :] + table_ref[1:2, :]).astype(BF16)
    put_wide(halves_ref, core[0], 0, nn(low.T, inner_ref[...]))
    copies = send_halves(halves_ref, kept_ref, sent_ref, sems.at[pl.ds(32, 2)], 0, 8)
    grad = grad + nt(inner_ref[...], wide(weight_ref, 0, 4))
    grad, gain, bias_row = norm_back(grad, unit, scale, table_ref[0:1, :])
    grad_first_ref[...] = grad
    small_rows = [gain, bias_row, gain_two, bias_two, small_one_ref[0:2, :], small_two_ref[...], small_one_ref[2:3, :]]
    put_rows(halves_ref, 9, small_rows)
    put(halves_ref, core[0], 8, nn(mix.get()[...].T, grad.astype(BF16)))
    copies += send_halves(halves_ref, kept_ref, sent_ref, sems.at[pl.ds(34, 2)], 8, 2)
    wait_all(copies)


def encoder_attention_backward(
    core, place, lengths, grad_in_ref, qkv, logs_in, x,
    part_a, part_b, part_c, part_d,
    kept_ref, sent_ref, grad_x_ref, bias_ref, grad_mix_ref, grad_proj_ref, weight_ref, halves_ref, sems,
):
    rows, width = grad_in_ref.shape
    weight_copies = bring_pieces(place, (part_a, part_b, part_c, part_d), weight_ref, sems)
    bias_ref[...] = segment_bias(lengths, rows)
    grad = grad_in_ref[...]
    wait_all(weight_copies)
    grad_mix_ref[...] = nt(grad.astype(BF16), block(weight_ref, 3)).astype(BF16)
    qkv_ref, log_ref = qkv.get(), logs_in.get()
    for pair in range(HEADS // 2):
        at = lanes(pair)
        queries, keys, values = [[qkv_ref[i, :, at]] for i in range(3)]
        logs = [log_ref[:, 2 * pair + head : 2 * pair + head + 1] for head in range(2)]
        parts = pair_weights(queries, keys, bias_ref[...], logs)
        grad_query, grads_k, grads_v = pair_backward(queries, keys, values, parts, [grad_mix_ref[:, at]])
        grad_proj_ref[0, :, at] = grad_query
        grad_proj_ref[1, :, at] = grads_k[0]
        grad_proj_ref[2, :, at] = grads_v[0]
    turned = x.get()[...].T
    for i in range(3):
        put(halves_ref, core[0], i, nn(turned, grad_proj_ref[i]))
    copies = send_halves(halves_ref, kept_ref, sent_ref, sems.at[pl.ds(32, 2)])
    for i in range(3):
        grad = grad + nt(grad_proj_ref[i], block(weight_ref, i))
    grad_x_ref[...] = grad
    wait_all(copies)


def finish(counts, me, *refs):
    terms, outs = refs[: 4 * len(counts)], refs[4 * len(counts) :]
    for chain, count in enumerate(counts):
        total = terms[4 * chain][...].astype(F32)
        for ref in terms[4 * chain + 1 : 4 * chain + 4]:
            total = total + ref[...].astype(F32)
        width = total.shape[1]
        at = 0
        own = None
        for ref in outs[:count]:
            columns = ref.shape[-1]
            if columns < width and own is None:
                total = pltpu.roll(total[at:, :], width - me[0] * columns, axis=1)[:, :columns]
                own, at = True, 0
            if len(ref.shape) == 3:
                parts = [ref.at[i] for i in range(ref.shape[0])]
            else:
                parts = [ref.at[:, i * width : (i + 1) * width] for i in range(columns // width)] or [ref]
            for one in parts:
                rows = one.shape[0]
                one[...] = total[at : at + rows, :]
                at += rows
        outs = outs[count:]


VMEM = pl.BlockSpec(memory_space=pltpu.VMEM)
SMEM = pl.BlockSpec(memory_space=pltpu.SMEM)
ANY = pl.BlockSpec(memory_space=pl.ANY)


class Late:
    def __init__(self, ref, target, sem):
        self.ref, self.copy = target, pltpu.make_async_copy(ref, target, sem)
        self.copy.start()

    def get(self):
        self.copy.wait()
        return self.ref


class Early:
    def __init__(self, ref, target, sem):
        self.ref, self.copy = ref, pltpu.make_async_copy(ref, target, sem)

    def send(self):
        self.copy.start()


def run(
    kernel, scalars, arrays, outs, scratch=(), late=(), far=(), far_outs=(), early=(), sems=0, us=1.0, start=(), end=()
):
    moving = len(late) + len(early)
    kinds = [pltpu.VMEM(one.shape, one.dtype) for one in late]
    kinds += [pltpu.VMEM(shape, kind) for shape, kind in tuple(early) + tuple(scratch)]
    kinds += [pltpu.SemaphoreType.DMA((count,)) for count in (moving, sems) if count]

    def body(*refs):
        left = list(refs)

        def take(count):
            taken = left[:count]
            del left[:count]
            return taken

        given = take(len(scalars) + len(arrays))
        late_in, far_in, out, early_out = take(len(late)), take(len(far)), take(len(outs)), take(len(early))
        late_at, early_at, rest = take(len(late)), take(len(early)), take(len(scratch))
        own = left[0] if moving else None
        lates = [Late(ref, at, own.at[i]) for i, (ref, at) in enumerate(zip(late_in, late_at))]
        earlies = [Early(at, ref, own.at[len(late) + i]) for i, (ref, at) in enumerate(zip(early_out, early_at))]
        kernel(*given, *lates, *far_in, *out, *earlies, *rest, *left[1 if moving else 0 :])
        for one in earlies:
            one.copy.wait()

    given, sends = (tuple(scalars), tuple(arrays), tuple(late), tuple(far)), [one.sends for one in start]
    if start:
        given, sends = lax.optimization_barrier((given, sends))
    for one, ready in zip(start, sends):
        one.sends = ready
        one.start()
    results = pl.pallas_call(
        body,
        out_shape=[jax.ShapeDtypeStruct(shape, kind) for shape, kind in tuple(outs) + tuple(early)],
        in_specs=[SMEM] * len(scalars) + [VMEM] * len(arrays) + [ANY] * (len(late) + len(far)),
        out_specs=[ANY if index in far_outs or index >= len(outs) else VMEM for index in range(len(outs) + len(early))],
        scratch_shapes=kinds,
        compiler_params=pltpu.CompilerParams(vmem_limit_bytes=56 << 20),
        cost_estimate=pl.CostEstimate(flops=int(us * 1.15e9), bytes_accessed=1 << 20, transcendentals=0),
    )(*given[0], *given[1], *given[2], *given[3])
    if end:
        results, got = lax.optimization_barrier((results, [one.got for one in end]))
        for one, blocks in zip(end, got):
            one.got = blocks
            one.finish()
    return results


def exchange(block, pairs):
    return lax.ppermute(block, AXES, pairs)


def pick(blocks, place):
    return lax.dynamic_index_in_dim(blocks, place, 0, keepdims=False)


def added(one, other):
    return (one.astype(F32) + other.astype(F32)).astype(BF16)


RING = (0, 1, 3, 2)


def sum_scatter(packs, count):
    me = lax.axis_index(AXES)
    core, low, high = me % 2, (me // 2) % 2, (me // 4) % 2
    rest = count // 8
    by_core = [pack.reshape((rest * 4, 2) + pack.shape[1:]) for pack in packs]
    sent, kept = [
        jnp.concatenate([lax.dynamic_index_in_dim(pack, side, 1, keepdims=False) for pack in by_core], axis=1)
        for side in (1 - core, core)
    ]
    tail = sent.shape[1:]
    kept = added(kept, exchange(sent, [(i, i ^ 1) for i in range(count)]))
    quads = kept.reshape((rest, 4) + tail)

    def two(first, second):
        parts = [lax.dynamic_index_in_dim(quads, place, 1, keepdims=True) for place in (first, second)]
        return jnp.concatenate(parts, axis=1)

    other_high, other_low = 1 - high, 1 - low
    sent = two(
        jnp.where(core == 0, 2 * other_high, other_low),
        jnp.where(core == 0, 2 * other_high + 1, other_low + 2),
    )
    kept = two(jnp.where(core == 0, 2 * high, low), jnp.where(core == 0, 2 * high + 1, low + 2))
    kept = added(kept, exchange(sent, [(i, i ^ (2 if i % 2 else 4)) for i in range(count)]))
    mine = jnp.where(core == 0, low, high)
    sent = lax.dynamic_index_in_dim(kept, 1 - mine, 1, keepdims=False)
    kept = lax.dynamic_index_in_dim(kept, mine, 1, keepdims=False)
    kept = added(kept, exchange(sent, [(i, i ^ (4 if i % 2 else 2)) for i in range(count)]))
    stride = 8
    while rest > 4:
        bit = (me // stride) % 2
        halves = kept.reshape((rest // 2, 2) + tail)
        sent = lax.dynamic_index_in_dim(halves, 1 - bit, 1, keepdims=False)
        kept = lax.dynamic_index_in_dim(halves, bit, 1, keepdims=False)
        kept = added(kept, exchange(sent, [(i, i ^ stride) for i in range(count)]))
        rest, stride = rest // 2, stride * 2
    order = RING if rest == 4 else tuple(range(rest))
    place_of = jnp.asarray([order.index(z) for z in range(rest)], jnp.int32)
    ring = jnp.asarray(order, jnp.int32)
    here = place_of[me // stride]
    onward = [
        (i, order[(order.index(i // stride) + 1) % rest] * stride + i % stride) for i in range(count)
    ]
    moving = pick(kept, ring[(here - 1) % rest]) if rest > 1 else kept[0]
    for step in range(rest - 1):
        arrived = exchange(moving, onward)
        own = pick(kept, ring[(here - 2 - step) % rest])
        moving = arrived.astype(F32) + own.astype(F32)
        if step < rest - 2:
            moving = moving.astype(BF16)
    return moving.astype(F32)


OUT_FIRST = [(i, i ^ (2 if i % 2 else 4)) for i in range(32)]
OUT_SECOND = [(i, i ^ (4 if i % 2 else 2)) for i in range(32)]
CORES = [(i, i ^ 1) for i in range(32)]


def gather_places():
    table = np.zeros((32, 32), np.int32)
    for me in range(32):
        for number in range(32):
            core = (me ^ (number // 16)) % 2
            first, second, level = (number // 8) % 2, (number // 4) % 2, number % 4
            x, y = (first, second) if core == 0 else (second, first)
            table[me, number] = ((me - me % 2) ^ (level * 8) ^ (x * 4) ^ (y * 2)) + core
    return table


def gather_blocks(mine):
    levels = [exchange(mine, [(i, i ^ (8 * k)) for i in range(32)]) for k in (1, 2, 3)]
    near = jnp.stack([mine] + levels)
    near = jnp.concatenate([near, exchange(near, OUT_SECOND)])
    far = exchange(near, OUT_FIRST)
    return near, far, exchange(near, CORES), exchange(far, CORES)


def together(*steps):
    arrived = lax.optimization_barrier([step.got for step in steps])
    for step, blocks in zip(steps, arrived):
        step.got = blocks


class Scatter:
    def __init__(self, kept, sent):
        me = lax.axis_index(AXES)
        core, low, high = me % 2, (me // 2) % 2, (me // 4) % 2
        self.bits = (jnp.where(core == 0, high, low), jnp.where(core == 0, low, high))
        self.level = me // 8
        self.kept, self.sends, self.stage = kept, [sent], 0

    def start(self):
        pairs = ([CORES], [OUT_FIRST], [OUT_SECOND], [[(i, i ^ (8 * k)) for i in range(32)] for k in (1, 2, 3)])
        self.got = [exchange(block, to) for block, to in zip(self.sends, pairs[self.stage])]
        return self.got

    def finish(self):
        if self.stage == 3:
            self.sends = []
            return self.sends
        got, size = self.got[0], self.kept.shape[0]

        def summed(place, count):
            return added(
                lax.dynamic_slice_in_dim(self.kept, place, count, 0), lax.dynamic_slice_in_dim(got, place, count, 0)
            )

        if self.stage < 2:
            half = size // 2
            bit = self.bits[self.stage]
            kept, sends = summed(bit * half, half), [summed((1 - bit) * half, half)]
        else:
            kept = summed(self.level, 1)[0]
            sends = [summed(jnp.bitwise_xor(self.level, k), 1)[0] for k in (1, 2, 3)]
        self.kept, self.sends, self.stage = kept, sends, self.stage + 1
        return self.sends


def on_device(
    enc_input,
    dec_input,
    target_mask,
    src_lengths,
    tgt_lengths,
    memory_route,
    enc_qkv,
    enc_out,
    enc_ffn_in,
    enc_ffn_out,
    enc_norms,
    dec_qkv,
    dec_out,
    cross_qkv,
    cross_out,
    dec_ffn_in,
    dec_ffn_out,
    dec_norms,
    mask_vector,
    out_cotangent,
):
    dp_count, groups = lax.axis_size("dp"), lax.axis_size("fsdp")
    count = dp_count * groups
    rows, width = enc_input.shape
    slots = src_lengths.shape[1]
    longest = rows // 2
    slot_rows = rows // slots
    part = enc_out.shape[0]
    inner = enc_ffn_in.shape[1]
    pieces_in = inner // width

    direct = count == 32 and part == 16
    kernel_part = width // 32
    joined = kernel_part // part
    me = lax.axis_index(AXES)
    my_dp, my_group = lax.axis_index("dp"), lax.axis_index("fsdp")

    def split(pack, squares):
        first = pack[:, : squares * part].reshape(32, joined, squares, part, width).transpose(0, 2, 1, 3, 4)
        return jnp.concatenate([first.reshape(32, -1, width), pack[:, squares * part :].reshape(32, -1, width)], axis=1)

    def unsplit(kept, sent, squares, used):
        kept = kept.reshape((2, 2, 4) + kept.shape[1:]).transpose(2, 0, 1, 3, 4)
        sent = sent.reshape((2, 2, 4) + sent.shape[1:]).transpose(2, 1, 0, 3, 4)
        pack = jnp.stack([kept, sent], axis=3).reshape(32, -1, width)
        first = pack[:, : squares * kernel_part].reshape(32, squares, joined, part, width).transpose(0, 2, 1, 3, 4)
        rest = pack[:, squares * kernel_part : used * kernel_part].reshape(count, -1, width)
        return jnp.concatenate([first.reshape(count, -1, width), rest], axis=1)

    if direct:
        core = (me % 2).reshape(1)
        attention_pack, ffn_pack, decoder_pack = run(
            pack_weights,
            (me.reshape(1),),
            (
                src_lengths, memory_route, mask_vector.reshape(1, part),
                enc_qkv, enc_out, enc_ffn_in, enc_ffn_out, enc_norms,
                dec_qkv, dec_out, cross_qkv, cross_out, dec_ffn_in, dec_ffn_out, dec_norms,
            ),
            (((5 * part, width), BF16), ((8 * part, width), BF16), ((16 * part, width), BF16)),
            us=2.0,
        )
        dec_all = lax.all_gather(decoder_pack, AXES, axis=0, tiled=False)
        attention_blocks = gather_blocks(attention_pack)
        ffn_blocks = gather_blocks(ffn_pack)
        place = jnp.asarray(gather_places())[me]
    else:
        core = jnp.zeros((1,), jnp.int32)

        def square(weight):
            return weight.reshape(-1, width)

        def wide(weight):
            return weight.reshape(part, pieces_in, width).transpose(1, 0, 2).reshape(-1, width)

        def whole(norms):
            return lax.all_gather(norms, AXES, axis=norms.ndim - 1, tiled=True).reshape(-1, width)

        def gathered(weights):
            return lax.all_gather(jnp.concatenate(weights), AXES, axis=0, tiled=False)

        rows_of = [whole(enc_norms), whole(dec_norms), whole(mask_vector)]
        first_rows = jnp.pad(jnp.concatenate(rows_of), ((0, kernel_part - 11), (0, 0)))
        small_blocks = jnp.concatenate([first_rows[None], jnp.zeros((31, kernel_part, width), BF16)])
        attention_all = split(gathered([square(enc_qkv), enc_out]), 4)
        attention_all = jnp.concatenate([attention_all, small_blocks], axis=1)
        attention_blocks = tuple(attention_all[i * 8 : i * 8 + 8] for i in range(4))
        ffn_all = split(gathered([wide(enc_ffn_in), enc_ffn_out]), pieces_in)
        ffn_blocks = tuple(ffn_all[i * 8 : i * 8 + 8] for i in range(4))
        decoder = [square(dec_qkv), dec_out, square(cross_qkv), cross_out, wide(dec_ffn_in), dec_ffn_out]
        dec_all = split(gathered(decoder), 8 + pieces_in)
        place = jnp.arange(32, dtype=jnp.int32)

    def some(*chains):
        return chains if direct else ()

    plane, three = (rows, width), (3, rows, width)
    memory_shape = (groups, longest, width)
    logs_shape = (rows, HEADS)
    parts_shape = (HEADS, rows, longest)

    def half_of(pieces):
        return ((16, pieces * kernel_part, width), BF16)

    def halves_of(pieces):
        return ((2, 16, pieces * kernel_part, width), BF16)

    def weights_of(pieces):
        return ((32, pieces * kernel_part, width), BF16)

    half_ffn = ((rows, inner), BF16)
    e_mix, e_logs, e_hidden_one, table, e_qkv = run(
        encoder_attention,
        (place, src_lengths),
        (enc_input,),
        ((plane, BF16), (logs_shape, F32), (plane, F32), ((kernel_part, width), F32)),
        (((rows, rows), F32), weights_of(5)),
        far=attention_blocks,
        early=((three, BF16),),
        sems=32,
        us=9.5,
    )
    pieces, e_active, e_slope, e_hidden_two = run(
        encoder_ffn,
        (place, src_lengths, memory_route),
        (e_hidden_one, table),
        ((memory_shape, BF16),),
        (weights_of(2 * pieces_in),),
        far=ffn_blocks,
        early=(half_ffn, half_ffn, (plane, F32)),
        sems=32,
        us=9.0,
    )
    memory_in = lax.all_to_all(pieces, "fsdp", split_axis=0, concat_axis=0, tiled=True)
    d_mix, d_logs, d_hidden, target, d_qkv = run(
        self_forward,
        (tgt_lengths,),
        (dec_input, target_mask[:, None], table),
        ((plane, BF16), (logs_shape, F32), (plane, F32), ((rows, 1), jnp.int32)),
        (weights_of(4),),
        far=(dec_all,),
        early=((three, BF16),),
        sems=1,
        us=6.4,
    )
    if direct:
        ints = table[11].reshape(dp_count, groups, part)
        ints = lax.dynamic_index_in_dim(ints, my_dp, 0, keepdims=False).astype(jnp.int32)
        lengths_near, route_near = ints[:, :slots], ints[:, slots : 2 * slots]
    else:
        lengths_near = lax.all_gather(src_lengths[0], "fsdp")
        route_near = lax.all_gather(memory_route[0], "fsdp")
    ids = jnp.arange(groups, dtype=jnp.int32)
    wanted = my_group * slots + jnp.arange(slots, dtype=jnp.int32)
    chosen = route_near[None] == wanted[:, None, None]
    slot_source = jnp.sum(jnp.where(chosen, ids[None, :, None], 0), axis=(1, 2))
    slot_length = jnp.sum(jnp.where(chosen, lengths_near[None], 0), axis=(1, 2))

    dec_output, *dffn_halves, grad_second, small_two, parts, q_rows, kv_rows, c_mix = run(
        decoder_upper,
        (core, slot_source, slot_length),
        (d_hidden, memory_in, table),
        ((plane, BF16), half_of(8), half_of(8), (plane, F32), ((4, width), F32)),
        (((rows, inner), F32), half_ffn, half_ffn, weights_of(4), weights_of(8), halves_of(8)),
        late=(out_cotangent,),
        far=(dec_all,),
        far_outs=(1, 2),
        early=((parts_shape, F32), (plane, BF16), ((2,) + memory_shape, BF16), (plane, BF16)),
        sems=4,
        us=19.0,
    )

    def begin(halves):
        return Scatter(*halves) if direct else None

    dffn = begin(dffn_halves)
    grad_memory, grad_q, grad_kv = run(
        cross_backward,
        (slot_source,),
        (grad_second,),
        ((memory_shape, BF16), (plane, BF16), ((2,) + memory_shape, BF16)),
        ((plane, BF16), weights_of(4)),
        late=(q_rows, kv_rows, parts),
        far=(dec_all,),
        sems=1,
        us=10.0,
        start=some(dffn),
        end=some(dffn),
    )
    returned = lax.all_to_all(grad_memory, "fsdp", split_axis=0, concat_axis=0, tiled=True)
    *middle_halves, dec_input_grad, small_one = run(
        decoder_lower,
        (core, tgt_lengths),
        (table, grad_second, grad_q, d_hidden),
        (half_of(8), half_of(8), (plane, F32), ((3, width), F32)),
        ((plane, BF16), (three, BF16), weights_of(5), halves_of(8)),
        late=(c_mix, memory_in, grad_kv, d_mix, d_qkv, d_logs, dec_input, target),
        far=(dec_all,),
        far_outs=(0, 1),
        sems=5,
        us=16.0,
        start=some(dffn),
        end=some(dffn),
    )
    returned, middle_halves = lax.optimization_barrier((returned, middle_halves))
    middle = begin(middle_halves)
    if direct:
        middle.start()
        middle.finish()
    *effn_halves, grad_enc = run(
        encoder_ffn_backward,
        (core, place, src_lengths, memory_route),
        (returned, e_hidden_two, table, small_one, small_two),
        (half_of(10), half_of(10), (plane, F32)),
        (weights_of(8), half_ffn, halves_of(10)),
        late=(e_hidden_one, e_active, e_slope, e_mix),
        far=ffn_blocks,
        far_outs=(0, 1),
        sems=36,
        us=12.0,
        start=some(dffn, middle),
        end=some(dffn, middle),
    )
    effn = begin(effn_halves)
    if direct:
        effn.start()
        effn.finish()
    *eatt_halves, enc_input_grad = run(
        encoder_attention_backward,
        (core, place, src_lengths),
        (grad_enc,),
        (half_of(3), half_of(3), (plane, F32)),
        (((rows, rows), F32), (plane, BF16), (three, BF16), weights_of(5), halves_of(3)),
        late=(e_qkv, e_logs, enc_input),
        far=attention_blocks,
        far_outs=(0, 1),
        sems=34,
        us=12.0,
        start=some(dffn, middle, effn),
        end=some(dffn, middle),
    )
    eatt = begin(eatt_halves)

    def ends(*given, start=(), end=()):
        chains = [one for one in given if isinstance(one, Scatter)]
        shapes, counts = [], []
        for one in given:
            if isinstance(one, Scatter):
                counts.append(0)
            else:
                counts[-1] += 1
                shapes.append((one, F32))
        terms = [term for chain in chains for term in (chain.kept, *chain.got)]
        return run(partial(finish, tuple(counts)), (me.reshape(1),), terms, shapes, us=2.5, start=start, end=end)

    cube, square_part, wide_part, tall_part = (3, part, width), (part, width), (part, inner), (inner // count, width)
    if direct:
        middle.start()
        eatt.start()
        together(eatt, effn)
        for one in (eatt, effn):
            one.finish()
            one.start()
        together(eatt, effn)
        for one in (eatt, effn):
            one.finish()
        decoder_grads = ends(
            dffn, wide_part, tall_part, middle, cube, square_part, cube, square_part, start=(effn, eatt), end=(eatt,)
        )
        dec_ffn_grads, middle_grads = decoder_grads[:2], decoder_grads[2:]
        norm_shapes = ((2, 2, part), (3, 2, part), (1, part))
        encoder_grads = ends(effn, wide_part, tall_part, square_part, *norm_shapes, start=(eatt,))
        enc_ffn_grads, small_grads = encoder_grads[:3], list(encoder_grads[3:])
        small_grads[2] = small_grads[2].reshape(part)
        (qkv_grads,) = ends(eatt, cube)
    else:

        def piece(summed, first, pieces=1):
            return summed[first * part : (first + pieces) * part]

        def wide_piece(summed):
            picked = piece(summed, 0, pieces_in).reshape(pieces_in, part, width)
            return picked.transpose(1, 0, 2).reshape(part, inner)

        effn_pack = unsplit(*[half[:, : 8 * kernel_part] for half in effn_halves], 4, 8)
        eout_pack = unsplit(*[half[:, 8 * kernel_part : 9 * kernel_part] for half in effn_halves], 1, 1)
        packs = [
            unsplit(*dffn_halves, 4, 8),
            unsplit(*middle_halves, 8, 8),
            jnp.concatenate([effn_pack, eout_pack], axis=1),
            unsplit(*eatt_halves, 3, 3),
        ]
        dffn_sum, middle_sum, effn_sum, eatt_sum = [sum_scatter([pack], count) for pack in packs]
        dec_ffn_grads = (wide_piece(dffn_sum), piece(dffn_sum, pieces_in, pieces_in))
        enc_ffn_grads = (wide_piece(effn_sum), piece(effn_sum, pieces_in, pieces_in), piece(effn_sum, 8))
        middle_grads = [
            piece(middle_sum, 0, 3).reshape(cube), piece(middle_sum, 3), piece(middle_sum, 4, 3).reshape(cube), piece(middle_sum, 7)
        ]
        qkv_grads = piece(eatt_sum, 0, 3).reshape(cube)
        small_sum = lax.psum(effn_halves[0][0, 9 * kernel_part :].astype(F32), AXES)
        small_sum = lax.dynamic_slice_in_dim(small_sum[:11], me * part, part, 1)
        small_grads = small_sum[:4].reshape(2, 2, part), small_sum[4:10].reshape(3, 2, part), small_sum[10]

    return (
        dec_output,
        enc_input_grad,
        dec_input_grad,
        qkv_grads,
        enc_ffn_grads[2],
        *enc_ffn_grads[:2],
        small_grads[0],
        *middle_grads[2:],
        *middle_grads[:2],
        *dec_ffn_grads,
        small_grads[1],
        small_grads[2],
    )


def solution(mesh):
    rows = P(AXES, None)
    flat = P(AXES)
    cube = P(None, AXES, None)
    norm = P(None, None, AXES)
    in_specs = (
        (rows, rows, flat, rows, rows, rows)
        + (cube, rows, rows, rows, norm)
        + (cube, rows, cube, rows, rows, rows, norm, flat)
        + (rows,)
    )
    out_specs = (
        (rows, rows, rows)
        + (cube, rows, rows, rows, norm)
        + (cube, rows, cube, rows, rows, rows, norm, flat)
    )
    return jax.shard_map(on_device, mesh=mesh, in_specs=in_specs, out_specs=out_specs, check_vma=False)
```

```python
import math
from functools import partial

import jax
import jax.numpy as jnp
import numpy as np
from jax import lax
from jax.experimental import pallas as pl
from jax.experimental.pallas import tpu as pltpu
from jax.sharding import PartitionSpec as P

HEADS = 8
HEAD_DIM = 64
SCALE = 1.0 / math.sqrt(HEAD_DIM)
AXES = ("dp", "fsdp")
F32 = jnp.float32
BF16 = jnp.bfloat16


MASKED = -1e30
GELU_C = math.sqrt(2.0 / math.pi)
GELU_A = 0.044715


def nn(left, right):
    return jnp.dot(left, right, preferred_element_type=F32)


def nt(left, right):
    return lax.dot_general(left, right, (((1,), (1,)), ((), ())), preferred_element_type=F32)


def norm_parts(hidden):
    center = hidden - jnp.mean(hidden, axis=-1, keepdims=True)
    scale = lax.rsqrt(jnp.mean(center * center, axis=-1, keepdims=True) + 1e-05)
    return center * scale, scale


def norm_back(grad, unit, scale, gain):
    inner = grad * gain
    mean_one = jnp.mean(inner, axis=-1, keepdims=True)
    mean_two = jnp.mean(inner * unit, axis=-1, keepdims=True)
    return (
        scale * (inner - mean_one - unit * mean_two),
        jnp.sum(grad * unit, axis=0, keepdims=True),
        jnp.sum(grad, axis=0, keepdims=True),
    )


def gelu_tanh(pre):
    return jnp.tanh(GELU_C * (pre + GELU_A * (pre * pre * pre)))


def gelu_back(pre):
    tanh = gelu_tanh(pre)
    slope = GELU_C * (1.0 + 3.0 * GELU_A * (pre * pre))
    return 0.5 * pre * (1.0 + tanh), 0.5 * (1.0 + tanh) + 0.5 * pre * (1.0 - tanh * tanh) * slope


def block(ref, first):
    width = ref.shape[2]
    part = width // ref.shape[0]
    return ref[:, first * part : (first + 1) * part, :].reshape(width, width)


def wide(ref, first, count):
    return jnp.concatenate([block(ref, first + index) for index in range(count)], axis=1)


def tall(ref, first):
    count, _, width = ref.shape
    part = width // count
    return ref[:, first * part : (first + 4) * part, :].reshape(4 * width, width)


CORNERS = [(x, y, side) for x in range(2) for y in range(2) for side in range(2)]


def place_of(x, y, side):
    return 8 * x + 4 * y if side == 0 else 8 * y + 4 * x


def put(ref, core, first, grad):
    width = grad.shape[1]
    part = width // 32
    cut = grad.astype(BF16).reshape(4, 2, 2, 2, part, width)
    rows = slice(first * part, (first + 1) * part)
    for x, y, side in CORNERS:
        half = core if side == 0 else 1 - core
        place = place_of(x, y, side)
        ref[half, place : place + 4, rows, :] = cut[:, x, y, side]


def put_wide(ref, core, first, grad):
    width = ref.shape[3]
    for index in range(grad.shape[1] // width):
        put(ref, core, first + index, grad[:, index * width : (index + 1) * width])


def put_tall(ref, core, first, grad):
    width = grad.shape[1]
    part = width // 32
    rows = slice(first * part, (first + 4) * part)
    cut = grad.astype(BF16).reshape(4, 2, 2, 2, 4 * part, width)
    for x, y, side in CORNERS:
        half = core if side == 0 else 1 - core
        place = place_of(x, y, side)
        ref[half, place : place + 4, rows, :] = cut[:, x, y, side]


def put_rows(ref, first, rows_of):
    halves, count, _, width = ref.shape
    part = width // (halves * count)
    used = sum(row.shape[0] for row in rows_of)
    rows = jnp.concatenate(rows_of + [jnp.zeros((part - used, width), F32)], axis=0)
    ref[:, :, first * part : (first + 1) * part, :] = jnp.broadcast_to(
        rows.astype(BF16)[None, None], (halves, count, part, width)
    )


def bring_pieces(place, refs, target, sems, first=0):
    part = target.shape[2] // target.shape[0]
    rows = pl.ds(first * part, target.shape[1])
    copies = []
    for array, ref in enumerate(refs):
        for index in range(8):
            number = array * 8 + index
            copies.append(pltpu.make_async_copy(ref.at[index, rows], target.at[place[number]], sems.at[number]))
    for copy in copies:
        copy.start()
    return copies


def bring_rows(ref, first, count, target, sem):
    copy = pltpu.make_async_copy(ref.at[:, pl.ds(first, count), :], target, sem)
    copy.start()
    return copy


def send_halves(halves_ref, kept_ref, sent_ref, sems, first=0, count=None):
    part = halves_ref.shape[3] // 32
    rows = pl.ds(first * part, halves_ref.shape[2] if count is None else count * part)
    copies = [
        pltpu.make_async_copy(halves_ref.at[half, :, rows], ref.at[:, rows], sems.at[half])
        for half, ref in enumerate((kept_ref, sent_ref))
    ]
    for copy in copies:
        copy.start()
    return copies


def wait_all(copies):
    for copy in copies:
        copy.wait()


PAIR = 2 * HEAD_DIM


def twice(pair_rows):
    lane = lax.broadcasted_iota(jnp.int32, pair_rows.shape, 1)
    zero = jnp.zeros_like(pair_rows)
    return jnp.concatenate(
        [jnp.where(lane < HEAD_DIM, pair_rows, zero), jnp.where(lane < HEAD_DIM, zero, pair_rows)], axis=0
    )


def each_head(scores, count):
    return [scores[:, head * count : (head + 1) * count] for head in range(2)]


def pair_scores(queries, keys):
    return jnp.concatenate([nt(q, twice(k)) for q, k in zip(queries, keys)], axis=0)


def pair_forward(queries, keys, values, bias):
    count = keys[0][0].shape[0]
    scores = [pair_scores(q, k) for q, k in zip(queries, keys)]
    masked = [part + bias for both in scores for part in each_head(both, count)]
    tops = [jnp.max(part, axis=-1, keepdims=True) for part in masked]
    raised = [jnp.exp(part - top) for part, top in zip(masked, tops)]
    totals = [jnp.sum(part, axis=-1, keepdims=True) for part in raised]
    parts = [part * (1.0 / total) for part, total in zip(raised, totals)]
    logs = [top + jnp.log(total) for top, total in zip(tops, totals)]
    mixtures = []
    for pair, blocks in enumerate(values):
        low = jnp.concatenate([part.astype(BF16) for part in parts[2 * pair : 2 * pair + 2]], axis=1)
        rows = low.shape[0] // len(blocks)
        mixed = [nn(low[i * rows : (i + 1) * rows], twice(v)) for i, v in enumerate(blocks)]
        mixtures.append(jnp.concatenate(mixed, axis=0))
    return mixtures, parts, logs


def pair_weights(queries, keys, bias, logs):
    scores = each_head(pair_scores(queries, keys), keys[0].shape[0])
    return [jnp.exp(part + bias - log) for part, log in zip(scores, logs)]


def turned_products(rows_of, weights, count):
    rows = weights.shape[0] // len(rows_of)
    results = []
    for index, block_rows in enumerate(rows_of):
        both = nn(block_rows.T, weights[index * rows : (index + 1) * rows])
        own = jnp.concatenate([both[:HEAD_DIM, :count], both[HEAD_DIM:, count:]], axis=0)
        results.append(own.astype(BF16).T)
    return results


def pair_backward(queries, keys, values, parts, grads_out):
    count = keys[0].shape[0]
    grad_parts = each_head(pair_scores(grads_out, values), count)
    grad_scores = []
    for part, grad_part in zip(parts, grad_parts):
        delta = jnp.sum(part * grad_part, axis=-1, keepdims=True)
        grad_scores.append((part * (grad_part - delta)).astype(BF16))
    grad_scores = jnp.concatenate(grad_scores, axis=1)
    weights = jnp.concatenate([part.astype(BF16) for part in parts], axis=1)
    rows = grad_scores.shape[0] // len(keys)
    grad_query = [nn(grad_scores[i * rows : (i + 1) * rows], twice(k)) for i, k in enumerate(keys)]
    return (
        (jnp.concatenate(grad_query, axis=0) * SCALE).astype(BF16),
        turned_products(queries, grad_scores, count),
        turned_products(grads_out, weights, count),
    )


def sentence_starts(lengths):
    starts = [0]
    for sentence in range(lengths.shape[1] - 1):
        starts.append(starts[-1] + lengths[0, sentence])
    return starts


def longest_start(lengths, rows):
    starts = sentence_starts(lengths)
    place = jnp.int32(0)
    for sentence, start in enumerate(starts):
        place = place + jnp.where(lengths[0, sentence] == rows // 2, start, 0)
    return place


def turned_starts(lengths, rows):
    shift = longest_start(lengths, rows)
    places = [start - shift for start in sentence_starts(lengths)]
    return [jnp.where(place < 0, place + rows, place) for place in places]


def piece_places(lengths, route, slots, rows):
    starts = turned_starts(lengths, rows)
    first, length = [], []
    for device in range(route.shape[1]):
        here, count = jnp.int32(0), jnp.int32(0)
        for sentence in range(route.shape[1]):
            goes = route[0, sentence] // slots == device
            here = here + jnp.where(goes, starts[sentence], 0)
            count = count + jnp.where(goes, lengths[0, sentence], 0)
        first.append(here)
        length.append(count)
    return first, length


def segment_bias(lengths, rows):
    half = rows // 2
    down = lax.broadcasted_iota(jnp.int32, (half, 1), 0) + half
    across = lax.broadcasted_iota(jnp.int32, (1, half), 1) + half
    segment_down = jnp.zeros_like(down)
    segment_across = jnp.zeros_like(across)
    for start in turned_starts(lengths, rows):
        segment_down += (down >= start).astype(jnp.int32)
        segment_across += (across >= start).astype(jnp.int32)
    second = jnp.where(segment_down == segment_across, 0.0, MASKED)
    return jnp.concatenate([jnp.zeros((half, half), F32), second], axis=0)


def halves_of_rows(rows):
    return [slice(0, rows // 2), slice(rows // 2, rows)]


def lanes(pair):
    return slice(pair * PAIR, (pair + 1) * PAIR)


def pack_weights(
    me, src_ref, route_ref, mask_ref, e_qkv_ref, e_out_ref, e_in_ref, e_outff_ref, e_norm_ref,
    d_qkv_ref, d_out_ref, c_qkv_ref, c_out_ref, d_in_ref, d_outff_ref, d_norm_ref,
    attention_ref, ffn_ref, decoder_ref,
):
    part, width = e_out_ref.shape
    lane = lax.broadcasted_iota(jnp.int32, (part, width), 1)
    row = lax.broadcasted_iota(jnp.int32, (part, width), 0)
    spread = jnp.where(lane - row == me[0] * part, 1.0, 0.0).astype(BF16)
    ints = [nn(ref[...].astype(F32).astype(BF16), spread[4 * i : 4 * i + 4]) for i, ref in enumerate((src_ref, route_ref))]
    rows = [nn(e_norm_ref[i], spread) for i in range(2)] + [nn(d_norm_ref[i], spread) for i in range(3)]
    rows = rows + [nn(mask_ref[...], spread), ints[0] + ints[1]]
    used = sum(r.shape[0] for r in rows)
    rows = jnp.concatenate(rows + [jnp.zeros((part - used, width), F32)], axis=0)

    def fill(ref, first, weight):
        ref[first * part : first * part + weight.shape[0], :] = weight

    for i in range(3):
        fill(attention_ref, i, e_qkv_ref[i])
        fill(decoder_ref, i, d_qkv_ref[i])
        fill(decoder_ref, 4 + i, c_qkv_ref[i])
    fill(attention_ref, 3, e_out_ref[...])
    fill(attention_ref, 4, rows.astype(BF16))
    fill(decoder_ref, 3, d_out_ref[...])
    fill(decoder_ref, 7, c_out_ref[...])
    for j in range(4):
        fill(ffn_ref, j, e_in_ref[:, j * width : (j + 1) * width])
        fill(decoder_ref, 8 + j, d_in_ref[:, j * width : (j + 1) * width])
    fill(ffn_ref, 4, e_outff_ref[...])
    fill(decoder_ref, 12, d_outff_ref[...])


def put_logs(log_ref, pairs, logs):
    for index, log in enumerate(logs):
        head = 2 * pairs[0] + index
        log_ref[:, head : head + 1] = log


def encoder_attention(
    place, lengths, x_ref, part_a, part_b, part_c, part_d,
    mix_ref, log_ref, hidden_ref, table_ref, qkv, x_turned, bias_ref, weight_ref, sems,
):
    rows, width = x_ref.shape
    copies = bring_pieces(place, (part_a, part_b, part_c, part_d), weight_ref, sems)
    turned = pltpu.roll(x_ref[...].astype(F32), rows - longest_start(lengths, rows), axis=0)
    rows_in = turned.astype(BF16)
    x_turned.ref[...] = rows_in
    x_turned.send()
    bias_ref[...] = segment_bias(lengths, rows)
    wait_all(copies)
    part = width // weight_ref.shape[0]
    table_ref[...] = jnp.sum(weight_ref[:, 4 * part : 5 * part, :].astype(F32), axis=0)
    qkv_ref = qkv.ref
    qkv_ref[0] = (nn(rows_in, block(weight_ref, 0)) * SCALE).astype(BF16)
    qkv_ref[1] = nn(rows_in, block(weight_ref, 1)).astype(BF16)
    qkv_ref[2] = nn(rows_in, block(weight_ref, 2)).astype(BF16)
    qkv.send()
    halves = halves_of_rows(rows)
    for first in range(0, HEADS // 2, 2):
        pairs = (first, first + 1)
        mixtures, _, logs = pair_forward(
            *[[[qkv_ref[i, half, lanes(pair)] for half in halves] for pair in pairs] for i in range(3)], bias_ref[...]
        )
        for pair, mixture in zip(pairs, mixtures):
            mix_ref[:, lanes(pair)] = mixture.astype(BF16)
        put_logs(log_ref, pairs, logs)
    hidden_ref[...] = turned + nn(mix_ref[...], block(weight_ref, 3))


def encoder_ffn(
    place, lengths, route, hidden_one_ref, table_ref, part_a, part_b, part_c, part_d,
    pieces_ref, active, slope, hidden_two, weight_ref, sems,
):
    rows, width = hidden_one_ref.shape
    groups, longest, _ = pieces_ref.shape
    copies = bring_pieces(place, (part_a, part_b, part_c, part_d), weight_ref, sems)
    unit, _ = norm_parts(hidden_one_ref[...])
    first = unit * table_ref[0:1, :] + table_ref[1:2, :]
    low = first.astype(BF16)
    wait_all(copies)
    for j in range(4):
        value, slope_value = gelu_back(nn(low, block(weight_ref, j)))
        active.ref[:, j * width : (j + 1) * width] = value.astype(BF16)
        slope.ref[:, j * width : (j + 1) * width] = slope_value.astype(BF16)
    active.send()
    slope.send()
    hidden = first + nn(active.ref[...], tall(weight_ref, 4))
    hidden_two.ref[...] = hidden
    hidden_two.send()
    unit, _ = norm_parts(hidden)
    memory = (unit * table_ref[2:3, :] + table_ref[3:4, :]).astype(BF16)
    down = lax.broadcasted_iota(jnp.int32, (longest, rows), 0)
    across = lax.broadcasted_iota(jnp.int32, (longest, rows), 1)
    starts, _ = piece_places(lengths, route, lengths.shape[1], rows)
    for g in range(groups):
        chosen = jnp.where(across - down == starts[g], 1.0, 0.0).astype(BF16)
        pieces_ref[g] = nn(chosen, memory).astype(BF16)


def replaced(target_ref, table_ref, rows_ref):
    marked = target_ref[...] == 1
    return jnp.where(marked, table_ref[10:11, :], rows_ref[...].astype(F32))


def slot_bias(length, count):
    across = lax.broadcasted_iota(jnp.int32, (1, count), 1)
    return jnp.where(across < length, 0.0, MASKED)


def slot_biases(lengths, count, rows):
    return jnp.concatenate(
        [jnp.broadcast_to(slot_bias(length, count), (rows, count)) for length in lengths], axis=0
    )


def slot_rows_of(rows, slots):
    return [slice(slot * (rows // slots), (slot + 1) * (rows // slots)) for slot in range(slots)]


def self_forward(
    lengths, x_ref, target_ref, table_ref, gathered_ref,
    mix_ref, log_ref, hidden_ref, target_out_ref, qkv, weight_ref, sems,
):
    rows, width = x_ref.shape
    slots = lengths.shape[1]
    target_out_ref[...] = target_ref[...]
    copies = [bring_rows(gathered_ref, 0, weight_ref.shape[1], weight_ref, sems.at[0])]
    start = replaced(target_ref, table_ref, x_ref)
    low = start.astype(BF16)
    bias = slot_biases([lengths[0, slot] for slot in range(slots)], rows // slots, rows // slots)
    wait_all(copies)
    qkv_ref = qkv.ref
    qkv_ref[0] = (nn(low, block(weight_ref, 0)) * SCALE).astype(BF16)
    qkv_ref[1] = nn(low, block(weight_ref, 1)).astype(BF16)
    qkv_ref[2] = nn(low, block(weight_ref, 2)).astype(BF16)
    qkv.send()
    for first in range(0, HEADS // 2, 2):
        pairs = (first, first + 1)
        mixtures, _, logs = pair_forward(
            *[[[qkv_ref[i, here, lanes(pair)] for here in slot_rows_of(rows, slots)] for pair in pairs] for i in range(3)], bias
        )
        for pair, mixture in zip(pairs, mixtures):
            mix_ref[:, lanes(pair)] = mixture.astype(BF16)
        put_logs(log_ref, pairs, logs)
    hidden_ref[...] = start + nn(mix_ref[...], block(weight_ref, 3))


def decoder_upper(
    core, slot_source, slot_length, hidden_ref, memory_ref, table_ref, cotangent, gathered_ref,
    output_ref, kept_ref, sent_ref, grad_ref, small_ref, parts, q, kv, mix,
    slope_ref, active_ref, inner_ref, weight_ref, ffn_ref, halves_ref, sems,
):
    rows, width = hidden_ref.shape
    slots = slot_source.shape[0]
    groups, longest, _ = memory_ref.shape
    part_rows = weight_ref.shape[1]
    cross_copy = bring_rows(gathered_ref, part_rows, part_rows, weight_ref, sems.at[0])
    ffn_copy = bring_rows(gathered_ref, 2 * part_rows, 2 * part_rows, ffn_ref, sems.at[1])
    unit, _ = norm_parts(hidden_ref[...])
    first = unit * table_ref[4:5, :] + table_ref[5:6, :]
    first_low = first.astype(BF16)
    memory = memory_ref[...].reshape(groups * longest, width)
    cross_copy.wait()
    q.ref[...] = (nn(first_low, block(weight_ref, 0)) * SCALE).astype(BF16)
    for i in range(2):
        kv.ref[i] = nn(memory, block(weight_ref, 1 + i)).astype(BF16).reshape(groups, longest, width)
    q.send()
    kv.send()
    bias = slot_biases([slot_length[slot] for slot in range(slots)], longest, rows // slots)
    sources = [slot_source[slot] for slot in range(slots)]
    for start in range(0, HEADS // 2, 2):
        pairs = (start, start + 1)
        mixtures, weights, _ = pair_forward(
            [[q.ref[here, lanes(pair)] for here in slot_rows_of(rows, slots)] for pair in pairs],
            [[kv.ref[0, source, :, lanes(pair)] for source in sources] for pair in pairs],
            [[kv.ref[1, source, :, lanes(pair)] for source in sources] for pair in pairs],
            bias,
        )
        for index, pair in enumerate(pairs):
            mix.ref[:, lanes(pair)] = mixtures[index].astype(BF16)
            for head in range(2):
                parts.ref[2 * pair + head] = weights[2 * index + head]
    parts.send()
    mix.send()
    hidden = first + nn(mix.ref[...], block(weight_ref, 3))
    unit_two, scale_two = norm_parts(hidden)
    second = unit_two * table_ref[6:7, :] + table_ref[7:8, :]
    low = second.astype(BF16)
    ffn_copy.wait()
    for j in range(4):
        at = slice(j * width, (j + 1) * width)
        active, slope = gelu_back(nn(low, block(ffn_ref, j)))
        slope_ref[:, at] = slope
        active_ref[:, at] = active.astype(BF16)
    hidden = second + nn(active_ref[...], tall(ffn_ref, 4))
    unit_three, scale_three = norm_parts(hidden)
    output_ref[...] = (unit_three * table_ref[8:9, :] + table_ref[9:10, :]).astype(BF16)
    grad, gain_three, bias_three = norm_back(
        cotangent.get()[...].astype(F32), unit_three, scale_three, table_ref[8:9, :]
    )
    grad_low = grad.astype(BF16)
    put_tall(halves_ref, core[0], 4, nn(active_ref[...].T, grad_low))
    inner_ref[...] = (nt(grad_low, tall(ffn_ref, 4)) * slope_ref[...]).astype(BF16)
    put_wide(halves_ref, core[0], 0, nn(low.T, inner_ref[...]))
    copies = send_halves(halves_ref, kept_ref, sent_ref, sems.at[pl.ds(2, 2)])
    grad = grad + nt(inner_ref[...], wide(ffn_ref, 0, 4))
    grad, gain_two, bias_two = norm_back(grad, unit_two, scale_two, table_ref[6:7, :])
    grad_ref[...] = grad
    for index, row in enumerate((gain_two, bias_two, gain_three, bias_three)):
        small_ref[index : index + 1, :] = row
    wait_all(copies)


def cross_backward(
    slot_source, grad_second_ref, q, kv, parts, gathered_ref,
    grad_memory_ref, grad_q_ref, grad_kv_ref, grad_mix_ref, weight_ref, sems,
):
    rows, width = grad_second_ref.shape
    slots = slot_source.shape[0]
    _, groups, longest, _ = grad_kv_ref.shape
    part_rows = weight_ref.shape[1]
    cross_copy = bring_rows(gathered_ref, part_rows, part_rows, weight_ref, sems.at[0])
    grad_low = grad_second_ref[...].astype(BF16)
    cross_copy.wait()
    grad_mix_ref[...] = nt(grad_low, block(weight_ref, 3)).astype(BF16)
    q_ref, kv_ref, parts_ref = q.get(), kv.get(), parts.get()
    sources = [slot_source[slot] for slot in range(slots)]
    slices = slot_rows_of(rows, slots)
    for pair in range(HEADS // 2):
        at = lanes(pair)
        grad_query, grads_k, grads_v = pair_backward(
            [q_ref[here, at] for here in slices],
            [kv_ref[0, source, :, at] for source in sources],
            [kv_ref[1, source, :, at] for source in sources],
            [parts_ref[2 * pair + head] for head in range(2)],
            [grad_mix_ref[here, at] for here in slices],
        )
        grad_q_ref[:, at] = grad_query
        for source, grad_k, grad_v in zip(sources, grads_k, grads_v):
            grad_kv_ref[0, source, :, at] = grad_k
            grad_kv_ref[1, source, :, at] = grad_v
    grad_k = grad_kv_ref[0].reshape(groups * longest, width)
    grad_v = grad_kv_ref[1].reshape(groups * longest, width)
    grad_memory_ref[...] = (
        (nt(grad_k, block(weight_ref, 1)) + nt(grad_v, block(weight_ref, 2)))
        .astype(BF16)
        .reshape(groups, longest, width)
    )


def decoder_lower(
    core, lengths, table_ref, grad_second_ref, grad_q_ref, hidden_ref, mix, memory, grad_kv, own_mix, qkv, logs_in, x, target, gathered_ref,
    kept_ref, sent_ref, grad_x_ref, small_ref, grad_mix_ref, grad_proj_ref, weight_ref, halves_ref, sems,
):
    rows, width = hidden_ref.shape
    slots = lengths.shape[1]
    copies = [bring_rows(gathered_ref, 0, weight_ref.shape[1], weight_ref, sems.at[0])]
    unit, scale = norm_parts(hidden_ref[...])
    first_low = (unit * table_ref[4:5, :] + table_ref[5:6, :]).astype(BF16)
    put(halves_ref, core[0], 0, nn(first_low.T, grad_q_ref[...]))
    grad_second = grad_second_ref[...]
    put(halves_ref, core[0], 3, nn(mix.get()[...].T, grad_second.astype(BF16)))
    wait_all(copies)
    grad = grad_second + nt(grad_q_ref[...], block(weight_ref, 4))
    grad, gain, bias_row = norm_back(grad, unit, scale, table_ref[4:5, :])
    grad_low = grad.astype(BF16)
    grad_mix_ref[...] = nt(grad_low, block(weight_ref, 3)).astype(BF16)
    put(halves_ref, core[0], 7, nn(own_mix.get()[...].T, grad_low))
    memory_ref, grad_kv_ref = memory.get(), grad_kv.get()
    turned = memory_ref[...].reshape(-1, width).T
    for i in range(2):
        put(halves_ref, core[0], 1 + i, nn(turned, grad_kv_ref[i].reshape(-1, width)))
    copies = send_halves(halves_ref, kept_ref, sent_ref, sems.at[pl.ds(1, 2)], 0, 4)
    bias = slot_biases([lengths[0, slot] for slot in range(slots)], rows // slots, rows // slots)
    qkv_ref, log_ref = qkv.get(), logs_in.get()
    slices = slot_rows_of(rows, slots)
    for pair in range(HEADS // 2):
        at = lanes(pair)
        queries, keys, values = [[qkv_ref[i, here, at] for here in slices] for i in range(3)]
        logs = [log_ref[:, 2 * pair + head : 2 * pair + head + 1] for head in range(2)]
        parts = pair_weights(queries, keys, bias, logs)
        grad_query, grads_k, grads_v = pair_backward(queries, keys, values, parts, [grad_mix_ref[here, at] for here in slices])
        grad_proj_ref[0, :, at] = grad_query
        grad_proj_ref[1, :, at] = jnp.concatenate(grads_k, axis=0)
        grad_proj_ref[2, :, at] = jnp.concatenate(grads_v, axis=0)
    x_ref, target_ref = x.get(), target.get()
    turned = replaced(target_ref, table_ref, x_ref).astype(BF16).T
    for i in range(3):
        put(halves_ref, core[0], 4 + i, nn(turned, grad_proj_ref[i]))
    copies += send_halves(halves_ref, kept_ref, sent_ref, sems.at[pl.ds(3, 2)], 4, 4)
    for i in range(3):
        grad = grad + nt(grad_proj_ref[i], block(weight_ref, i))
    marked = target_ref[...] == 1
    grad_x_ref[...] = jnp.where(marked, 0.0, grad)
    small_ref[0:1, :] = gain
    small_ref[1:2, :] = bias_row
    small_ref[2:3, :] = jnp.sum(jnp.where(marked, grad, 0.0), axis=0, keepdims=True)
    wait_all(copies)


def encoder_ffn_backward(
    core, place, lengths, route, pieces_ref, table_ref, small_one_ref, small_two_ref,
    hidden_two, hidden_one, active, slope, mix, part_a, part_b, part_c, part_d,
    kept_ref, sent_ref, grad_first_ref, weight_ref, inner_ref, halves_ref, sems,
):
    rows, width = grad_first_ref.shape
    groups, longest, _ = pieces_ref.shape
    weight_copies = bring_pieces(place, (part_a, part_b, part_c, part_d), weight_ref, sems)
    down = lax.broadcasted_iota(jnp.int32, (rows, longest), 0)
    across = lax.broadcasted_iota(jnp.int32, (rows, longest), 1)
    starts, counts = piece_places(lengths, route, lengths.shape[1], rows)
    grad = jnp.zeros((rows, width), F32)
    for g in range(groups):
        chosen = (down - across == starts[g]) & (across < counts[g])
        grad = grad + nn(jnp.where(chosen, 1.0, 0.0).astype(BF16), pieces_ref[g])
    unit, scale = norm_parts(hidden_two.get()[...])
    grad, gain_two, bias_two = norm_back(grad, unit, scale, table_ref[2:3, :])
    grad_low = grad.astype(BF16)
    put_tall(halves_ref, core[0], 4, nn(active.get()[...].T, grad_low))
    wait_all(weight_copies)
    inner_ref[...] = (nt(grad_low, tall(weight_ref, 4)) * slope.get()[...].astype(F32)).astype(BF16)
    unit, scale = norm_parts(hidden_one.get()[...])
    low = (unit * table_ref[0:1, :] + table_ref[1:2, :]).astype(BF16)
    put_wide(halves_ref, core[0], 0, nn(low.T, inner_ref[...]))
    copies = send_halves(halves_ref, kept_ref, sent_ref, sems.at[pl.ds(32, 2)], 0, 8)
    grad = grad + nt(inner_ref[...], wide(weight_ref, 0, 4))
    grad, gain, bias_row = norm_back(grad, unit, scale, table_ref[0:1, :])
    grad_first_ref[...] = grad
    small_rows = [gain, bias_row, gain_two, bias_two, small_one_ref[0:2, :], small_two_ref[...], small_one_ref[2:3, :]]
    put_rows(halves_ref, 9, small_rows)
    put(halves_ref, core[0], 8, nn(mix.get()[...].T, grad.astype(BF16)))
    copies += send_halves(halves_ref, kept_ref, sent_ref, sems.at[pl.ds(34, 2)], 8, 2)
    wait_all(copies)


def encoder_attention_backward(
    core, place, lengths, grad_in_ref, qkv, logs_in, x,
    part_a, part_b, part_c, part_d,
    kept_ref, sent_ref, grad_x_ref, bias_ref, grad_mix_ref, grad_proj_ref, weight_ref, halves_ref, sems,
):
    rows, width = grad_in_ref.shape
    weight_copies = bring_pieces(place, (part_a, part_b, part_c, part_d), weight_ref, sems)
    bias_ref[...] = segment_bias(lengths, rows)
    grad = grad_in_ref[...]
    wait_all(weight_copies)
    grad_mix_ref[...] = nt(grad.astype(BF16), block(weight_ref, 3)).astype(BF16)
    qkv_ref, log_ref = qkv.get(), logs_in.get()
    halves = halves_of_rows(rows)
    for pair in range(HEADS // 2):
        at = lanes(pair)
        queries, keys, values = [[qkv_ref[i, half, at] for half in halves] for i in range(3)]
        logs = [log_ref[:, 2 * pair + head : 2 * pair + head + 1] for head in range(2)]
        parts = pair_weights(queries, keys, bias_ref[...], logs)
        grad_query, grads_k, grads_v = pair_backward(queries, keys, values, parts, [grad_mix_ref[half, at] for half in halves])
        grad_proj_ref[0, :, at] = grad_query
        grad_proj_ref[1, :, at] = jnp.concatenate(grads_k, axis=0)
        grad_proj_ref[2, :, at] = jnp.concatenate(grads_v, axis=0)
    turned = x.get()[...].T
    for i in range(3):
        put(halves_ref, core[0], i, nn(turned, grad_proj_ref[i]))
    copies = send_halves(halves_ref, kept_ref, sent_ref, sems.at[pl.ds(32, 2)])
    for i in range(3):
        grad = grad + nt(grad_proj_ref[i], block(weight_ref, i))
    grad_x_ref[...] = pltpu.roll(grad, longest_start(lengths, rows), axis=0)
    wait_all(copies)


def finish(counts, me, *refs):
    terms, outs = refs[: 4 * len(counts)], refs[4 * len(counts) :]
    for chain, count in enumerate(counts):
        total = terms[4 * chain][...].astype(F32)
        for ref in terms[4 * chain + 1 : 4 * chain + 4]:
            total = total + ref[...].astype(F32)
        width = total.shape[1]
        at = 0
        own = None
        for ref in outs[:count]:
            columns = ref.shape[-1]
            if columns < width and own is None:
                total = pltpu.roll(total[at:, :], width - me[0] * columns, axis=1)[:, :columns]
                own, at = True, 0
            if len(ref.shape) == 3:
                parts = [ref.at[i] for i in range(ref.shape[0])]
            else:
                parts = [ref.at[:, i * width : (i + 1) * width] for i in range(columns // width)] or [ref]
            for one in parts:
                rows = one.shape[0]
                one[...] = total[at : at + rows, :]
                at += rows
        outs = outs[count:]


VMEM = pl.BlockSpec(memory_space=pltpu.VMEM)
SMEM = pl.BlockSpec(memory_space=pltpu.SMEM)
ANY = pl.BlockSpec(memory_space=pl.ANY)


class Late:
    def __init__(self, ref, target, sem):
        self.ref, self.copy = target, pltpu.make_async_copy(ref, target, sem)
        self.copy.start()

    def get(self):
        self.copy.wait()
        return self.ref


class Early:
    def __init__(self, ref, target, sem):
        self.ref, self.copy = ref, pltpu.make_async_copy(ref, target, sem)

    def send(self):
        self.copy.start()


def run(
    kernel, scalars, arrays, outs, scratch=(), late=(), far=(), far_outs=(), early=(), sems=0, us=1.0, start=(), end=()
):
    moving = len(late) + len(early)
    kinds = [pltpu.VMEM(one.shape, one.dtype) for one in late]
    kinds += [pltpu.VMEM(shape, kind) for shape, kind in tuple(early) + tuple(scratch)]
    kinds += [pltpu.SemaphoreType.DMA((count,)) for count in (moving, sems) if count]

    def body(*refs):
        left = list(refs)

        def take(count):
            taken = left[:count]
            del left[:count]
            return taken

        given = take(len(scalars) + len(arrays))
        late_in, far_in, out, early_out = take(len(late)), take(len(far)), take(len(outs)), take(len(early))
        late_at, early_at, rest = take(len(late)), take(len(early)), take(len(scratch))
        own = left[0] if moving else None
        lates = [Late(ref, at, own.at[i]) for i, (ref, at) in enumerate(zip(late_in, late_at))]
        earlies = [Early(at, ref, own.at[len(late) + i]) for i, (ref, at) in enumerate(zip(early_out, early_at))]
        kernel(*given, *lates, *far_in, *out, *earlies, *rest, *left[1 if moving else 0 :])
        for one in earlies:
            one.copy.wait()

    given, sends = (tuple(scalars), tuple(arrays), tuple(late), tuple(far)), [one.sends for one in start]
    if start:
        given, sends = lax.optimization_barrier((given, sends))
    for one, ready in zip(start, sends):
        one.sends = ready
        one.start()
    results = pl.pallas_call(
        body,
        out_shape=[jax.ShapeDtypeStruct(shape, kind) for shape, kind in tuple(outs) + tuple(early)],
        in_specs=[SMEM] * len(scalars) + [VMEM] * len(arrays) + [ANY] * (len(late) + len(far)),
        out_specs=[ANY if index in far_outs or index >= len(outs) else VMEM for index in range(len(outs) + len(early))],
        scratch_shapes=kinds,
        compiler_params=pltpu.CompilerParams(vmem_limit_bytes=56 << 20),
        cost_estimate=pl.CostEstimate(flops=int(us * 1.15e9), bytes_accessed=1 << 20, transcendentals=0),
    )(*given[0], *given[1], *given[2], *given[3])
    if end:
        results, got = lax.optimization_barrier((results, [one.got for one in end]))
        for one, blocks in zip(end, got):
            one.got = blocks
            one.finish()
    return results


def exchange(block, pairs):
    return lax.ppermute(block, AXES, pairs)


def pick(blocks, place):
    return lax.dynamic_index_in_dim(blocks, place, 0, keepdims=False)


def added(one, other):
    return (one.astype(F32) + other.astype(F32)).astype(BF16)


RING = (0, 1, 3, 2)


def sum_scatter(packs, count):
    me = lax.axis_index(AXES)
    core, low, high = me % 2, (me // 2) % 2, (me // 4) % 2
    rest = count // 8
    by_core = [pack.reshape((rest * 4, 2) + pack.shape[1:]) for pack in packs]
    sent, kept = [
        jnp.concatenate([lax.dynamic_index_in_dim(pack, side, 1, keepdims=False) for pack in by_core], axis=1)
        for side in (1 - core, core)
    ]
    tail = sent.shape[1:]
    kept = added(kept, exchange(sent, [(i, i ^ 1) for i in range(count)]))
    quads = kept.reshape((rest, 4) + tail)

    def two(first, second):
        parts = [lax.dynamic_index_in_dim(quads, place, 1, keepdims=True) for place in (first, second)]
        return jnp.concatenate(parts, axis=1)

    other_high, other_low = 1 - high, 1 - low
    sent = two(
        jnp.where(core == 0, 2 * other_high, other_low),
        jnp.where(core == 0, 2 * other_high + 1, other_low + 2),
    )
    kept = two(jnp.where(core == 0, 2 * high, low), jnp.where(core == 0, 2 * high + 1, low + 2))
    kept = added(kept, exchange(sent, [(i, i ^ (2 if i % 2 else 4)) for i in range(count)]))
    mine = jnp.where(core == 0, low, high)
    sent = lax.dynamic_index_in_dim(kept, 1 - mine, 1, keepdims=False)
    kept = lax.dynamic_index_in_dim(kept, mine, 1, keepdims=False)
    kept = added(kept, exchange(sent, [(i, i ^ (4 if i % 2 else 2)) for i in range(count)]))
    stride = 8
    while rest > 4:
        bit = (me // stride) % 2
        halves = kept.reshape((rest // 2, 2) + tail)
        sent = lax.dynamic_index_in_dim(halves, 1 - bit, 1, keepdims=False)
        kept = lax.dynamic_index_in_dim(halves, bit, 1, keepdims=False)
        kept = added(kept, exchange(sent, [(i, i ^ stride) for i in range(count)]))
        rest, stride = rest // 2, stride * 2
    order = RING if rest == 4 else tuple(range(rest))
    place_of = jnp.asarray([order.index(z) for z in range(rest)], jnp.int32)
    ring = jnp.asarray(order, jnp.int32)
    here = place_of[me // stride]
    onward = [
        (i, order[(order.index(i // stride) + 1) % rest] * stride + i % stride) for i in range(count)
    ]
    moving = pick(kept, ring[(here - 1) % rest]) if rest > 1 else kept[0]
    for step in range(rest - 1):
        arrived = exchange(moving, onward)
        own = pick(kept, ring[(here - 2 - step) % rest])
        moving = arrived.astype(F32) + own.astype(F32)
        if step < rest - 2:
            moving = moving.astype(BF16)
    return moving.astype(F32)


OUT_FIRST = [(i, i ^ (2 if i % 2 else 4)) for i in range(32)]
OUT_SECOND = [(i, i ^ (4 if i % 2 else 2)) for i in range(32)]
CORES = [(i, i ^ 1) for i in range(32)]


def gather_places():
    table = np.zeros((32, 32), np.int32)
    for me in range(32):
        for number in range(32):
            core = (me ^ (number // 16)) % 2
            first, second, level = (number // 8) % 2, (number // 4) % 2, number % 4
            x, y = (first, second) if core == 0 else (second, first)
            table[me, number] = ((me - me % 2) ^ (level * 8) ^ (x * 4) ^ (y * 2)) + core
    return table


def gather_blocks(mine):
    levels = [exchange(mine, [(i, i ^ (8 * k)) for i in range(32)]) for k in (1, 2, 3)]
    near = jnp.stack([mine] + levels)
    near = jnp.concatenate([near, exchange(near, OUT_SECOND)])
    far = exchange(near, OUT_FIRST)
    return near, far, exchange(near, CORES), exchange(far, CORES)


def together(*steps):
    arrived = lax.optimization_barrier([step.got for step in steps])
    for step, blocks in zip(steps, arrived):
        step.got = blocks


class Scatter:
    def __init__(self, kept, sent):
        me = lax.axis_index(AXES)
        core, low, high = me % 2, (me // 2) % 2, (me // 4) % 2
        self.bits = (jnp.where(core == 0, high, low), jnp.where(core == 0, low, high))
        self.level = me // 8
        self.kept, self.sends, self.stage = kept, [sent], 0

    def start(self):
        pairs = ([CORES], [OUT_FIRST], [OUT_SECOND], [[(i, i ^ (8 * k)) for i in range(32)] for k in (1, 2, 3)])
        self.got = [exchange(block, to) for block, to in zip(self.sends, pairs[self.stage])]
        return self.got

    def finish(self):
        if self.stage == 3:
            self.sends = []
            return self.sends
        got, size = self.got[0], self.kept.shape[0]

        def summed(place, count):
            return added(
                lax.dynamic_slice_in_dim(self.kept, place, count, 0), lax.dynamic_slice_in_dim(got, place, count, 0)
            )

        if self.stage < 2:
            half = size // 2
            bit = self.bits[self.stage]
            kept, sends = summed(bit * half, half), [summed((1 - bit) * half, half)]
        else:
            kept = summed(self.level, 1)[0]
            sends = [summed(jnp.bitwise_xor(self.level, k), 1)[0] for k in (1, 2, 3)]
        self.kept, self.sends, self.stage = kept, sends, self.stage + 1
        return self.sends


def on_device(
    enc_input,
    dec_input,
    target_mask,
    src_lengths,
    tgt_lengths,
    memory_route,
    enc_qkv,
    enc_out,
    enc_ffn_in,
    enc_ffn_out,
    enc_norms,
    dec_qkv,
    dec_out,
    cross_qkv,
    cross_out,
    dec_ffn_in,
    dec_ffn_out,
    dec_norms,
    mask_vector,
    out_cotangent,
):
    dp_count, groups = lax.axis_size("dp"), lax.axis_size("fsdp")
    count = dp_count * groups
    rows, width = enc_input.shape
    slots = src_lengths.shape[1]
    longest = rows // 2
    slot_rows = rows // slots
    part = enc_out.shape[0]
    inner = enc_ffn_in.shape[1]
    pieces_in = inner // width

    direct = count == 32 and part == 16
    kernel_part = width // 32
    joined = kernel_part // part
    me = lax.axis_index(AXES)
    my_dp, my_group = lax.axis_index("dp"), lax.axis_index("fsdp")

    def split(pack, squares):
        first = pack[:, : squares * part].reshape(32, joined, squares, part, width).transpose(0, 2, 1, 3, 4)
        return jnp.concatenate([first.reshape(32, -1, width), pack[:, squares * part :].reshape(32, -1, width)], axis=1)

    def unsplit(kept, sent, squares, used):
        kept = kept.reshape((2, 2, 4) + kept.shape[1:]).transpose(2, 0, 1, 3, 4)
        sent = sent.reshape((2, 2, 4) + sent.shape[1:]).transpose(2, 1, 0, 3, 4)
        pack = jnp.stack([kept, sent], axis=3).reshape(32, -1, width)
        first = pack[:, : squares * kernel_part].reshape(32, squares, joined, part, width).transpose(0, 2, 1, 3, 4)
        rest = pack[:, squares * kernel_part : used * kernel_part].reshape(count, -1, width)
        return jnp.concatenate([first.reshape(count, -1, width), rest], axis=1)

    if direct:
        core = (me % 2).reshape(1)
        attention_pack, ffn_pack, decoder_pack = run(
            pack_weights,
            (me.reshape(1),),
            (
                src_lengths, memory_route, mask_vector.reshape(1, part),
                enc_qkv, enc_out, enc_ffn_in, enc_ffn_out, enc_norms,
                dec_qkv, dec_out, cross_qkv, cross_out, dec_ffn_in, dec_ffn_out, dec_norms,
            ),
            (((5 * part, width), BF16), ((8 * part, width), BF16), ((16 * part, width), BF16)),
            us=2.0,
        )
        dec_all = lax.all_gather(decoder_pack, AXES, axis=0, tiled=False)
        attention_blocks = gather_blocks(attention_pack)
        ffn_blocks = gather_blocks(ffn_pack)
        place = jnp.asarray(gather_places())[me]
    else:
        core = jnp.zeros((1,), jnp.int32)

        def square(weight):
            return weight.reshape(-1, width)

        def wide(weight):
            return weight.reshape(part, pieces_in, width).transpose(1, 0, 2).reshape(-1, width)

        def whole(norms):
            return lax.all_gather(norms, AXES, axis=norms.ndim - 1, tiled=True).reshape(-1, width)

        def gathered(weights):
            return lax.all_gather(jnp.concatenate(weights), AXES, axis=0, tiled=False)

        rows_of = [whole(enc_norms), whole(dec_norms), whole(mask_vector)]
        first_rows = jnp.pad(jnp.concatenate(rows_of), ((0, kernel_part - 11), (0, 0)))
        small_blocks = jnp.concatenate([first_rows[None], jnp.zeros((31, kernel_part, width), BF16)])
        attention_all = split(gathered([square(enc_qkv), enc_out]), 4)
        attention_all = jnp.concatenate([attention_all, small_blocks], axis=1)
        attention_blocks = tuple(attention_all[i * 8 : i * 8 + 8] for i in range(4))
        ffn_all = split(gathered([wide(enc_ffn_in), enc_ffn_out]), pieces_in)
        ffn_blocks = tuple(ffn_all[i * 8 : i * 8 + 8] for i in range(4))
        decoder = [square(dec_qkv), dec_out, square(cross_qkv), cross_out, wide(dec_ffn_in), dec_ffn_out]
        dec_all = split(gathered(decoder), 8 + pieces_in)
        place = jnp.arange(32, dtype=jnp.int32)

    def some(*chains):
        return chains if direct else ()

    plane, three = (rows, width), (3, rows, width)
    memory_shape = (groups, longest, width)
    logs_shape = (rows, HEADS)
    parts_shape = (HEADS, rows, longest)

    def half_of(pieces):
        return ((16, pieces * kernel_part, width), BF16)

    def halves_of(pieces):
        return ((2, 16, pieces * kernel_part, width), BF16)

    def weights_of(pieces):
        return ((32, pieces * kernel_part, width), BF16)

    half_ffn = ((rows, inner), BF16)
    e_mix, e_logs, e_hidden_one, table, e_qkv, x_turned = run(
        encoder_attention,
        (place, src_lengths),
        (enc_input,),
        ((plane, BF16), (logs_shape, F32), (plane, F32), ((kernel_part, width), F32)),
        (((rows, longest), F32), weights_of(5)),
        far=attention_blocks,
        early=((three, BF16), (plane, BF16)),
        sems=32,
        us=9.5,
    )
    pieces, e_active, e_slope, e_hidden_two = run(
        encoder_ffn,
        (place, src_lengths, memory_route),
        (e_hidden_one, table),
        ((memory_shape, BF16),),
        (weights_of(2 * pieces_in),),
        far=ffn_blocks,
        early=(half_ffn, half_ffn, (plane, F32)),
        sems=32,
        us=9.0,
    )
    memory_in = lax.all_to_all(pieces, "fsdp", split_axis=0, concat_axis=0, tiled=True)
    d_mix, d_logs, d_hidden, target, d_qkv = run(
        self_forward,
        (tgt_lengths,),
        (dec_input, target_mask[:, None], table),
        ((plane, BF16), (logs_shape, F32), (plane, F32), ((rows, 1), jnp.int32)),
        (weights_of(4),),
        far=(dec_all,),
        early=((three, BF16),),
        sems=1,
        us=6.4,
    )
    if direct:
        ints = table[11].reshape(dp_count, groups, part)
        ints = lax.dynamic_index_in_dim(ints, my_dp, 0, keepdims=False).astype(jnp.int32)
        lengths_near, route_near = ints[:, :slots], ints[:, slots : 2 * slots]
    else:
        lengths_near = lax.all_gather(src_lengths[0], "fsdp")
        route_near = lax.all_gather(memory_route[0], "fsdp")
    ids = jnp.arange(groups, dtype=jnp.int32)
    wanted = my_group * slots + jnp.arange(slots, dtype=jnp.int32)
    chosen = route_near[None] == wanted[:, None, None]
    slot_source = jnp.sum(jnp.where(chosen, ids[None, :, None], 0), axis=(1, 2))
    slot_length = jnp.sum(jnp.where(chosen, lengths_near[None], 0), axis=(1, 2))

    dec_output, *dffn_halves, grad_second, small_two, parts, q_rows, kv_rows, c_mix = run(
        decoder_upper,
        (core, slot_source, slot_length),
        (d_hidden, memory_in, table),
        ((plane, BF16), half_of(8), half_of(8), (plane, F32), ((4, width), F32)),
        (((rows, inner), F32), half_ffn, half_ffn, weights_of(4), weights_of(8), halves_of(8)),
        late=(out_cotangent,),
        far=(dec_all,),
        far_outs=(1, 2),
        early=((parts_shape, F32), (plane, BF16), ((2,) + memory_shape, BF16), (plane, BF16)),
        sems=4,
        us=19.0,
    )

    def begin(halves):
        return Scatter(*halves) if direct else None

    dffn = begin(dffn_halves)
    grad_memory, grad_q, grad_kv = run(
        cross_backward,
        (slot_source,),
        (grad_second,),
        ((memory_shape, BF16), (plane, BF16), ((2,) + memory_shape, BF16)),
        ((plane, BF16), weights_of(4)),
        late=(q_rows, kv_rows, parts),
        far=(dec_all,),
        sems=1,
        us=10.0,
        start=some(dffn),
        end=some(dffn),
    )
    returned = lax.all_to_all(grad_memory, "fsdp", split_axis=0, concat_axis=0, tiled=True)
    *middle_halves, dec_input_grad, small_one = run(
        decoder_lower,
        (core, tgt_lengths),
        (table, grad_second, grad_q, d_hidden),
        (half_of(8), half_of(8), (plane, F32), ((3, width), F32)),
        ((plane, BF16), (three, BF16), weights_of(5), halves_of(8)),
        late=(c_mix, memory_in, grad_kv, d_mix, d_qkv, d_logs, dec_input, target),
        far=(dec_all,),
        far_outs=(0, 1),
        sems=5,
        us=16.0,
        start=some(dffn),
        end=some(dffn),
    )
    returned, middle_halves = lax.optimization_barrier((returned, middle_halves))
    middle = begin(middle_halves)
    if direct:
        middle.start()
        middle.finish()
    *effn_halves, grad_enc = run(
        encoder_ffn_backward,
        (core, place, src_lengths, memory_route),
        (returned, table, small_one, small_two),
        (half_of(10), half_of(10), (plane, F32)),
        (weights_of(8), half_ffn, halves_of(10)),
        late=(e_hidden_two, e_hidden_one, e_active, e_slope, e_mix),
        far=ffn_blocks,
        far_outs=(0, 1),
        sems=36,
        us=12.0,
        start=some(dffn, middle),
        end=some(dffn, middle),
    )
    effn = begin(effn_halves)
    if direct:
        effn.start()
        effn.finish()
    *eatt_halves, enc_input_grad = run(
        encoder_attention_backward,
        (core, place, src_lengths),
        (grad_enc,),
        (half_of(3), half_of(3), (plane, F32)),
        (((rows, longest), F32), (plane, BF16), (three, BF16), weights_of(5), halves_of(3)),
        late=(e_qkv, e_logs, x_turned),
        far=attention_blocks,
        far_outs=(0, 1),
        sems=34,
        us=12.0,
        start=some(dffn, middle, effn),
        end=some(dffn, middle),
    )
    eatt = begin(eatt_halves)

    def ends(*given, start=(), end=()):
        chains = [one for one in given if isinstance(one, Scatter)]
        shapes, counts = [], []
        for one in given:
            if isinstance(one, Scatter):
                counts.append(0)
            else:
                counts[-1] += 1
                shapes.append((one, F32))
        terms = [term for chain in chains for term in (chain.kept, *chain.got)]
        return run(partial(finish, tuple(counts)), (me.reshape(1),), terms, shapes, us=2.5, start=start, end=end)

    cube, square_part, wide_part, tall_part = (3, part, width), (part, width), (part, inner), (inner // count, width)
    if direct:
        middle.start()
        eatt.start()
        together(eatt, effn)
        for one in (eatt, effn):
            one.finish()
            one.start()
        together(eatt, effn)
        for one in (eatt, effn):
            one.finish()
        decoder_grads = ends(
            dffn, wide_part, tall_part, middle, cube, square_part, cube, square_part, start=(effn, eatt), end=(eatt,)
        )
        dec_ffn_grads, middle_grads = decoder_grads[:2], decoder_grads[2:]
        norm_shapes = ((2, 2, part), (3, 2, part), (1, part))
        eatt.start()
        encoder_grads = ends(effn, wide_part, tall_part, square_part, *norm_shapes, eatt, cube)
        enc_ffn_grads, small_grads, qkv_grads = encoder_grads[:3], list(encoder_grads[3:6]), encoder_grads[6]
        small_grads[2] = small_grads[2].reshape(part)
    else:

        def piece(summed, first, pieces=1):
            return summed[first * part : (first + pieces) * part]

        def wide_piece(summed):
            picked = piece(summed, 0, pieces_in).reshape(pieces_in, part, width)
            return picked.transpose(1, 0, 2).reshape(part, inner)

        effn_pack = unsplit(*[half[:, : 8 * kernel_part] for half in effn_halves], 4, 8)
        eout_pack = unsplit(*[half[:, 8 * kernel_part : 9 * kernel_part] for half in effn_halves], 1, 1)
        packs = [
            unsplit(*dffn_halves, 4, 8),
            unsplit(*middle_halves, 8, 8),
            jnp.concatenate([effn_pack, eout_pack], axis=1),
            unsplit(*eatt_halves, 3, 3),
        ]
        dffn_sum, middle_sum, effn_sum, eatt_sum = [sum_scatter([pack], count) for pack in packs]
        dec_ffn_grads = (wide_piece(dffn_sum), piece(dffn_sum, pieces_in, pieces_in))
        enc_ffn_grads = (wide_piece(effn_sum), piece(effn_sum, pieces_in, pieces_in), piece(effn_sum, 8))
        middle_grads = [
            piece(middle_sum, 0, 3).reshape(cube), piece(middle_sum, 3), piece(middle_sum, 4, 3).reshape(cube), piece(middle_sum, 7)
        ]
        qkv_grads = piece(eatt_sum, 0, 3).reshape(cube)
        small_sum = lax.psum(effn_halves[0][0, 9 * kernel_part :].astype(F32), AXES)
        small_sum = lax.dynamic_slice_in_dim(small_sum[:11], me * part, part, 1)
        small_grads = small_sum[:4].reshape(2, 2, part), small_sum[4:10].reshape(3, 2, part), small_sum[10]

    return (
        dec_output,
        enc_input_grad,
        dec_input_grad,
        qkv_grads,
        enc_ffn_grads[2],
        *enc_ffn_grads[:2],
        small_grads[0],
        *middle_grads[2:],
        *middle_grads[:2],
        *dec_ffn_grads,
        small_grads[1],
        small_grads[2],
    )


def solution(mesh):
    rows = P(AXES, None)
    flat = P(AXES)
    cube = P(None, AXES, None)
    norm = P(None, None, AXES)
    in_specs = (
        (rows, rows, flat, rows, rows, rows)
        + (cube, rows, rows, rows, norm)
        + (cube, rows, cube, rows, rows, rows, norm, flat)
        + (rows,)
    )
    out_specs = (
        (rows, rows, rows)
        + (cube, rows, rows, rows, norm)
        + (cube, rows, cube, rows, rows, rows, norm, flat)
    )
    return jax.shard_map(on_device, mesh=mesh, in_specs=in_specs, out_specs=out_specs, check_vma=False)
```

```python
import math
from functools import partial

import jax
import jax.numpy as jnp
import numpy as np
from jax import lax
from jax.experimental import pallas as pl
from jax.experimental.pallas import tpu as pltpu
from jax.sharding import PartitionSpec as P

HEADS = 8
HEAD_DIM = 64
SCALE = 1.0 / math.sqrt(HEAD_DIM)
AXES = ("dp", "fsdp")
F32 = jnp.float32
BF16 = jnp.bfloat16


MASKED = -1e30
GELU_C = math.sqrt(2.0 / math.pi)
GELU_A = 0.044715


def nn(left, right):
    return jnp.dot(left, right, preferred_element_type=F32)


def nt(left, right):
    return lax.dot_general(left, right, (((1,), (1,)), ((), ())), preferred_element_type=F32)


def norm_parts(hidden):
    center = hidden - jnp.mean(hidden, axis=-1, keepdims=True)
    scale = lax.rsqrt(jnp.mean(center * center, axis=-1, keepdims=True) + 1e-05)
    return center * scale, scale


def norm_back(grad, unit, scale, gain):
    inner = grad * gain
    mean_one = jnp.mean(inner, axis=-1, keepdims=True)
    mean_two = jnp.mean(inner * unit, axis=-1, keepdims=True)
    return (
        scale * (inner - mean_one - unit * mean_two),
        jnp.sum(grad * unit, axis=0, keepdims=True),
        jnp.sum(grad, axis=0, keepdims=True),
    )


def gelu_tanh(pre):
    return jnp.tanh(GELU_C * (pre + GELU_A * (pre * pre * pre)))


def gelu_back(pre):
    tanh = gelu_tanh(pre)
    slope = GELU_C * (1.0 + 3.0 * GELU_A * (pre * pre))
    return 0.5 * pre * (1.0 + tanh), 0.5 * (1.0 + tanh) + 0.5 * pre * (1.0 - tanh * tanh) * slope


def block(ref, first):
    width = ref.shape[2]
    part = width // ref.shape[0]
    return ref[:, first * part : (first + 1) * part, :].reshape(width, width)


def wide(ref, first, count):
    return jnp.concatenate([block(ref, first + index) for index in range(count)], axis=1)


def tall(ref, first):
    count, _, width = ref.shape
    part = width // count
    return ref[:, first * part : (first + 4) * part, :].reshape(4 * width, width)


CORNERS = [(x, y, side) for x in range(2) for y in range(2) for side in range(2)]


def place_of(x, y, side):
    return 8 * x + 4 * y if side == 0 else 8 * y + 4 * x


def put(ref, core, first, grad):
    width = grad.shape[1]
    part = width // 32
    cut = grad.astype(BF16).reshape(4, 2, 2, 2, part, width)
    rows = slice(first * part, (first + 1) * part)
    for x, y, side in CORNERS:
        half = core if side == 0 else 1 - core
        place = place_of(x, y, side)
        ref[half, place : place + 4, rows, :] = cut[:, x, y, side]


def put_wide(ref, core, first, grad):
    width = ref.shape[3]
    for index in range(grad.shape[1] // width):
        put(ref, core, first + index, grad[:, index * width : (index + 1) * width])


def put_tall(ref, core, first, grad):
    width = grad.shape[1]
    part = width // 32
    rows = slice(first * part, (first + 4) * part)
    cut = grad.astype(BF16).reshape(4, 2, 2, 2, 4 * part, width)
    for x, y, side in CORNERS:
        half = core if side == 0 else 1 - core
        place = place_of(x, y, side)
        ref[half, place : place + 4, rows, :] = cut[:, x, y, side]


def put_rows(ref, first, rows_of):
    halves, count, _, width = ref.shape
    part = width // (halves * count)
    used = sum(row.shape[0] for row in rows_of)
    rows = jnp.concatenate(rows_of + [jnp.zeros((part - used, width), F32)], axis=0)
    ref[:, :, first * part : (first + 1) * part, :] = jnp.broadcast_to(
        rows.astype(BF16)[None, None], (halves, count, part, width)
    )


def bring_pieces(place, refs, target, sems, first=0):
    part = target.shape[2] // target.shape[0]
    rows = pl.ds(first * part, target.shape[1])
    copies = []
    for array, ref in enumerate(refs):
        for index in range(8):
            number = array * 8 + index
            copies.append(pltpu.make_async_copy(ref.at[index, rows], target.at[place[number]], sems.at[number]))
    for copy in copies:
        copy.start()
    return copies


def bring_rows(ref, first, count, target, sem):
    copy = pltpu.make_async_copy(ref.at[:, pl.ds(first, count), :], target, sem)
    copy.start()
    return copy


def send_halves(halves_ref, kept_ref, sent_ref, sems, first=0, count=None):
    part = halves_ref.shape[3] // 32
    rows = pl.ds(first * part, halves_ref.shape[2] if count is None else count * part)
    copies = [
        pltpu.make_async_copy(halves_ref.at[half, :, rows], ref.at[:, rows], sems.at[half])
        for half, ref in enumerate((kept_ref, sent_ref))
    ]
    for copy in copies:
        copy.start()
    return copies


def wait_all(copies):
    for copy in copies:
        copy.wait()


PAIR = 2 * HEAD_DIM


def twice(pair_rows):
    lane = lax.broadcasted_iota(jnp.int32, pair_rows.shape, 1)
    zero = jnp.zeros_like(pair_rows)
    return jnp.concatenate(
        [jnp.where(lane < HEAD_DIM, pair_rows, zero), jnp.where(lane < HEAD_DIM, zero, pair_rows)], axis=0
    )


def each_head(scores, count):
    return [scores[:, head * count : (head + 1) * count] for head in range(2)]


def pair_scores(queries, keys):
    return jnp.concatenate([nt(q, twice(k)) for q, k in zip(queries, keys)], axis=0)


def pair_forward(queries, keys, values, bias):
    count = keys[0][0].shape[0]
    scores = [pair_scores(q, k) for q, k in zip(queries, keys)]
    masked = [part + bias for both in scores for part in each_head(both, count)]
    tops = [jnp.max(part, axis=-1, keepdims=True) for part in masked]
    raised = [jnp.exp(part - top) for part, top in zip(masked, tops)]
    totals = [jnp.sum(part, axis=-1, keepdims=True) for part in raised]
    parts = [part * (1.0 / total) for part, total in zip(raised, totals)]
    logs = [top + jnp.log(total) for top, total in zip(tops, totals)]
    mixtures = []
    for pair, blocks in enumerate(values):
        low = jnp.concatenate([part.astype(BF16) for part in parts[2 * pair : 2 * pair + 2]], axis=1)
        rows = low.shape[0] // len(blocks)
        mixed = [nn(low[i * rows : (i + 1) * rows], twice(v)) for i, v in enumerate(blocks)]
        mixtures.append(jnp.concatenate(mixed, axis=0))
    return mixtures, parts, logs


def pair_weights(queries, keys, bias, logs):
    scores = each_head(pair_scores(queries, keys), keys[0].shape[0])
    return [jnp.exp(part + bias - log) for part, log in zip(scores, logs)]


def turned_products(rows_of, weights, count):
    rows = weights.shape[0] // len(rows_of)
    results = []
    for index, block_rows in enumerate(rows_of):
        both = nn(block_rows.T, weights[index * rows : (index + 1) * rows])
        own = jnp.concatenate([both[:HEAD_DIM, :count], both[HEAD_DIM:, count:]], axis=0)
        results.append(own.astype(BF16).T)
    return results


def pair_backward(queries, keys, values, parts, grads_out):
    count = keys[0].shape[0]
    grad_parts = each_head(pair_scores(grads_out, values), count)
    grad_scores = []
    for part, grad_part in zip(parts, grad_parts):
        delta = jnp.sum(part * grad_part, axis=-1, keepdims=True)
        grad_scores.append((part * (grad_part - delta)).astype(BF16))
    grad_scores = jnp.concatenate(grad_scores, axis=1)
    weights = jnp.concatenate([part.astype(BF16) for part in parts], axis=1)
    rows = grad_scores.shape[0] // len(keys)
    grad_query = [nn(grad_scores[i * rows : (i + 1) * rows], twice(k)) for i, k in enumerate(keys)]
    return (
        (jnp.concatenate(grad_query, axis=0) * SCALE).astype(BF16),
        turned_products(queries, grad_scores, count),
        turned_products(grads_out, weights, count),
    )


def sentence_starts(lengths):
    starts = [0]
    for sentence in range(lengths.shape[1] - 1):
        starts.append(starts[-1] + lengths[0, sentence])
    return starts


def longest_start(lengths, rows):
    starts = sentence_starts(lengths)
    place = jnp.int32(0)
    for sentence, start in enumerate(starts):
        place = place + jnp.where(lengths[0, sentence] == rows // 2, start, 0)
    return place


def turned_starts(lengths, rows):
    shift = longest_start(lengths, rows)
    places = [start - shift for start in sentence_starts(lengths)]
    return [jnp.where(place < 0, place + rows, place) for place in places]


def piece_places(lengths, route, slots, rows):
    starts = turned_starts(lengths, rows)
    first, length = [], []
    for device in range(route.shape[1]):
        here, count = jnp.int32(0), jnp.int32(0)
        for sentence in range(route.shape[1]):
            goes = route[0, sentence] // slots == device
            here = here + jnp.where(goes, starts[sentence], 0)
            count = count + jnp.where(goes, lengths[0, sentence], 0)
        first.append(here)
        length.append(count)
    return first, length


def segment_bias(lengths, rows):
    half = rows // 2
    down = lax.broadcasted_iota(jnp.int32, (half, 1), 0) + half
    across = lax.broadcasted_iota(jnp.int32, (1, half), 1) + half
    segment_down = jnp.zeros_like(down)
    segment_across = jnp.zeros_like(across)
    for start in turned_starts(lengths, rows):
        segment_down += (down >= start).astype(jnp.int32)
        segment_across += (across >= start).astype(jnp.int32)
    second = jnp.where(segment_down == segment_across, 0.0, MASKED)
    return jnp.concatenate([jnp.zeros((half, half), F32), second], axis=0)


def halves_of_rows(rows):
    return [slice(0, rows // 2), slice(rows // 2, rows)]


def lanes(pair):
    return slice(pair * PAIR, (pair + 1) * PAIR)


def pack_weights(
    me, src_ref, route_ref, mask_ref, e_qkv_ref, e_out_ref, e_in_ref, e_outff_ref, e_norm_ref,
    d_qkv_ref, d_out_ref, c_qkv_ref, c_out_ref, d_in_ref, d_outff_ref, d_norm_ref,
    attention_ref, ffn_ref, decoder_ref,
):
    part, width = e_out_ref.shape
    lane = lax.broadcasted_iota(jnp.int32, (part, width), 1)
    row = lax.broadcasted_iota(jnp.int32, (part, width), 0)
    spread = jnp.where(lane - row == me[0] * part, 1.0, 0.0).astype(BF16)
    ints = [nn(ref[...].astype(F32).astype(BF16), spread[4 * i : 4 * i + 4]) for i, ref in enumerate((src_ref, route_ref))]
    rows = [nn(e_norm_ref[i], spread) for i in range(2)] + [nn(d_norm_ref[i], spread) for i in range(3)]
    rows = rows + [nn(mask_ref[...], spread), ints[0] + ints[1]]
    used = sum(r.shape[0] for r in rows)
    rows = jnp.concatenate(rows + [jnp.zeros((part - used, width), F32)], axis=0)

    def fill(ref, first, weight):
        ref[first * part : first * part + weight.shape[0], :] = weight

    for i in range(3):
        fill(attention_ref, i, e_qkv_ref[i])
        fill(decoder_ref, i, d_qkv_ref[i])
        fill(decoder_ref, 4 + i, c_qkv_ref[i])
    fill(attention_ref, 3, e_out_ref[...])
    fill(attention_ref, 4, rows.astype(BF16))
    fill(decoder_ref, 3, d_out_ref[...])
    fill(decoder_ref, 7, c_out_ref[...])
    for j in range(4):
        fill(ffn_ref, j, e_in_ref[:, j * width : (j + 1) * width])
        fill(decoder_ref, 8 + j, d_in_ref[:, j * width : (j + 1) * width])
    fill(ffn_ref, 4, e_outff_ref[...])
    fill(decoder_ref, 12, d_outff_ref[...])


def put_logs(log_ref, pairs, logs):
    for index, log in enumerate(logs):
        head = 2 * pairs[0] + index
        log_ref[:, head : head + 1] = log


def encoder_attention(
    place, lengths, x_ref, part_a, part_b, part_c, part_d,
    log_ref, hidden_ref, table_ref, qkv, x_turned, mix, bias_ref, weight_ref, sems,
):
    rows, width = x_ref.shape
    copies = bring_pieces(place, (part_a, part_b, part_c, part_d), weight_ref, sems)
    turned = pltpu.roll(x_ref[...].astype(F32), rows - longest_start(lengths, rows), axis=0)
    rows_in = turned.astype(BF16)
    x_turned.ref[...] = rows_in
    x_turned.send()
    bias_ref[...] = segment_bias(lengths, rows)
    wait_all(copies)
    part = width // weight_ref.shape[0]
    table_ref[...] = jnp.sum(weight_ref[:, 4 * part : 5 * part, :].astype(F32), axis=0)
    qkv_ref, mix_ref = qkv.ref, mix.ref
    qkv_ref[0] = (nn(rows_in, block(weight_ref, 0)) * SCALE).astype(BF16)
    qkv_ref[1] = nn(rows_in, block(weight_ref, 1)).astype(BF16)
    qkv_ref[2] = nn(rows_in, block(weight_ref, 2)).astype(BF16)
    qkv.send()
    halves = halves_of_rows(rows)
    for first in range(0, HEADS // 2, 2):
        pairs = (first, first + 1)
        mixtures, _, logs = pair_forward(
            *[[[qkv_ref[i, half, lanes(pair)] for half in halves] for pair in pairs] for i in range(3)], bias_ref[...]
        )
        for pair, mixture in zip(pairs, mixtures):
            mix_ref[:, lanes(pair)] = mixture.astype(BF16)
        put_logs(log_ref, pairs, logs)
    mix.send()
    hidden_ref[...] = turned + nn(mix_ref[...], block(weight_ref, 3))


def encoder_ffn(
    place, lengths, route, hidden_one_ref, table_ref, part_a, part_b, part_c, part_d,
    pieces_ref, active, slope, hidden_two, weight_ref, sems,
):
    rows, width = hidden_one_ref.shape
    groups, longest, _ = pieces_ref.shape
    copies = bring_pieces(place, (part_a, part_b, part_c, part_d), weight_ref, sems)
    unit, _ = norm_parts(hidden_one_ref[...])
    first = unit * table_ref[0:1, :] + table_ref[1:2, :]
    low = first.astype(BF16)
    wait_all(copies)
    for j in range(4):
        value, slope_value = gelu_back(nn(low, block(weight_ref, j)))
        active.ref[:, j * width : (j + 1) * width] = value.astype(BF16)
        slope.ref[:, j * width : (j + 1) * width] = slope_value.astype(BF16)
    active.send()
    slope.send()
    hidden = first + nn(active.ref[...], tall(weight_ref, 4))
    hidden_two.ref[...] = hidden
    hidden_two.send()
    unit, _ = norm_parts(hidden)
    memory = (unit * table_ref[2:3, :] + table_ref[3:4, :]).astype(BF16)
    down = lax.broadcasted_iota(jnp.int32, (longest, rows), 0)
    across = lax.broadcasted_iota(jnp.int32, (longest, rows), 1)
    starts, _ = piece_places(lengths, route, lengths.shape[1], rows)
    for g in range(groups):
        chosen = jnp.where(across - down == starts[g], 1.0, 0.0).astype(BF16)
        pieces_ref[g] = nn(chosen, memory).astype(BF16)


def replaced(target_ref, table_ref, rows_ref):
    marked = target_ref[...] == 1
    return jnp.where(marked, table_ref[10:11, :], rows_ref[...].astype(F32))


def slot_bias(length, count):
    across = lax.broadcasted_iota(jnp.int32, (1, count), 1)
    return jnp.where(across < length, 0.0, MASKED)


def slot_biases(lengths, count, rows):
    return jnp.concatenate(
        [jnp.broadcast_to(slot_bias(length, count), (rows, count)) for length in lengths], axis=0
    )


def slot_rows_of(rows, slots):
    return [slice(slot * (rows // slots), (slot + 1) * (rows // slots)) for slot in range(slots)]


def self_forward(
    lengths, x_ref, target_ref, table_ref, gathered_ref,
    log_ref, hidden_ref, target_out_ref, qkv, mix, weight_ref, sems,
):
    rows, width = x_ref.shape
    slots = lengths.shape[1]
    target_out_ref[...] = target_ref[...]
    copies = [bring_rows(gathered_ref, 0, weight_ref.shape[1], weight_ref, sems.at[0])]
    start = replaced(target_ref, table_ref, x_ref)
    low = start.astype(BF16)
    bias = slot_biases([lengths[0, slot] for slot in range(slots)], rows // slots, rows // slots)
    wait_all(copies)
    qkv_ref, mix_ref = qkv.ref, mix.ref
    qkv_ref[0] = (nn(low, block(weight_ref, 0)) * SCALE).astype(BF16)
    qkv_ref[1] = nn(low, block(weight_ref, 1)).astype(BF16)
    qkv_ref[2] = nn(low, block(weight_ref, 2)).astype(BF16)
    qkv.send()
    for first in range(0, HEADS // 2, 2):
        pairs = (first, first + 1)
        mixtures, _, logs = pair_forward(
            *[[[qkv_ref[i, here, lanes(pair)] for here in slot_rows_of(rows, slots)] for pair in pairs] for i in range(3)], bias
        )
        for pair, mixture in zip(pairs, mixtures):
            mix_ref[:, lanes(pair)] = mixture.astype(BF16)
        put_logs(log_ref, pairs, logs)
    mix.send()
    hidden_ref[...] = start + nn(mix_ref[...], block(weight_ref, 3))


def decoder_upper(
    core, slot_source, slot_length, hidden_ref, memory_ref, table_ref, cotangent, gathered_ref,
    output_ref, kept_ref, sent_ref, grad_ref, small_ref, parts, q, kv, mix,
    slope_ref, active_ref, inner_ref, weight_ref, ffn_ref, halves_ref, sems,
):
    rows, width = hidden_ref.shape
    slots = slot_source.shape[0]
    groups, longest, _ = memory_ref.shape
    part_rows = weight_ref.shape[1]
    cross_copy = bring_rows(gathered_ref, part_rows, part_rows, weight_ref, sems.at[0])
    ffn_copy = bring_rows(gathered_ref, 2 * part_rows, 2 * part_rows, ffn_ref, sems.at[1])
    unit, _ = norm_parts(hidden_ref[...])
    first = unit * table_ref[4:5, :] + table_ref[5:6, :]
    first_low = first.astype(BF16)
    memory = memory_ref[...].reshape(groups * longest, width)
    cross_copy.wait()
    q.ref[...] = (nn(first_low, block(weight_ref, 0)) * SCALE).astype(BF16)
    for i in range(2):
        kv.ref[i] = nn(memory, block(weight_ref, 1 + i)).astype(BF16).reshape(groups, longest, width)
    q.send()
    kv.send()
    bias = slot_biases([slot_length[slot] for slot in range(slots)], longest, rows // slots)
    sources = [slot_source[slot] for slot in range(slots)]
    for start in range(0, HEADS // 2, 2):
        pairs = (start, start + 1)
        mixtures, weights, _ = pair_forward(
            [[q.ref[here, lanes(pair)] for here in slot_rows_of(rows, slots)] for pair in pairs],
            [[kv.ref[0, source, :, lanes(pair)] for source in sources] for pair in pairs],
            [[kv.ref[1, source, :, lanes(pair)] for source in sources] for pair in pairs],
            bias,
        )
        for index, pair in enumerate(pairs):
            mix.ref[:, lanes(pair)] = mixtures[index].astype(BF16)
            for head in range(2):
                parts.ref[2 * pair + head] = weights[2 * index + head]
    parts.send()
    mix.send()
    hidden = first + nn(mix.ref[...], block(weight_ref, 3))
    unit_two, scale_two = norm_parts(hidden)
    second = unit_two * table_ref[6:7, :] + table_ref[7:8, :]
    low = second.astype(BF16)
    ffn_copy.wait()
    for j in range(4):
        at = slice(j * width, (j + 1) * width)
        active, slope = gelu_back(nn(low, block(ffn_ref, j)))
        slope_ref[:, at] = slope
        active_ref[:, at] = active.astype(BF16)
    hidden = second + nn(active_ref[...], tall(ffn_ref, 4))
    unit_three, scale_three = norm_parts(hidden)
    output_ref[...] = (unit_three * table_ref[8:9, :] + table_ref[9:10, :]).astype(BF16)
    grad, gain_three, bias_three = norm_back(
        cotangent.get()[...].astype(F32), unit_three, scale_three, table_ref[8:9, :]
    )
    grad_low = grad.astype(BF16)
    put_tall(halves_ref, core[0], 4, nn(active_ref[...].T, grad_low))
    inner_ref[...] = (nt(grad_low, tall(ffn_ref, 4)) * slope_ref[...]).astype(BF16)
    put_wide(halves_ref, core[0], 0, nn(low.T, inner_ref[...]))
    copies = send_halves(halves_ref, kept_ref, sent_ref, sems.at[pl.ds(2, 2)])
    grad = grad + nt(inner_ref[...], wide(ffn_ref, 0, 4))
    grad, gain_two, bias_two = norm_back(grad, unit_two, scale_two, table_ref[6:7, :])
    grad_ref[...] = grad
    for index, row in enumerate((gain_two, bias_two, gain_three, bias_three)):
        small_ref[index : index + 1, :] = row
    wait_all(copies)


def cross_backward(
    slot_source, grad_second_ref, q, kv, parts, gathered_ref,
    grad_memory_ref, grad_q, grad_kv, grad_mix_ref, weight_ref, sems,
):
    rows, width = grad_second_ref.shape
    slots = slot_source.shape[0]
    grad_q_ref, grad_kv_ref = grad_q.ref, grad_kv.ref
    _, groups, longest, _ = grad_kv_ref.shape
    part_rows = weight_ref.shape[1]
    cross_copy = bring_rows(gathered_ref, part_rows, part_rows, weight_ref, sems.at[0])
    grad_low = grad_second_ref[...].astype(BF16)
    cross_copy.wait()
    grad_mix_ref[...] = nt(grad_low, block(weight_ref, 3)).astype(BF16)
    q_ref, kv_ref, parts_ref = q.get(), kv.get(), parts.get()
    sources = [slot_source[slot] for slot in range(slots)]
    slices = slot_rows_of(rows, slots)
    for pair in range(HEADS // 2):
        at = lanes(pair)
        grad_query, grads_k, grads_v = pair_backward(
            [q_ref[here, at] for here in slices],
            [kv_ref[0, source, :, at] for source in sources],
            [kv_ref[1, source, :, at] for source in sources],
            [parts_ref[2 * pair + head] for head in range(2)],
            [grad_mix_ref[here, at] for here in slices],
        )
        grad_q_ref[:, at] = grad_query
        for source, grad_k, grad_v in zip(sources, grads_k, grads_v):
            grad_kv_ref[0, source, :, at] = grad_k
            grad_kv_ref[1, source, :, at] = grad_v
    grad_q.send()
    grad_kv.send()
    grad_k = grad_kv_ref[0].reshape(groups * longest, width)
    grad_v = grad_kv_ref[1].reshape(groups * longest, width)
    grad_memory_ref[...] = (
        (nt(grad_k, block(weight_ref, 1)) + nt(grad_v, block(weight_ref, 2)))
        .astype(BF16)
        .reshape(groups, longest, width)
    )


def decoder_lower(
    core, lengths, table_ref, grad_second_ref, grad_q_ref, hidden_ref, mix, memory, grad_kv, own_mix, qkv, logs_in, x, target, gathered_ref,
    kept_ref, sent_ref, grad_x_ref, small_ref, grad_mix_ref, grad_proj_ref, weight_ref, halves_ref, sems,
):
    rows, width = hidden_ref.shape
    slots = lengths.shape[1]
    copies = [bring_rows(gathered_ref, 0, weight_ref.shape[1], weight_ref, sems.at[0])]
    unit, scale = norm_parts(hidden_ref[...])
    first_low = (unit * table_ref[4:5, :] + table_ref[5:6, :]).astype(BF16)
    put(halves_ref, core[0], 0, nn(first_low.T, grad_q_ref[...]))
    grad_second = grad_second_ref[...]
    put(halves_ref, core[0], 3, nn(mix.get()[...].T, grad_second.astype(BF16)))
    wait_all(copies)
    grad = grad_second + nt(grad_q_ref[...], block(weight_ref, 4))
    grad, gain, bias_row = norm_back(grad, unit, scale, table_ref[4:5, :])
    grad_low = grad.astype(BF16)
    grad_mix_ref[...] = nt(grad_low, block(weight_ref, 3)).astype(BF16)
    put(halves_ref, core[0], 7, nn(own_mix.get()[...].T, grad_low))
    memory_ref, grad_kv_ref = memory.get(), grad_kv.get()
    turned = memory_ref[...].reshape(-1, width).T
    for i in range(2):
        put(halves_ref, core[0], 1 + i, nn(turned, grad_kv_ref[i].reshape(-1, width)))
    copies = send_halves(halves_ref, kept_ref, sent_ref, sems.at[pl.ds(1, 2)], 0, 4)
    bias = slot_biases([lengths[0, slot] for slot in range(slots)], rows // slots, rows // slots)
    qkv_ref, log_ref = qkv.get(), logs_in.get()
    slices = slot_rows_of(rows, slots)
    for pair in range(HEADS // 2):
        at = lanes(pair)
        queries, keys, values = [[qkv_ref[i, here, at] for here in slices] for i in range(3)]
        logs = [log_ref[:, 2 * pair + head : 2 * pair + head + 1] for head in range(2)]
        parts = pair_weights(queries, keys, bias, logs)
        grad_query, grads_k, grads_v = pair_backward(queries, keys, values, parts, [grad_mix_ref[here, at] for here in slices])
        grad_proj_ref[0, :, at] = grad_query
        grad_proj_ref[1, :, at] = jnp.concatenate(grads_k, axis=0)
        grad_proj_ref[2, :, at] = jnp.concatenate(grads_v, axis=0)
    x_ref, target_ref = x.get(), target.get()
    turned = replaced(target_ref, table_ref, x_ref).astype(BF16).T
    for i in range(3):
        put(halves_ref, core[0], 4 + i, nn(turned, grad_proj_ref[i]))
    copies += send_halves(halves_ref, kept_ref, sent_ref, sems.at[pl.ds(3, 2)], 4, 4)
    for i in range(3):
        grad = grad + nt(grad_proj_ref[i], block(weight_ref, i))
    marked = target_ref[...] == 1
    grad_x_ref[...] = jnp.where(marked, 0.0, grad)
    small_ref[0:1, :] = gain
    small_ref[1:2, :] = bias_row
    small_ref[2:3, :] = jnp.sum(jnp.where(marked, grad, 0.0), axis=0, keepdims=True)
    wait_all(copies)


def encoder_ffn_backward(
    core, place, lengths, route, pieces_ref, table_ref, small_one_ref, small_two_ref,
    hidden_two, hidden_one, active, slope, mix, part_a, part_b, part_c, part_d,
    kept_ref, sent_ref, grad_first, weight_ref, inner_ref, halves_ref, sems,
):
    rows, width = grad_first.ref.shape
    groups, longest, _ = pieces_ref.shape
    weight_copies = bring_pieces(place, (part_a, part_b, part_c, part_d), weight_ref, sems)
    down = lax.broadcasted_iota(jnp.int32, (rows, longest), 0)
    across = lax.broadcasted_iota(jnp.int32, (rows, longest), 1)
    starts, counts = piece_places(lengths, route, lengths.shape[1], rows)
    grad = jnp.zeros((rows, width), F32)
    for g in range(groups):
        chosen = (down - across == starts[g]) & (across < counts[g])
        grad = grad + nn(jnp.where(chosen, 1.0, 0.0).astype(BF16), pieces_ref[g])
    unit, scale = norm_parts(hidden_two.get()[...])
    grad, gain_two, bias_two = norm_back(grad, unit, scale, table_ref[2:3, :])
    grad_low = grad.astype(BF16)
    put_tall(halves_ref, core[0], 4, nn(active.get()[...].T, grad_low))
    wait_all(weight_copies)
    inner_ref[...] = (nt(grad_low, tall(weight_ref, 4)) * slope.get()[...].astype(F32)).astype(BF16)
    unit, scale = norm_parts(hidden_one.get()[...])
    low = (unit * table_ref[0:1, :] + table_ref[1:2, :]).astype(BF16)
    put_wide(halves_ref, core[0], 0, nn(low.T, inner_ref[...]))
    copies = send_halves(halves_ref, kept_ref, sent_ref, sems.at[pl.ds(32, 2)], 0, 8)
    grad = grad + nt(inner_ref[...], wide(weight_ref, 0, 4))
    grad, gain, bias_row = norm_back(grad, unit, scale, table_ref[0:1, :])
    grad_first.ref[...] = grad
    grad_first.send()
    small_rows = [gain, bias_row, gain_two, bias_two, small_one_ref[0:2, :], small_two_ref[...], small_one_ref[2:3, :]]
    put_rows(halves_ref, 9, small_rows)
    put(halves_ref, core[0], 8, nn(mix.get()[...].T, grad.astype(BF16)))
    copies += send_halves(halves_ref, kept_ref, sent_ref, sems.at[pl.ds(34, 2)], 8, 2)
    wait_all(copies)


def encoder_attention_backward(
    core, place, lengths, grad_in_ref, qkv, logs_in, x,
    part_a, part_b, part_c, part_d,
    kept_ref, sent_ref, grad_x_ref, bias_ref, grad_mix_ref, grad_proj_ref, weight_ref, halves_ref, sems,
):
    rows, width = grad_in_ref.shape
    weight_copies = bring_pieces(place, (part_a, part_b, part_c, part_d), weight_ref, sems)
    bias_ref[...] = segment_bias(lengths, rows)
    grad = grad_in_ref[...]
    wait_all(weight_copies)
    grad_mix_ref[...] = nt(grad.astype(BF16), block(weight_ref, 3)).astype(BF16)
    qkv_ref, log_ref = qkv.get(), logs_in.get()
    halves = halves_of_rows(rows)
    for pair in range(HEADS // 2):
        at = lanes(pair)
        queries, keys, values = [[qkv_ref[i, half, at] for half in halves] for i in range(3)]
        logs = [log_ref[:, 2 * pair + head : 2 * pair + head + 1] for head in range(2)]
        parts = pair_weights(queries, keys, bias_ref[...], logs)
        grad_query, grads_k, grads_v = pair_backward(queries, keys, values, parts, [grad_mix_ref[half, at] for half in halves])
        grad_proj_ref[0, :, at] = grad_query
        grad_proj_ref[1, :, at] = jnp.concatenate(grads_k, axis=0)
        grad_proj_ref[2, :, at] = jnp.concatenate(grads_v, axis=0)
    turned = x.get()[...].T
    for i in range(3):
        put(halves_ref, core[0], i, nn(turned, grad_proj_ref[i]))
    copies = send_halves(halves_ref, kept_ref, sent_ref, sems.at[pl.ds(32, 2)])
    for i in range(3):
        grad = grad + nt(grad_proj_ref[i], block(weight_ref, i))
    grad_x_ref[...] = pltpu.roll(grad, longest_start(lengths, rows), axis=0)
    wait_all(copies)


def finish(counts, me, *refs):
    terms, outs = refs[: 4 * len(counts)], refs[4 * len(counts) :]
    for chain, count in enumerate(counts):
        total = terms[4 * chain][...].astype(F32)
        for ref in terms[4 * chain + 1 : 4 * chain + 4]:
            total = total + ref[...].astype(F32)
        width = total.shape[1]
        at = 0
        own = None
        for ref in outs[:count]:
            columns = ref.shape[-1]
            if columns < width and own is None:
                total = pltpu.roll(total[at:, :], width - me[0] * columns, axis=1)[:, :columns]
                own, at = True, 0
            if len(ref.shape) == 3:
                parts = [ref.at[i] for i in range(ref.shape[0])]
            else:
                parts = [ref.at[:, i * width : (i + 1) * width] for i in range(columns // width)] or [ref]
            for one in parts:
                rows = one.shape[0]
                one[...] = total[at : at + rows, :]
                at += rows
        outs = outs[count:]


VMEM = pl.BlockSpec(memory_space=pltpu.VMEM)
SMEM = pl.BlockSpec(memory_space=pltpu.SMEM)
ANY = pl.BlockSpec(memory_space=pl.ANY)


class Late:
    def __init__(self, ref, target, sem):
        self.ref, self.copy = target, pltpu.make_async_copy(ref, target, sem)
        self.copy.start()

    def get(self):
        self.copy.wait()
        return self.ref


class Early:
    def __init__(self, ref, target, sem):
        self.ref, self.copy = ref, pltpu.make_async_copy(ref, target, sem)

    def send(self):
        self.copy.start()


def run(
    kernel, scalars, arrays, outs, scratch=(), late=(), far=(), far_outs=(), early=(), sems=0, us=1.0, start=(), end=()
):
    moving = len(late) + len(early)
    kinds = [pltpu.VMEM(one.shape, one.dtype) for one in late]
    kinds += [pltpu.VMEM(shape, kind) for shape, kind in tuple(early) + tuple(scratch)]
    kinds += [pltpu.SemaphoreType.DMA((count,)) for count in (moving, sems) if count]

    def body(*refs):
        left = list(refs)

        def take(count):
            taken = left[:count]
            del left[:count]
            return taken

        given = take(len(scalars) + len(arrays))
        late_in, far_in, out, early_out = take(len(late)), take(len(far)), take(len(outs)), take(len(early))
        late_at, early_at, rest = take(len(late)), take(len(early)), take(len(scratch))
        own = left[0] if moving else None
        lates = [Late(ref, at, own.at[i]) for i, (ref, at) in enumerate(zip(late_in, late_at))]
        earlies = [Early(at, ref, own.at[len(late) + i]) for i, (ref, at) in enumerate(zip(early_out, early_at))]
        kernel(*given, *lates, *far_in, *out, *earlies, *rest, *left[1 if moving else 0 :])
        for one in earlies:
            one.copy.wait()

    given, sends = (tuple(scalars), tuple(arrays), tuple(late), tuple(far)), [one.sends for one in start]
    if start:
        given, sends = lax.optimization_barrier((given, sends))
    for one, ready in zip(start, sends):
        one.sends = ready
        one.start()
    results = pl.pallas_call(
        body,
        out_shape=[jax.ShapeDtypeStruct(shape, kind) for shape, kind in tuple(outs) + tuple(early)],
        in_specs=[SMEM] * len(scalars) + [VMEM] * len(arrays) + [ANY] * (len(late) + len(far)),
        out_specs=[ANY if index in far_outs or index >= len(outs) else VMEM for index in range(len(outs) + len(early))],
        scratch_shapes=kinds,
        compiler_params=pltpu.CompilerParams(vmem_limit_bytes=56 << 20),
        cost_estimate=pl.CostEstimate(flops=int(us * 1.15e9), bytes_accessed=1 << 20, transcendentals=0),
    )(*given[0], *given[1], *given[2], *given[3])
    if end:
        results, got = lax.optimization_barrier((results, [one.got for one in end]))
        for one, blocks in zip(end, got):
            one.got = blocks
            one.finish()
    return results


def exchange(block, pairs):
    return lax.ppermute(block, AXES, pairs)


def pick(blocks, place):
    return lax.dynamic_index_in_dim(blocks, place, 0, keepdims=False)


def added(one, other):
    return (one.astype(F32) + other.astype(F32)).astype(BF16)


RING = (0, 1, 3, 2)


def sum_scatter(packs, count):
    me = lax.axis_index(AXES)
    core, low, high = me % 2, (me // 2) % 2, (me // 4) % 2
    rest = count // 8
    by_core = [pack.reshape((rest * 4, 2) + pack.shape[1:]) for pack in packs]
    sent, kept = [
        jnp.concatenate([lax.dynamic_index_in_dim(pack, side, 1, keepdims=False) for pack in by_core], axis=1)
        for side in (1 - core, core)
    ]
    tail = sent.shape[1:]
    kept = added(kept, exchange(sent, [(i, i ^ 1) for i in range(count)]))
    quads = kept.reshape((rest, 4) + tail)

    def two(first, second):
        parts = [lax.dynamic_index_in_dim(quads, place, 1, keepdims=True) for place in (first, second)]
        return jnp.concatenate(parts, axis=1)

    other_high, other_low = 1 - high, 1 - low
    sent = two(
        jnp.where(core == 0, 2 * other_high, other_low),
        jnp.where(core == 0, 2 * other_high + 1, other_low + 2),
    )
    kept = two(jnp.where(core == 0, 2 * high, low), jnp.where(core == 0, 2 * high + 1, low + 2))
    kept = added(kept, exchange(sent, [(i, i ^ (2 if i % 2 else 4)) for i in range(count)]))
    mine = jnp.where(core == 0, low, high)
    sent = lax.dynamic_index_in_dim(kept, 1 - mine, 1, keepdims=False)
    kept = lax.dynamic_index_in_dim(kept, mine, 1, keepdims=False)
    kept = added(kept, exchange(sent, [(i, i ^ (4 if i % 2 else 2)) for i in range(count)]))
    stride = 8
    while rest > 4:
        bit = (me // stride) % 2
        halves = kept.reshape((rest // 2, 2) + tail)
        sent = lax.dynamic_index_in_dim(halves, 1 - bit, 1, keepdims=False)
        kept = lax.dynamic_index_in_dim(halves, bit, 1, keepdims=False)
        kept = added(kept, exchange(sent, [(i, i ^ stride) for i in range(count)]))
        rest, stride = rest // 2, stride * 2
    order = RING if rest == 4 else tuple(range(rest))
    place_of = jnp.asarray([order.index(z) for z in range(rest)], jnp.int32)
    ring = jnp.asarray(order, jnp.int32)
    here = place_of[me // stride]
    onward = [
        (i, order[(order.index(i // stride) + 1) % rest] * stride + i % stride) for i in range(count)
    ]
    moving = pick(kept, ring[(here - 1) % rest]) if rest > 1 else kept[0]
    for step in range(rest - 1):
        arrived = exchange(moving, onward)
        own = pick(kept, ring[(here - 2 - step) % rest])
        moving = arrived.astype(F32) + own.astype(F32)
        if step < rest - 2:
            moving = moving.astype(BF16)
    return moving.astype(F32)


OUT_FIRST = [(i, i ^ (2 if i % 2 else 4)) for i in range(32)]
OUT_SECOND = [(i, i ^ (4 if i % 2 else 2)) for i in range(32)]
CORES = [(i, i ^ 1) for i in range(32)]


def gather_places():
    table = np.zeros((32, 32), np.int32)
    for me in range(32):
        for number in range(32):
            core = (me ^ (number // 16)) % 2
            first, second, level = (number // 8) % 2, (number // 4) % 2, number % 4
            x, y = (first, second) if core == 0 else (second, first)
            table[me, number] = ((me - me % 2) ^ (level * 8) ^ (x * 4) ^ (y * 2)) + core
    return table


def gather_blocks(mine):
    levels = [exchange(mine, [(i, i ^ (8 * k)) for i in range(32)]) for k in (1, 2, 3)]
    near = jnp.stack([mine] + levels)
    near = jnp.concatenate([near, exchange(near, OUT_SECOND)])
    far = exchange(near, OUT_FIRST)
    return near, far, exchange(near, CORES), exchange(far, CORES)


def together(*steps):
    arrived = lax.optimization_barrier([step.got for step in steps])
    for step, blocks in zip(steps, arrived):
        step.got = blocks


class Scatter:
    def __init__(self, kept, sent):
        me = lax.axis_index(AXES)
        core, low, high = me % 2, (me // 2) % 2, (me // 4) % 2
        self.bits = (jnp.where(core == 0, high, low), jnp.where(core == 0, low, high))
        self.level = me // 8
        self.kept, self.sends, self.stage = kept, [sent], 0

    def start(self):
        pairs = ([CORES], [OUT_FIRST], [OUT_SECOND], [[(i, i ^ (8 * k)) for i in range(32)] for k in (1, 2, 3)])
        self.got = [exchange(block, to) for block, to in zip(self.sends, pairs[self.stage])]
        return self.got

    def finish(self):
        if self.stage == 3:
            self.sends = []
            return self.sends
        got, size = self.got[0], self.kept.shape[0]

        def summed(place, count):
            return added(
                lax.dynamic_slice_in_dim(self.kept, place, count, 0), lax.dynamic_slice_in_dim(got, place, count, 0)
            )

        if self.stage < 2:
            half = size // 2
            bit = self.bits[self.stage]
            kept, sends = summed(bit * half, half), [summed((1 - bit) * half, half)]
        else:
            kept = summed(self.level, 1)[0]
            sends = [summed(jnp.bitwise_xor(self.level, k), 1)[0] for k in (1, 2, 3)]
        self.kept, self.sends, self.stage = kept, sends, self.stage + 1
        return self.sends


def on_device(
    enc_input,
    dec_input,
    target_mask,
    src_lengths,
    tgt_lengths,
    memory_route,
    enc_qkv,
    enc_out,
    enc_ffn_in,
    enc_ffn_out,
    enc_norms,
    dec_qkv,
    dec_out,
    cross_qkv,
    cross_out,
    dec_ffn_in,
    dec_ffn_out,
    dec_norms,
    mask_vector,
    out_cotangent,
):
    dp_count, groups = lax.axis_size("dp"), lax.axis_size("fsdp")
    count = dp_count * groups
    rows, width = enc_input.shape
    slots = src_lengths.shape[1]
    longest = rows // 2
    slot_rows = rows // slots
    part = enc_out.shape[0]
    inner = enc_ffn_in.shape[1]
    pieces_in = inner // width

    direct = count == 32 and part == 16
    kernel_part = width // 32
    joined = kernel_part // part
    me = lax.axis_index(AXES)
    my_dp, my_group = lax.axis_index("dp"), lax.axis_index("fsdp")

    def split(pack, squares):
        first = pack[:, : squares * part].reshape(32, joined, squares, part, width).transpose(0, 2, 1, 3, 4)
        return jnp.concatenate([first.reshape(32, -1, width), pack[:, squares * part :].reshape(32, -1, width)], axis=1)

    def unsplit(kept, sent, squares, used):
        kept = kept.reshape((2, 2, 4) + kept.shape[1:]).transpose(2, 0, 1, 3, 4)
        sent = sent.reshape((2, 2, 4) + sent.shape[1:]).transpose(2, 1, 0, 3, 4)
        pack = jnp.stack([kept, sent], axis=3).reshape(32, -1, width)
        first = pack[:, : squares * kernel_part].reshape(32, squares, joined, part, width).transpose(0, 2, 1, 3, 4)
        rest = pack[:, squares * kernel_part : used * kernel_part].reshape(count, -1, width)
        return jnp.concatenate([first.reshape(count, -1, width), rest], axis=1)

    if direct:
        core = (me % 2).reshape(1)
        attention_pack, ffn_pack, decoder_pack = run(
            pack_weights,
            (me.reshape(1),),
            (
                src_lengths, memory_route, mask_vector.reshape(1, part),
                enc_qkv, enc_out, enc_ffn_in, enc_ffn_out, enc_norms,
                dec_qkv, dec_out, cross_qkv, cross_out, dec_ffn_in, dec_ffn_out, dec_norms,
            ),
            (((5 * part, width), BF16), ((8 * part, width), BF16), ((16 * part, width), BF16)),
            us=2.0,
        )
        dec_all = lax.all_gather(decoder_pack, AXES, axis=0, tiled=False)
        attention_blocks = gather_blocks(attention_pack)
        ffn_blocks = gather_blocks(ffn_pack)
        place = jnp.asarray(gather_places())[me]
    else:
        core = jnp.zeros((1,), jnp.int32)

        def square(weight):
            return weight.reshape(-1, width)

        def wide(weight):
            return weight.reshape(part, pieces_in, width).transpose(1, 0, 2).reshape(-1, width)

        def whole(norms):
            return lax.all_gather(norms, AXES, axis=norms.ndim - 1, tiled=True).reshape(-1, width)

        def gathered(weights):
            return lax.all_gather(jnp.concatenate(weights), AXES, axis=0, tiled=False)

        rows_of = [whole(enc_norms), whole(dec_norms), whole(mask_vector)]
        first_rows = jnp.pad(jnp.concatenate(rows_of), ((0, kernel_part - 11), (0, 0)))
        small_blocks = jnp.concatenate([first_rows[None], jnp.zeros((31, kernel_part, width), BF16)])
        attention_all = split(gathered([square(enc_qkv), enc_out]), 4)
        attention_all = jnp.concatenate([attention_all, small_blocks], axis=1)
        attention_blocks = tuple(attention_all[i * 8 : i * 8 + 8] for i in range(4))
        ffn_all = split(gathered([wide(enc_ffn_in), enc_ffn_out]), pieces_in)
        ffn_blocks = tuple(ffn_all[i * 8 : i * 8 + 8] for i in range(4))
        decoder = [square(dec_qkv), dec_out, square(cross_qkv), cross_out, wide(dec_ffn_in), dec_ffn_out]
        dec_all = split(gathered(decoder), 8 + pieces_in)
        place = jnp.arange(32, dtype=jnp.int32)

    def some(*chains):
        return chains if direct else ()

    plane, three = (rows, width), (3, rows, width)
    memory_shape = (groups, longest, width)
    logs_shape = (rows, HEADS)
    parts_shape = (HEADS, rows, longest)

    def half_of(pieces):
        return ((16, pieces * kernel_part, width), BF16)

    def halves_of(pieces):
        return ((2, 16, pieces * kernel_part, width), BF16)

    def weights_of(pieces):
        return ((32, pieces * kernel_part, width), BF16)

    half_ffn = ((rows, inner), BF16)
    e_logs, e_hidden_one, table, e_qkv, x_turned, e_mix = run(
        encoder_attention,
        (place, src_lengths),
        (enc_input,),
        ((logs_shape, F32), (plane, F32), ((kernel_part, width), F32)),
        (((rows, longest), F32), weights_of(5)),
        far=attention_blocks,
        early=((three, BF16), (plane, BF16), (plane, BF16)),
        sems=32,
        us=9.5,
    )
    pieces, e_active, e_slope, e_hidden_two = run(
        encoder_ffn,
        (place, src_lengths, memory_route),
        (e_hidden_one, table),
        ((memory_shape, BF16),),
        (weights_of(2 * pieces_in),),
        far=ffn_blocks,
        early=(half_ffn, half_ffn, (plane, F32)),
        sems=32,
        us=9.0,
    )
    memory_in = lax.all_to_all(pieces, "fsdp", split_axis=0, concat_axis=0, tiled=True)
    d_logs, d_hidden, target, d_qkv, d_mix = run(
        self_forward,
        (tgt_lengths,),
        (dec_input, target_mask[:, None], table),
        ((logs_shape, F32), (plane, F32), ((rows, 1), jnp.int32)),
        (weights_of(4),),
        far=(dec_all,),
        early=((three, BF16), (plane, BF16)),
        sems=1,
        us=6.4,
    )
    if direct:
        ints = table[11].reshape(dp_count, groups, part)
        ints = lax.dynamic_index_in_dim(ints, my_dp, 0, keepdims=False).astype(jnp.int32)
        lengths_near, route_near = ints[:, :slots], ints[:, slots : 2 * slots]
    else:
        lengths_near = lax.all_gather(src_lengths[0], "fsdp")
        route_near = lax.all_gather(memory_route[0], "fsdp")
    ids = jnp.arange(groups, dtype=jnp.int32)
    wanted = my_group * slots + jnp.arange(slots, dtype=jnp.int32)
    chosen = route_near[None] == wanted[:, None, None]
    slot_source = jnp.sum(jnp.where(chosen, ids[None, :, None], 0), axis=(1, 2))
    slot_length = jnp.sum(jnp.where(chosen, lengths_near[None], 0), axis=(1, 2))

    dec_output, *dffn_halves, grad_second, small_two, parts, q_rows, kv_rows, c_mix = run(
        decoder_upper,
        (core, slot_source, slot_length),
        (d_hidden, memory_in, table),
        ((plane, BF16), half_of(8), half_of(8), (plane, F32), ((4, width), F32)),
        (((rows, inner), F32), half_ffn, half_ffn, weights_of(4), weights_of(8), halves_of(8)),
        late=(out_cotangent,),
        far=(dec_all,),
        far_outs=(1, 2),
        early=((parts_shape, F32), (plane, BF16), ((2,) + memory_shape, BF16), (plane, BF16)),
        sems=4,
        us=19.0,
    )

    def begin(halves):
        return Scatter(*halves) if direct else None

    dffn = begin(dffn_halves)
    grad_memory, grad_q, grad_kv = run(
        cross_backward,
        (slot_source,),
        (grad_second,),
        ((memory_shape, BF16),),
        ((plane, BF16), weights_of(4)),
        late=(q_rows, kv_rows, parts),
        early=((plane, BF16), ((2,) + memory_shape, BF16)),
        far=(dec_all,),
        sems=1,
        us=10.0,
        start=some(dffn),
        end=some(dffn),
    )
    returned = lax.all_to_all(grad_memory, "fsdp", split_axis=0, concat_axis=0, tiled=True)
    *middle_halves, dec_input_grad, small_one = run(
        decoder_lower,
        (core, tgt_lengths),
        (table, grad_second, grad_q, d_hidden),
        (half_of(8), half_of(8), (plane, F32), ((3, width), F32)),
        ((plane, BF16), (three, BF16), weights_of(5), halves_of(8)),
        late=(c_mix, memory_in, grad_kv, d_mix, d_qkv, d_logs, dec_input, target),
        far=(dec_all,),
        far_outs=(0, 1),
        sems=5,
        us=16.0,
        start=some(dffn),
        end=some(dffn),
    )
    returned, middle_halves = lax.optimization_barrier((returned, middle_halves))
    middle = begin(middle_halves)
    if direct:
        middle.start()
        middle.finish()
    *effn_halves, grad_enc = run(
        encoder_ffn_backward,
        (core, place, src_lengths, memory_route),
        (returned, table, small_one, small_two),
        (half_of(10), half_of(10)),
        (weights_of(8), half_ffn, halves_of(10)),
        late=(e_hidden_two, e_hidden_one, e_active, e_slope, e_mix),
        far=ffn_blocks,
        far_outs=(0, 1),
        early=((plane, F32),),
        sems=36,
        us=12.0,
        start=some(dffn, middle),
        end=some(dffn, middle),
    )
    effn = begin(effn_halves)
    if direct:
        effn.start()
        effn.finish()
    *eatt_halves, enc_input_grad = run(
        encoder_attention_backward,
        (core, place, src_lengths),
        (grad_enc,),
        (half_of(3), half_of(3), (plane, F32)),
        (((rows, longest), F32), (plane, BF16), (three, BF16), weights_of(5), halves_of(3)),
        late=(e_qkv, e_logs, x_turned),
        far=attention_blocks,
        far_outs=(0, 1),
        sems=34,
        us=12.0,
        start=some(dffn, middle, effn),
        end=some(dffn, middle),
    )
    eatt = begin(eatt_halves)

    def ends(*given, start=(), end=()):
        chains = [one for one in given if isinstance(one, Scatter)]
        shapes, counts = [], []
        for one in given:
            if isinstance(one, Scatter):
                counts.append(0)
            else:
                counts[-1] += 1
                shapes.append((one, F32))
        terms = [term for chain in chains for term in (chain.kept, *chain.got)]
        return run(partial(finish, tuple(counts)), (me.reshape(1),), terms, shapes, us=2.5, start=start, end=end)

    cube, square_part, wide_part, tall_part = (3, part, width), (part, width), (part, inner), (inner // count, width)
    if direct:
        middle.start()
        eatt.start()
        together(eatt, effn)
        for one in (eatt, effn):
            one.finish()
            one.start()
        together(eatt, effn)
        for one in (eatt, effn):
            one.finish()
        decoder_grads = ends(
            dffn, wide_part, tall_part, middle, cube, square_part, cube, square_part, start=(effn, eatt), end=(eatt,)
        )
        dec_ffn_grads, middle_grads = decoder_grads[:2], decoder_grads[2:]
        norm_shapes = ((2, 2, part), (3, 2, part), (1, part))
        eatt.start()
        encoder_grads = ends(effn, wide_part, tall_part, square_part, *norm_shapes, eatt, cube)
        enc_ffn_grads, small_grads, qkv_grads = encoder_grads[:3], list(encoder_grads[3:6]), encoder_grads[6]
        small_grads[2] = small_grads[2].reshape(part)
    else:

        def piece(summed, first, pieces=1):
            return summed[first * part : (first + pieces) * part]

        def wide_piece(summed):
            picked = piece(summed, 0, pieces_in).reshape(pieces_in, part, width)
            return picked.transpose(1, 0, 2).reshape(part, inner)

        effn_pack = unsplit(*[half[:, : 8 * kernel_part] for half in effn_halves], 4, 8)
        eout_pack = unsplit(*[half[:, 8 * kernel_part : 9 * kernel_part] for half in effn_halves], 1, 1)
        packs = [
            unsplit(*dffn_halves, 4, 8),
            unsplit(*middle_halves, 8, 8),
            jnp.concatenate([effn_pack, eout_pack], axis=1),
            unsplit(*eatt_halves, 3, 3),
        ]
        dffn_sum, middle_sum, effn_sum, eatt_sum = [sum_scatter([pack], count) for pack in packs]
        dec_ffn_grads = (wide_piece(dffn_sum), piece(dffn_sum, pieces_in, pieces_in))
        enc_ffn_grads = (wide_piece(effn_sum), piece(effn_sum, pieces_in, pieces_in), piece(effn_sum, 8))
        middle_grads = [
            piece(middle_sum, 0, 3).reshape(cube), piece(middle_sum, 3), piece(middle_sum, 4, 3).reshape(cube), piece(middle_sum, 7)
        ]
        qkv_grads = piece(eatt_sum, 0, 3).reshape(cube)
        small_sum = lax.psum(effn_halves[0][0, 9 * kernel_part :].astype(F32), AXES)
        small_sum = lax.dynamic_slice_in_dim(small_sum[:11], me * part, part, 1)
        small_grads = small_sum[:4].reshape(2, 2, part), small_sum[4:10].reshape(3, 2, part), small_sum[10]

    return (
        dec_output,
        enc_input_grad,
        dec_input_grad,
        qkv_grads,
        enc_ffn_grads[2],
        *enc_ffn_grads[:2],
        small_grads[0],
        *middle_grads[2:],
        *middle_grads[:2],
        *dec_ffn_grads,
        small_grads[1],
        small_grads[2],
    )


def solution(mesh):
    rows = P(AXES, None)
    flat = P(AXES)
    cube = P(None, AXES, None)
    norm = P(None, None, AXES)
    in_specs = (
        (rows, rows, flat, rows, rows, rows)
        + (cube, rows, rows, rows, norm)
        + (cube, rows, cube, rows, rows, rows, norm, flat)
        + (rows,)
    )
    out_specs = (
        (rows, rows, rows)
        + (cube, rows, rows, rows, norm)
        + (cube, rows, cube, rows, rows, rows, norm, flat)
    )
    return jax.shard_map(on_device, mesh=mesh, in_specs=in_specs, out_specs=out_specs, check_vma=False)
```
